32 devices in a mesh: seq: 16 (over z, x, core), head: 2 (over y).
Axes of the slice: x: 2, y: 2, z: 4, core: 2. Of those that a mesh axis runs over, the one named last changes fastest.
Arguments:
- tokens: bfloat16 [98304, 256], P(('seq', 'head')), may hold values from -6 to 6
- cotangent: bfloat16 [98304, 256], P(('seq', 'head')), may hold values from -6 to 6
- image_rows: int32 [128], replicated, may hold values from 1 to 32, as said below
- image_fill: int32 [128], replicated, may hold values from 1 to 96
- first_gain: float32 [256], replicated, may hold values from 0.1 to 1.9
- first_shift: float32 [256], replicated, may hold values from -2 to 2
- query_weight: bfloat16 [256, 256], P(None, 'head'), may hold values from -0.375 to 0.375
- key_weight: bfloat16 [256, 256], P(None, 'head'), may hold values from -0.375 to 0.375
- value_weight: bfloat16 [256, 256], P(None, 'head'), may hold values from -0.375 to 0.375
- out_weight: bfloat16 [256, 256], P('head'), may hold values from -2 to 2
- second_gain: float32 [256], replicated, may hold values from 0.1 to 1.9
- second_shift: float32 [256], replicated, may hold values from -2 to 2
- up_weight: bfloat16 [256, 1024], replicated, may hold values from -0.375 to 0.375
- up_bias: float32 [1024], replicated, may hold values from -3 to 3
- down_weight: bfloat16 [1024, 256], replicated, may hold values from -0.375 to 0.375
- down_bias: float32 [256], replicated, may hold values from -2 to 2
Outputs:
- mixed: bfloat16 [98304, 256], P(('seq', 'head'))
- input_grad: bfloat16 [98304, 256], P(('seq', 'head'))
- first_gain_grad: float32 [256], replicated
- first_shift_grad: float32 [256], replicated
- query_grad: float32 [256, 256], P(None, 'head')
- key_grad: float32 [256, 256], P(None, 'head')
- value_grad: float32 [256, 256], P(None, 'head')
- out_grad: float32 [256, 256], P('head')
- second_gain_grad: float32 [256], replicated
- second_shift_grad: float32 [256], replicated
- up_grad: float32 [256, 1024], replicated
- up_bias_grad: float32 [1024], replicated
- down_grad: float32 [1024, 256], replicated
- down_bias_grad: float32 [256], replicated
The draws below stay inside these ranges and needn't reach their ends.
Inputs may be any that keep to these rules, and one draw needn't show every extreme that they name: `image_rows`: image 1 has exactly 32 rows; the rows sum to 1024; the number of rows before any image but the first is never a multiple of 4.
All inputs are finite; a program needn't handle non-finite values.
Results may differ from the reference program's by a relative error of at most 0.012.
Values may be sent and summed in bfloat16 or wider, within the bound.
No kernel may reach another device: no remote copies, remote signals or barrier semaphores. Data moves between devices by JAX's collectives and lax.ppermute only.
A program may use at most 192 MiB of HBM per device.

```python
import jax
import jax.numpy as jnp
import numpy as np
from jax import lax

D = 256
HEADS = 2
HEAD_DIM = 128
FF = 1024
WINDOW = 96
IMG_ROWS = 32
UNIT = 4
IMAGES = 128
TOKENS = 98304


def draw_image_rows(key, part):
    key = jax.random.fold_in(key, 11)
    granules = IMAGES * 8 // UNIT - 1
    widest = IMG_ROWS // UNIT
    base_count = np.ones((IMAGES,), dtype=np.int32)
    base_count[0] = 0
    base_count[-1] = 0
    base_count[1] = widest
    room = np.full((IMAGES,), widest - 1, dtype=np.int32)
    room[1] = 0
    owner = np.repeat(np.arange(IMAGES, dtype=np.int32), room)
    spare = granules - int(base_count.sum())
    order = jax.random.permutation(key, owner.shape[0])
    chosen = jnp.asarray(owner, jnp.int32)[order[:spare]]
    extra = jnp.sum((chosen[:, None] == jnp.arange(IMAGES, dtype=jnp.int32)[None, :]).astype(jnp.int32), axis=0, dtype=jnp.int32)
    tails = np.zeros((IMAGES,), dtype=np.int32)
    tails[0] = 1
    tails[-1] = UNIT - 1
    return ((jnp.asarray(base_count, jnp.int32) + extra) * UNIT + jnp.asarray(tails, jnp.int32)).astype(jnp.int32)


def set_ends(drawn, stream_key, smallest, high):
    longest = drawn.shape.index(max(drawn.shape))
    spots = []
    for shift in (0, 1):
        where = [jax.random.randint(jax.random.fold_in(stream_key, axis), (), 0, length) for axis, length in enumerate(drawn.shape)]
        where[longest] = (where[longest] + shift) % drawn.shape[longest]
        spots.append(tuple(where))
    return drawn.at[spots[0]].set(smallest).at[spots[1]].set(high)


def levels(stream_key, shape, split, least, top_value):
    def one(dim, shards_of):
        draws = jax.random.uniform(jax.random.fold_in(jax.random.fold_in(stream_key, 6), dim), (shards_of,), jnp.float32, least / len(split), top_value / len(split))
        return jnp.repeat(jnp.exp(draws), shape[dim] // shards_of).reshape((-1,) + (1,) * (len(shape) - dim - 1))

    loudness = one(*split[0])
    for cut in split[1:]:
        loudness = loudness * one(*cut)
    return loudness


def normal_values(key, shape, scale, limit, pieces=(), kind=jnp.bfloat16):
    array = scale * jax.random.normal(key, shape, jnp.float32)
    if pieces:
        array = array * levels(key, shape, pieces, -0.22, 0.18)
    return jnp.clip(array, -limit, limit).astype(kind)


def setup_inputs(seed: int = 0) -> dict:
    seeds = jax.random.split(jax.random.key(seed), 17)
    return {
        "tokens": normal_values(seeds[0], (TOKENS, D), 1.0, 6.0, ((0, 32),)),
        "cotangent": normal_values(seeds[1], (TOKENS, D), 1.0, 6.0, ((0, 32),)),
        "image_rows": draw_image_rows(jax.random.fold_in(seeds[16], 71), 0),
        "image_fill": set_ends(jax.random.randint(seeds[3], (IMAGES,), 1, WINDOW + 1), jax.random.fold_in(seeds[3], 1), 1, WINDOW).astype(jnp.int32),
        "first_gain": jnp.clip(1.0 + 0.18 * jax.random.normal(seeds[4], (D,), jnp.float32), 0.1, 1.9),
        "first_shift": normal_values(seeds[5], (D,), 0.3, 2.0, (), jnp.float32),
        "query_weight": normal_values(seeds[6], (D, D), D ** -0.5, 0.375, ((1, 2),)),
        "key_weight": normal_values(seeds[7], (D, D), D ** -0.5, 0.375, ((1, 2),)),
        "value_weight": normal_values(seeds[8], (D, D), D ** -0.5, 0.375, ((1, 2),)),
        "out_weight": normal_values(seeds[9], (D, D), (D // 32) ** -0.5, 2.0, ((0, 2),)),
        "second_gain": jnp.clip(1.0 + 0.18 * jax.random.normal(seeds[10], (D,), jnp.float32), 0.1, 1.9),
        "second_shift": normal_values(seeds[11], (D,), 0.3, 2.0, (), jnp.float32),
        "up_weight": normal_values(seeds[12], (D, FF), D ** -0.5, 0.375),
        "up_bias": normal_values(seeds[13], (FF,), 0.5, 3.0, (), jnp.float32),
        "down_weight": normal_values(seeds[14], (FF, D), (FF // 4) ** -0.5, 0.375),
        "down_bias": normal_values(seeds[15], (D,), 0.3, 2.0, (), jnp.float32),
    }


EPSILON = 1e-05
MASKED = -1000000000.0
HIGHEST = lax.Precision.HIGHEST

@jax.custom_vjp
def low(v):
    return lax.optimization_barrier(v.astype(jnp.bfloat16)).astype(jnp.float32)

@jax.custom_vjp
def low_back(v):
    return v

def low_keep(v):
    return (low(v), None)

def low_pass(kept, grad):
    return (grad,)

def back_keep(v):
    return (v, None)

def back_low(kept, grad):
    return (low(grad),)
low.defvjp(low_keep, low_pass)
low_back.defvjp(back_keep, back_low)

def token_marks(image_rows, image_fill, first_token, span_count):
    row_ends = jnp.cumsum(image_rows, dtype=jnp.int32)
    starts = row_ends - image_rows
    token_id = first_token + jnp.arange(span_count, dtype=jnp.int32)
    row_index = jnp.floor_divide(token_id, WINDOW)
    image_id = lax.optimization_barrier(jnp.sum((row_ends[None, :] <= row_index[:, None]).astype(jnp.int32), axis=1, dtype=jnp.int32))
    member = jnp.arange(image_rows.shape[0], dtype=jnp.int32)[None, :] == image_id[:, None]
    start_token = lax.optimization_barrier(jnp.sum(jnp.where(member, starts[None, :], 0), axis=1, dtype=jnp.int32)) * WINDOW
    rows_here = lax.optimization_barrier(jnp.sum(jnp.where(member, image_rows[None, :], 0), axis=1, dtype=jnp.int32))
    filled = lax.optimization_barrier(jnp.sum(jnp.where(member, image_fill[None, :], 0), axis=1, dtype=jnp.int32))
    position = token_id - start_token
    length = (rows_here - 1) * WINDOW + filled
    image_id = jnp.where(token_id >= 0, image_id, -1)
    is_real = (token_id >= 0) & (position < length)
    return (image_id, position, is_real)

def allowed_pairs(query_info, key_info):
    distance = query_info[1][:, None] - key_info[1][None, :]
    same_image = query_info[0][:, None] == key_info[0][None, :]
    return same_image & (distance >= 0) & (distance < WINDOW) & key_info[2][None, :]

def normalize(inputs, scaling, offset_row):
    center = inputs - lax.optimization_barrier(jnp.mean(inputs, axis=1, keepdims=True))
    spread = lax.optimization_barrier(jnp.mean(center * center, axis=1, keepdims=True))
    return center * lax.rsqrt(spread + EPSILON) * scaling + offset_row

def reference(tokens, cotangent, image_rows, image_fill, first_gain, first_shift, query_weight, key_weight, value_weight, out_weight, second_gain, second_shift, up_weight, up_bias, down_weight, down_bias):
    token_count = tokens.shape[0]
    block_rows = min(512, token_count)
    query_marks = token_marks(image_rows, image_fill, 0, token_count)
    padded_marks = (jnp.concatenate([jnp.full((WINDOW,), -1, jnp.int32), query_marks[0]]), jnp.concatenate([jnp.zeros((WINDOW,), jnp.int32), query_marks[1]]), jnp.concatenate([jnp.zeros((WINDOW,), jnp.bool_), query_marks[2]]))
    score_scale = HEAD_DIM ** (-0.5)

    def forward(inputs, gain_one, shift_one, query_w, key_w, value_w, out_w, gain_two, shift_two, up_w, up_b, down_w, down_b):
        normed = low(normalize(inputs, gain_one, shift_one))
        queries = low(low_back(jnp.dot(normed, query_w, precision=HIGHEST)))
        key_rows = low(low_back(jnp.dot(normed, key_w, precision=HIGHEST)))
        value_rows = low(low_back(jnp.dot(normed, value_w, precision=HIGHEST)))
        lead_rows = jnp.zeros((WINDOW, D), jnp.float32)
        keys_all = jnp.concatenate([lead_rows, key_rows])
        values_all = jnp.concatenate([lead_rows, value_rows])

        def one_block(number):
            offset = number * block_rows
            query_block = lax.dynamic_slice_in_dim(queries, offset, block_rows, 0).reshape(block_rows, HEADS, HEAD_DIM)
            key_block = lax.dynamic_slice_in_dim(keys_all, offset, block_rows + WINDOW, 0).reshape(block_rows + WINDOW, HEADS, HEAD_DIM)
            value_block = lax.dynamic_slice_in_dim(values_all, offset, block_rows + WINDOW, 0).reshape(block_rows + WINDOW, HEADS, HEAD_DIM)
            query_info = tuple((lax.dynamic_slice_in_dim(marker, offset, block_rows, 0) for marker in query_marks))
            key_info = tuple((lax.dynamic_slice_in_dim(marker, offset, block_rows + WINDOW, 0) for marker in padded_marks))
            allowed = allowed_pairs(query_info, key_info)
            scores = low_back(jnp.einsum('qhe,khe->hqk', query_block, key_block, precision=HIGHEST) * score_scale)
            scores = jnp.where(allowed[None], scores, MASKED)
            weights = low(jax.nn.softmax(scores, axis=2))
            return jnp.einsum('hqk,khe->qhe', weights, value_block, precision=HIGHEST).reshape(block_rows, D)
        attended = lax.map(jax.checkpoint(one_block), jnp.arange(token_count // block_rows, dtype=jnp.int32))
        attended = low(low_back(attended.reshape(token_count, D)))
        mixing = low_back(jnp.dot(attended, out_w, precision=HIGHEST))
        middle = inputs + mixing
        normed_two = low(normalize(middle, gain_two, shift_two))
        hidden = low_back(jnp.dot(normed_two, up_w, precision=HIGHEST) + up_b)
        active = low(jax.nn.gelu(hidden, approximate=False))
        return middle + jnp.dot(active, down_w, precision=HIGHEST) + down_b
    primals = (tokens.astype(jnp.float32), first_gain, first_shift, query_weight.astype(jnp.float32), key_weight.astype(jnp.float32), value_weight.astype(jnp.float32), out_weight.astype(jnp.float32), second_gain, second_shift, up_weight.astype(jnp.float32), up_bias, down_weight.astype(jnp.float32), down_bias)
    mixed, pullback = jax.vjp(forward, *primals)
    gradients = pullback(cotangent.astype(jnp.float32))
    return (mixed.astype(jnp.bfloat16), gradients[0].astype(jnp.bfloat16), gradients[1], gradients[2], gradients[3], gradients[4], gradients[5], gradients[6], gradients[7], gradients[8], gradients[9], gradients[10], gradients[11], gradients[12])
```

```python
import functools

import jax
import jax.numpy as jnp
from jax import lax
from jax.experimental import pallas as pl
from jax.experimental.pallas import tpu as pltpu
from jax.sharding import PartitionSpec as P

HEAD_DIM = 128
HEADS = 2
WINDOW = 96
BOTH = ("seq", "head")

EPSILON = 1e-05
MASKED = -1000000000.0
LOG2E = 1.4426950408889634
SCALE = HEAD_DIM ** (-0.5)

F32 = jnp.float32
BF16 = jnp.bfloat16
LANES = (((1,), (1,)), ((), ()))
ROWS = (((0,), (0,)), ((), ()))


def dot(a, b):
    return jnp.dot(a, b, preferred_element_type=F32)


def dot_lanes(a, b):
    return lax.dot_general(a, b, LANES, preferred_element_type=F32)


def dot_rows(a, b):
    return lax.dot_general(a, b, ROWS, preferred_element_type=F32)


def standardize(inputs):
    center = inputs - jnp.mean(inputs, axis=1, keepdims=True)
    spread = jnp.mean(center * center, axis=1, keepdims=True)
    inverse = lax.rsqrt(spread + EPSILON)
    return center * inverse, inverse


def normalize_back(weighted, scaled, inverse):
    return inverse * (
        weighted
        - jnp.mean(weighted, axis=1, keepdims=True)
        - scaled * jnp.mean(weighted * scaled, axis=1, keepdims=True)
    )


def gelu_pair(x):
    below = 0.5 * (1.0 + lax.erf(x * 0.7071067811865476))
    bell = jnp.exp2(x * x * (-0.5 * LOG2E))
    return x * below, below + x * bell * 0.3989422804014327


def column_sums(value):
    return jnp.sum(value, axis=0, keepdims=True)


def layer_kernel(
    rows,
    x_ref,
    cot_ref,
    first_ref,
    fill_ref,
    gain1_ref,
    shift1_ref,
    heads_ref,
    gain2_ref,
    shift2_ref,
    up_ref,
    up_bias_ref,
    down_ref,
    down_bias_ref,
    mixed_ref,
    in_grad_ref,
    grads_ref,
    wqkv,
    wout,
    normed,
    xhat,
    inv,
    qbuf,
    kbuf,
    vbuf,
    att,
    probs,
    mid_grad,
    att_grad,
    dq,
    dk,
    dv,
    act,
    hid_grad,
    acc_down,
    acc_up,
    acc_qkv,
    acc_out,
    acc_vec,
):
    D = x_ref.shape[1]
    FF = up_ref.shape[1]
    for part in range(3):
        for h in range(HEADS):
            wqkv[:, part * D + h * HEAD_DIM : part * D + (h + 1) * HEAD_DIM] = heads_ref[
                h, part * D : (part + 1) * D, :
            ]
    for h in range(HEADS):
        for half in range(D // HEAD_DIM):
            wout[h * HEAD_DIM : (h + 1) * HEAD_DIM, half * HEAD_DIM : (half + 1) * HEAD_DIM] = (
                heads_ref[h, 3 * D + half * HEAD_DIM : 3 * D + (half + 1) * HEAD_DIM, :]
            )
    acc_down[...] = jnp.zeros_like(acc_down)
    acc_up[...] = jnp.zeros_like(acc_up)
    acc_qkv[...] = jnp.zeros_like(acc_qkv)
    acc_out[...] = jnp.zeros_like(acc_out)
    acc_vec[...] = jnp.zeros_like(acc_vec)

    rows_a = 17 if (rows + 2) % 17 == 0 else 1
    step_a = rows_a * WINDOW // 3

    def project(i, _):
        here = pl.ds(pl.multiple_of(i * step_a, 16), step_a)
        scaled, inverse = standardize(x_ref[here, :].astype(F32))
        xhat[here, :] = scaled
        inv[here, :] = inverse
        value = (scaled * gain1_ref[...] + shift1_ref[...]).astype(BF16)
        normed[here, :] = value
        qkv = dot(value, wqkv[...]).astype(BF16)
        qbuf[here, :] = qkv[:, :D]
        kbuf[here, :] = qkv[:, D : 2 * D]
        vbuf[here, :] = qkv[:, 2 * D :]
        return 0

    lax.fori_loop(0, (rows + 2) * WINDOW // step_a, project, 0)

    key_id = lax.broadcasted_iota(jnp.int32, (WINDOW, WINDOW), 0)
    query_id = lax.broadcasted_iota(jnp.int32, (WINDOW, WINDOW), 1)
    current = key_id <= query_id
    place = jnp.where(current, key_id, key_id - WINDOW)

    group = 3 if (rows + 1) % 3 == 0 else 1

    def attend(i, _):
        for g in range(group):
            r = i * group + g
            lowest = jnp.where(first_ref[r] > 0, 0, -WINDOW)
            keep = (place >= lowest) & (place < fill_ref[r])
            at = pl.multiple_of(r * WINDOW, 16)
            for h in range(HEADS):
                cols = slice(h * HEAD_DIM, (h + 1) * HEAD_DIM)
                keys = kbuf[pl.ds(at, 2 * WINDOW), cols]
                values = vbuf[pl.ds(at, 2 * WINDOW), cols]
                query = qbuf[pl.ds(at + WINDOW, WINDOW), cols]
                raw = dot_lanes(keys, query)
                scores = jnp.where(current, raw[WINDOW:], raw[:WINDOW]) * (SCALE * LOG2E)
                scores = jnp.where(keep, scores, MASKED * LOG2E)
                lifted = jnp.exp2(scores - jnp.max(scores, axis=0, keepdims=True))
                weights = lifted / jnp.sum(lifted, axis=0, keepdims=True)
                probs[r * HEADS + h] = weights
                both = jnp.concatenate(
                    [jnp.where(current, 0.0, weights), jnp.where(current, weights, 0.0)]
                ).astype(BF16)
                att[pl.ds(at, WINDOW), cols] = dot_rows(both, values).astype(BF16)
        return 0

    lax.fori_loop(0, (rows + 1) // group, attend, 0)

    def feed_forward(at, count, own):
        here = pl.ds(at, count)
        attended = att[here, :]
        cot = cot_ref[here, :]
        cot32 = cot.astype(F32)
        middle = x_ref[pl.ds(at + WINDOW, count), :].astype(F32) + dot(attended, wout[...])
        scaled, inverse = standardize(middle)
        normed_two = (scaled * gain2_ref[...] + shift2_ref[...]).astype(BF16)
        block = 256
        for f in range(FF // block):
            cols = slice(f * block, (f + 1) * block)
            hidden = dot(normed_two, up_ref[:, cols]) + up_bias_ref[:, cols]
            active, slope = gelu_pair(hidden)
            grad = (dot_lanes(cot, down_ref[cols, :]) * slope).astype(BF16)
            hid_grad[:count, cols] = grad
            if own:
                act[:count, cols] = active.astype(BF16)
                acc_vec[8:9, cols] += column_sums(grad.astype(F32))
        if own:
            mixed_ref[here, :] = (
                middle + dot(act[:count], down_ref[...]) + down_bias_ref[...]
            ).astype(BF16)
            acc_down[...] += dot_rows(cot, act[:count])
            acc_up[...] += dot_rows(normed_two, hid_grad[:count])
        g2 = dot_lanes(hid_grad[:count], up_ref[...])
        middle_grad = cot32 + normalize_back(g2 * gain2_ref[...], scaled, inverse)
        mixing_grad = middle_grad.astype(BF16)
        if own:
            mid_grad[here, :] = middle_grad
            acc_vec[2:3, :D] += column_sums(g2 * scaled)
            acc_vec[3:4, :D] += column_sums(g2)
            acc_vec[4:5, :D] += column_sums(cot32)
            acc_out[...] += dot_rows(attended, mixing_grad)
        att_grad[here, :] = dot_lanes(mixing_grad, wout[...]).astype(BF16)

    step_f = 4 * WINDOW if rows % 4 == 0 else WINDOW

    def feed_step(i, _):
        feed_forward(pl.multiple_of(i * step_f, 16), step_f, True)
        return 0

    lax.fori_loop(0, rows * WINDOW // step_f, feed_step, 0)
    feed_forward(rows * WINDOW, WINDOW, False)

    dk[:WINDOW, :] = jnp.zeros((WINDOW, D), F32)
    dv[:WINDOW, :] = jnp.zeros((WINDOW, D), F32)

    def attend_back(i, _):
        for g in range(group):
            r = i * group + g
            at = pl.multiple_of(r * WINDOW, 16)
            for h in range(HEADS):
                cols = slice(h * HEAD_DIM, (h + 1) * HEAD_DIM)
                keys = kbuf[pl.ds(at, 2 * WINDOW), cols]
                values = vbuf[pl.ds(at, 2 * WINDOW), cols]
                query = qbuf[pl.ds(at + WINDOW, WINDOW), cols]
                upstream = att_grad[pl.ds(at, WINDOW), cols]
                weights = probs[r * HEADS + h]
                raw = dot_lanes(values, upstream)
                dweights = jnp.where(current, raw[WINDOW:], raw[:WINDOW])
                inner = jnp.sum(weights * dweights, axis=0, keepdims=True)
                dscores = weights * (dweights - inner)
                both = jnp.concatenate(
                    [jnp.where(current, 0.0, dscores), jnp.where(current, dscores, 0.0)]
                ).astype(BF16)
                both_w = jnp.concatenate(
                    [jnp.where(current, 0.0, weights), jnp.where(current, weights, 0.0)]
                ).astype(BF16)
                key_part = dot(both, query) * SCALE
                value_part = dot(both_w, upstream)
                dk[pl.ds(at, WINDOW), cols] += key_part[:WINDOW]
                dk[pl.ds(at + WINDOW, WINDOW), cols] = key_part[WINDOW:]
                dv[pl.ds(at, WINDOW), cols] += value_part[:WINDOW]
                dv[pl.ds(at + WINDOW, WINDOW), cols] = value_part[WINDOW:]
                dq[pl.ds(at, WINDOW), cols] = (dot_rows(both, keys) * SCALE).astype(BF16)
        return 0

    lax.fori_loop(0, (rows + 1) // group, attend_back, 0)

    def project_back(i, _):
        at = pl.multiple_of(i * step_f, 16)
        here = pl.ds(at, step_f)
        there = pl.ds(at + WINDOW, step_f)
        grads = jnp.concatenate(
            [dq[here, :], dk[there, :].astype(BF16), dv[there, :].astype(BF16)], axis=1
        )
        acc_qkv[...] += dot_rows(normed[there, :], grads)
        g1 = dot_lanes(grads, wqkv[...])
        scaled = xhat[there, :]
        acc_vec[0:1, :D] += column_sums(g1 * scaled)
        acc_vec[1:2, :D] += column_sums(g1)
        in_grad_ref[here, :] = (
            mid_grad[here, :] + normalize_back(g1 * gain1_ref[...], scaled, inv[there, :])
        ).astype(BF16)
        return 0

    lax.fori_loop(0, rows * WINDOW // step_f, project_back, 0)

    for f in range(FF // D):
        cols = slice(f * D, (f + 1) * D)
        grads_ref[f * D : (f + 1) * D, :] = acc_down[:, cols].T.astype(BF16)
        grads_ref[FF + f * D : FF + (f + 1) * D, :] = acc_up[:, cols].astype(BF16)
    base = 2 * FF
    for part in range(3):
        grads_ref[base + part * D : base + (part + 1) * D, :] = acc_qkv[
            :, part * D : (part + 1) * D
        ].astype(BF16)
    grads_ref[base + 3 * D : base + 4 * D, :] = acc_out[...].astype(BF16)
    base = base + 4 * D
    tail = grads_ref.shape[0] - base
    vectors = jnp.concatenate(
        [acc_vec[0:8, :D]] + [acc_vec[8:9, f * D : (f + 1) * D] for f in range(FF // D)]
        + [jnp.zeros((tail - 8 - FF // D, D), F32)]
    )
    grads_ref[base:, :] = vectors.astype(BF16)


def layer(x_ext, cot_ext, first, fill, gain1, shift1, heads, gain2, shift2, up, up_bias, down, down_bias, piece):
    count, D = x_ext.shape
    FF = up.shape[1]
    rows = count // WINDOW - 2
    own = rows * WINDOW
    grad_rows = 2 * FF + 4 * D + 16
    grad_rows = -(-grad_rows // piece) * piece
    vmem = pl.BlockSpec(memory_space=pltpu.VMEM)
    smem = pl.BlockSpec(memory_space=pltpu.SMEM)
    step_f = 4 * WINDOW if rows % 4 == 0 else WINDOW
    return pl.pallas_call(
        functools.partial(layer_kernel, rows),
        out_shape=(
            jax.ShapeDtypeStruct((own, D), BF16),
            jax.ShapeDtypeStruct((own, D), BF16),
            jax.ShapeDtypeStruct((grad_rows, D), BF16),
        ),
        in_specs=[vmem, vmem, smem, smem] + [vmem] * 9,
        out_specs=(vmem, vmem, vmem),
        scratch_shapes=[
            pltpu.VMEM((D, 3 * D), BF16),
            pltpu.VMEM((D, D), BF16),
            pltpu.VMEM((count, D), BF16),
            pltpu.VMEM((count, D), F32),
            pltpu.VMEM((count, 1), F32),
            pltpu.VMEM((count, D), BF16),
            pltpu.VMEM((count, D), BF16),
            pltpu.VMEM((count, D), BF16),
            pltpu.VMEM((count - WINDOW, D), BF16),
            pltpu.VMEM(((rows + 1) * HEADS, WINDOW, WINDOW), F32),
            pltpu.VMEM((own, D), F32),
            pltpu.VMEM((count - WINDOW, D), BF16),
            pltpu.VMEM((count - WINDOW, D), BF16),
            pltpu.VMEM((count, D), F32),
            pltpu.VMEM((count, D), F32),
            pltpu.VMEM((step_f, FF), BF16),
            pltpu.VMEM((step_f, FF), BF16),
            pltpu.VMEM((D, FF), F32),
            pltpu.VMEM((D, FF), F32),
            pltpu.VMEM((D, 3 * D), F32),
            pltpu.VMEM((D, D), F32),
            pltpu.VMEM((16, FF), F32),
        ],
        compiler_params=pltpu.CompilerParams(vmem_limit_bytes=56 * 1024 * 1024),
        name="layer",
    )(x_ext, cot_ext, first, fill, gain1, shift1, heads, gain2, shift2, up, up_bias, down, down_bias)


def row_marks(image_rows, image_fill, first_row, count):
    ends = jnp.cumsum(image_rows, dtype=jnp.int32)
    starts = ends - image_rows
    row = first_row + jnp.arange(count, dtype=jnp.int32)
    opens = jnp.any(starts[None, :] == row[:, None], axis=1) | (row >= ends[-1])
    short = jnp.sum(
        jnp.where(ends[None, :] == row[:, None] + 1, WINDOW - image_fill[None, :], 0),
        axis=1,
        dtype=jnp.int32,
    )
    return opens.astype(jnp.int32), WINDOW - short


def swapped(value, mask):
    count = lax.axis_size("seq") * lax.axis_size("head")
    return lax.ppermute(value, BOTH, [(i, i ^ mask) for i in range(count)])


def stages():
    count = lax.axis_size("seq") * lax.axis_size("head")
    bits = [1 << b for b in range(count.bit_length() - 1)]
    if len(bits) < 3:
        return [bits]
    rest = bits[3:]
    return [[bits[1]], [bits[0], bits[2]]] + [rest[i : i + 2] for i in range(0, len(rest), 2)]


def spans(masks):
    found = [0]
    for mask in masks:
        found = found + [f ^ mask for f in found]
    return found


def all_sum(value):
    place = lax.axis_index("seq") * lax.axis_size("head") + lax.axis_index("head")
    width = value.shape[1]
    codes = []
    for masks in stages():
        code = sum(((place & mask) // mask) << j for j, mask in enumerate(masks))
        codes.append(code)
        parts = value.reshape(1 << len(masks), -1, width)
        total = lax.dynamic_index_in_dim(parts, code, 0, False).astype(F32)
        arrived = [
            swapped(lax.dynamic_index_in_dim(parts, code ^ k, 0, False), mask)
            for k, mask in enumerate(spans(masks))
            if k
        ]
        for part in arrived:
            total = total + part.astype(F32)
        value = total.astype(BF16)
    for masks, code in list(zip(stages(), codes))[::-1]:
        found = [value] + [swapped(value, mask) for k, mask in enumerate(spans(masks)) if k]
        whole = jnp.zeros((len(found),) + value.shape, value.dtype)
        for k, part in enumerate(found):
            whole = lax.dynamic_update_index_in_dim(whole, part, code ^ k, 0)
        value = whole.reshape(-1, width)
    return value


def shards(
    tokens,
    cotangent,
    image_rows,
    image_fill,
    first_gain,
    first_shift,
    query_weight,
    key_weight,
    value_weight,
    out_weight,
    second_gain,
    second_shift,
    up_weight,
    up_bias,
    down_weight,
    down_bias,
):
    own, D = tokens.shape
    FF = up_weight.shape[1]
    devices = lax.axis_size("seq") * lax.axis_size("head")
    head = lax.axis_index("head")
    place = lax.axis_index("seq") * lax.axis_size("head") + head
    rows = own // WINDOW
    mine = jnp.concatenate(
        [query_weight, key_weight, value_weight]
        + [out_weight[:, c : c + HEAD_DIM] for c in range(0, D, HEAD_DIM)]
    )
    other = lax.ppermute(mine, "head", [(0, 1), (1, 0)])
    before = lax.ppermute(tokens[own - WINDOW :], BOTH, [(i, i + 1) for i in range(devices - 1)])
    after = lax.ppermute(
        jnp.concatenate([tokens[:WINDOW], cotangent[:WINDOW]]),
        BOTH,
        [(i + 1, i) for i in range(devices - 1)],
    )
    heads = jnp.stack([jnp.where(head == 0, mine, other), jnp.where(head == 0, other, mine)])
    x_ext = jnp.concatenate([before, tokens, after[:WINDOW]])
    cot_ext = jnp.concatenate([cotangent, after[WINDOW:]])
    opens, fill = row_marks(image_rows, image_fill, place * rows, rows + 1)
    mixed, input_grad, grads = layer(
        x_ext,
        cot_ext,
        opens,
        fill,
        first_gain[None],
        first_shift[None],
        heads,
        second_gain[None],
        second_shift[None],
        up_weight,
        up_bias[None],
        down_weight,
        down_bias[None],
        8 * devices,
    )
    total = all_sum(grads)
    column = head * HEAD_DIM
    base = 2 * FF
    sums = [total[base + p * D : base + (p + 1) * D] for p in range(4)]
    vectors = total[base + 4 * D : base + 4 * D + 16].astype(F32)
    up_grad = jnp.concatenate([total[FF + c : FF + c + D] for c in range(0, FF, D)], axis=1)
    return (
        mixed,
        input_grad,
        vectors[0],
        vectors[1],
        lax.dynamic_slice_in_dim(sums[0], column, HEAD_DIM, 1).astype(F32),
        lax.dynamic_slice_in_dim(sums[1], column, HEAD_DIM, 1).astype(F32),
        lax.dynamic_slice_in_dim(sums[2], column, HEAD_DIM, 1).astype(F32),
        lax.dynamic_slice_in_dim(sums[3], column, HEAD_DIM, 0).astype(F32),
        vectors[2],
        vectors[3],
        up_grad.astype(F32),
        vectors[8 : 8 + FF // D].reshape(FF),
        total[:FF].astype(F32),
        vectors[4],
    )


def solution(mesh):
    stream = P(("seq", "head"), None)
    columns = P(None, "head")
    in_specs = (stream, stream) + (P(),) * 4 + (columns,) * 3 + (P("head", None),) + (P(),) * 6
    out_specs = (
        (stream, stream) + (P(),) * 2 + (columns,) * 3 + (P("head", None),) + (P(),) * 6
    )
    return jax.shard_map(shards, mesh=mesh, in_specs=in_specs, out_specs=out_specs, check_vma=False)
```

```python
import functools

import jax
import jax.numpy as jnp
from jax import lax
from jax.experimental import pallas as pl
from jax.experimental.pallas import tpu as pltpu
from jax.sharding import PartitionSpec as P

HEAD_DIM = 128
HEADS = 2
WINDOW = 96
BOTH = ("seq", "head")

EPSILON = 1e-05
MASKED = -1000000000.0
LOG2E = 1.4426950408889634
SCALE = HEAD_DIM ** (-0.5)

F32 = jnp.float32
BF16 = jnp.bfloat16
LANES = (((1,), (1,)), ((), ()))
ROWS = (((0,), (0,)), ((), ()))

CHUNK = 8
LAG = 4


def dot(a, b):
    return jnp.dot(a, b, preferred_element_type=F32)


def dot_lanes(a, b):
    return lax.dot_general(a, b, LANES, preferred_element_type=F32)


def dot_rows(a, b):
    return lax.dot_general(a, b, ROWS, preferred_element_type=F32)


def standardize(inputs):
    center = inputs - jnp.mean(inputs, axis=1, keepdims=True)
    spread = jnp.mean(center * center, axis=1, keepdims=True)
    inverse = lax.rsqrt(spread + EPSILON)
    return center * inverse, inverse


def normalize_back(weighted, scaled, inverse):
    return inverse * (
        weighted
        - jnp.mean(weighted, axis=1, keepdims=True)
        - scaled * jnp.mean(weighted * scaled, axis=1, keepdims=True)
    )


def twice_gelu(x):
    z = x * 0.7071067811865476
    below = 1.0 + lax.erf(z)
    bell = jnp.exp2(z * z * -LOG2E)
    return x * below, below + x * bell * 0.7978845608028654


def column_sums(value):
    return jnp.sum(value, axis=0, keepdims=True)


def merge(*lists):
    marked = [
        ((n + 0.5) / len(work), k, n, job) for k, work in enumerate(lists) for n, job in enumerate(work)
    ]
    return [job for *_, job in sorted(marked, key=lambda item: item[:3])]


VECTOR_ROWS = 128


def half_rows(FF, D):
    return (2 * FF * D + 4 * D * D) // (2 * HEAD_DIM) + VECTOR_ROWS


def vector_slots(FF, D):
    found = [
        (n, slice(c, c + HEAD_DIM)) for n in range(5) for c in range(0, D, HEAD_DIM)
    ]
    return found + [(8, slice(c, c + HEAD_DIM)) for c in range(0, FF, HEAD_DIM)]


def layer_kernel(
    rows,
    tok_ref,
    cot_in_ref,
    rim_ref,
    image_rows_ref,
    image_fill_ref,
    gain1_ref,
    shift1_ref,
    query_ref,
    key_ref,
    value_ref,
    out_ref,
    heads_ref,
    gain2_ref,
    shift2_ref,
    up_in_ref,
    up_bias_ref,
    down_in_ref,
    down_bias_ref,
    mixed_ref,
    in_grad_ref,
    keep_ref,
    send_ref,
    x_ref,
    cot_ref,
    up_ref,
    down_ref,
    wqkv,
    wout,
    low_mark,
    fill_mark,
    normed,
    xhat,
    inv,
    qbuf,
    kbuf,
    vbuf,
    gbuf,
    att,
    probs,
    mid_grad,
    dqkv,
    act,
    hid_grad,
    mixed_buf,
    in_grad_buf,
    acc_down,
    acc_up,
    acc_qkv,
    acc_out,
    acc_vec,
    vec_rows,
    in_sem,
    out_sem,
):
    D = x_ref.shape[1]
    FF = up_ref.shape[1]
    own = rows * WINDOW
    head = lax.axis_index("head")
    place = lax.axis_index("seq") * lax.axis_size("head") + head
    step = CHUNK * WINDOW
    steps = rows // CHUNK

    arriving = {}
    for i in range(steps):
        piece = pl.ds(i * step, step)
        arriving["x", i] = pltpu.make_async_copy(
            tok_ref.at[piece], x_ref.at[pl.ds(WINDOW + i * step, step)], in_sem.at[i]
        )
    arriving["up"] = pltpu.make_async_copy(up_in_ref, up_ref, in_sem.at[steps])
    arriving["down"] = pltpu.make_async_copy(down_in_ref, down_ref, in_sem.at[steps + 1])
    arriving["cot"] = pltpu.make_async_copy(cot_in_ref, cot_ref.at[pl.ds(0, own)], in_sem.at[steps + 2])
    for copy in arriving.values():
        copy.start()
    leaving = []

    mine = [query_ref[...], key_ref[...], value_ref[...]]
    for part in range(3):
        theirs = heads_ref[part * D : (part + 1) * D, :]
        at = pl.multiple_of(part * D + head * HEAD_DIM, HEAD_DIM)
        wqkv[:, pl.ds(at, HEAD_DIM)] = mine[part]
        at = pl.multiple_of(part * D + (1 - head) * HEAD_DIM, HEAD_DIM)
        wqkv[:, pl.ds(at, HEAD_DIM)] = theirs
    wout[pl.ds(pl.multiple_of(head * HEAD_DIM, HEAD_DIM), HEAD_DIM), :] = out_ref[...]
    for half in range(D // HEAD_DIM):
        wout[
            pl.ds(pl.multiple_of((1 - head) * HEAD_DIM, HEAD_DIM), HEAD_DIM),
            half * HEAD_DIM : (half + 1) * HEAD_DIM,
        ] = heads_ref[3 * D + half * HEAD_DIM : 3 * D + (half + 1) * HEAD_DIM, :]
    acc_vec[...] = jnp.zeros_like(acc_vec)
    for half in range(D // HEAD_DIM):
        cols = slice(half * HEAD_DIM, (half + 1) * HEAD_DIM)
        near = heads_ref[4 * D + half * 2 * WINDOW : 4 * D + (half + 1) * 2 * WINDOW, :]
        far = rim_ref[half * 2 * WINDOW : (half + 1) * 2 * WINDOW, :]
        x_ref[:WINDOW, cols] = jnp.where(head == 0, far[:WINDOW], near[:WINDOW])
        x_ref[WINDOW + own :, cols] = jnp.where(head == 0, near[:WINDOW], far[:WINDOW])
        cot_ref[own:, cols] = jnp.where(head == 0, near[WINDOW:], far[WINDOW:])

    images = image_rows_ref.shape[1]
    earlier = lax.broadcasted_iota(jnp.int32, (images, images), 0) <= lax.broadcasted_iota(
        jnp.int32, (images, images), 1
    )
    counts = jnp.broadcast_to(image_rows_ref[...], (8, images)).astype(F32)
    ends = dot(counts.astype(BF16), jnp.where(earlier, 1.0, 0.0).astype(BF16))[:1]
    starts = ends - counts[:1]
    mark_rows = low_mark.shape[0]
    row = (place * rows + lax.broadcasted_iota(jnp.int32, (mark_rows, 1), 0)).astype(F32)
    opens = jnp.sum(jnp.where(starts == row, 1.0, 0.0), axis=1, keepdims=True)
    opens = jnp.where(row >= ends[:, images - 1 :], 1.0, opens)
    missing = WINDOW - image_fill_ref[...].astype(F32)
    short = jnp.sum(jnp.where(ends == row + 1.0, missing, 0.0), axis=1, keepdims=True)
    low_mark[...] = jnp.broadcast_to(
        jnp.where(opens > 0.0, 0.0, -1.0 * WINDOW), low_mark.shape
    ).astype(jnp.int32)
    fill_mark[...] = jnp.broadcast_to(WINDOW - short, fill_mark.shape).astype(jnp.int32)

    def project(first, count):
        here = slice(first * WINDOW, (first + count) * WINDOW)
        scaled, inverse = standardize(x_ref[here, :].astype(F32))
        xhat[here, :] = scaled
        inv[here, :] = inverse
        value = (scaled * gain1_ref[...] + shift1_ref[...]).astype(BF16)
        normed[here, :] = value
        for part, buf in enumerate((qbuf, kbuf, vbuf)):
            made = dot(value, wqkv[:, part * D : (part + 1) * D]).astype(BF16)
            for g in range(count):
                buf[(first + g) * WINDOW : (first + g + 1) * WINDOW, :] = made[
                    g * WINDOW : (g + 1) * WINDOW
                ]

    key_id = lax.broadcasted_iota(jnp.int32, (WINDOW, WINDOW), 0)
    query_id = lax.broadcasted_iota(jnp.int32, (WINDOW, WINDOW), 1)
    current = key_id <= query_id
    current_t = key_id >= query_id
    offset = jnp.where(current, key_id, key_id - WINDOW)
    columns = [slice(h * HEAD_DIM, (h + 1) * HEAD_DIM) for h in range(HEADS)]
    held = {}

    def pair(buf, j, h):
        return buf[(j - 1) * WINDOW : (j + 1) * WINDOW, columns[h]]

    def row_of(buf, j, h):
        return buf[j * WINDOW : (j + 1) * WINDOW, columns[h]]

    def window_sum(weights, buf, j, h):
        turned = weights.T
        zero = jnp.zeros_like(turned)
        both = pair(buf, j, h)
        return dot(jnp.where(current_t, zero, turned), both[:WINDOW]) + dot(
            jnp.where(current_t, turned, zero), both[WINDOW:]
        )

    def key_sum(weights, queries):
        zero = jnp.zeros_like(weights)
        both = jnp.concatenate([jnp.where(current, zero, weights), jnp.where(current, weights, zero)])
        made = dot(both, queries)
        return made[:WINDOW], made[WINDOW:]

    def score(j, h):
        raw = dot_lanes(pair(kbuf, j, h), row_of(qbuf, j, h))
        held[j, h] = jnp.where(current, raw[WINDOW:], raw[:WINDOW])

    def soften(j, h):
        r = j - 1
        keep = (offset >= low_mark[r : r + 1, :WINDOW]) & (offset < fill_mark[r : r + 1, :WINDOW])
        scores = jnp.where(keep, held.pop((j, h)) * (SCALE * LOG2E), MASKED * LOG2E)
        lifted = jnp.exp2(scores - jnp.max(scores, axis=0, keepdims=True))
        weights = lifted * (1.0 / jnp.sum(lifted, axis=0, keepdims=True))
        probs[r * HEADS + h] = weights
        held[j, h] = weights.astype(BF16)

    def gather(j, h):
        r = j - 1
        att[r * WINDOW : (r + 1) * WINDOW, columns[h]] = window_sum(
            held.pop((j, h)), vbuf, j, h
        ).astype(BF16)

    def feed_forward(first, count, own_rows):
        at = first * WINDOW
        size = count * WINDOW
        here = slice(at, at + size)
        held = {}
        block = 256

        def enter():
            attended = att[here, :]
            middle = x_ref[at + WINDOW : at + WINDOW + size, :].astype(F32) + dot(attended, wout[...])
            scaled, inverse = standardize(middle)
            held.update(middle=middle, scaled=scaled, inverse=inverse)
            held["normed"] = (scaled * gain2_ref[...] + shift2_ref[...]).astype(BF16)

        def hide(f):
            cols = slice(f * block, (f + 1) * block)
            cot = cot_ref[here, :]
            hidden = dot(held["normed"], up_ref[:, cols]) + up_bias_ref[:, cols]
            active, slope = twice_gelu(hidden)
            grad = dot_lanes(cot, down_ref[cols, :]) * slope
            hid_grad[:size, cols] = grad.astype(BF16)
            if own_rows:
                act[:size, cols] = active.astype(BF16)
                acc_vec[8:9, cols] += column_sums(grad)

        def weigh(f):
            cols = slice(f * block, (f + 1) * block)
            down_part = dot_rows(cot_ref[here, :], act[:size, cols])
            up_part = dot_rows(held["normed"], hid_grad[:size, cols])
            if at:
                acc_down[:, cols] += down_part
                acc_up[:, cols] += up_part
            else:
                acc_down[:, cols] = down_part
                acc_up[:, cols] = up_part

        def mix():
            mixed_buf[here, :] = (
                held["middle"] + dot(act[:size], down_ref[...]) + down_bias_ref[...]
            ).astype(BF16)
            copy = pltpu.make_async_copy(
                mixed_buf.at[pl.ds(at, size)], mixed_ref.at[pl.ds(at, size)], out_sem.at[0, at // size]
            )
            copy.start()
            leaving.append(copy)

        def back():
            scaled = held["scaled"]
            g2 = dot_lanes(hid_grad[:size], up_ref[...])
            cot32 = cot_ref[here, :].astype(F32)
            middle_grad = cot32 + normalize_back(g2 * gain2_ref[...], scaled, held["inverse"])
            mixing_grad = middle_grad.astype(BF16)
            if own_rows:
                mid_grad[here, :] = middle_grad
                acc_vec[2:3, :D] += column_sums(g2 * scaled)
                acc_vec[3:4, :D] += column_sums(g2)
                acc_vec[4:5, :D] += column_sums(cot32)
                out_part = dot_rows(att[here, :], mixing_grad)
                if at:
                    acc_out[...] += out_part
                else:
                    acc_out[...] = out_part
            made = dot_lanes(mixing_grad, wout[...]).astype(BF16)
            for g in range(count):
                j = first + 1 + g
                gbuf[j * WINDOW : (j + 1) * WINDOW, :] = made[g * WINDOW : (g + 1) * WINDOW]

        jobs = [enter]
        for f in range(FF // block):
            jobs.append(functools.partial(hide, f))
            if own_rows and f:
                jobs.append(functools.partial(weigh, f - 1))
        if own_rows:
            jobs.append(functools.partial(weigh, FF // block - 1))
            jobs.append(mix)
        jobs.append(back)
        return jobs

    held_back = {}
    unfinished = {}

    def weigh_grads(j, h):
        raw = dot_lanes(pair(vbuf, j, h), row_of(gbuf, j, h))
        held_back[j, h] = jnp.where(current, raw[WINDOW:], raw[:WINDOW])

    def soften_back(j, h):
        dweights = held_back.pop((j, h))
        weights = probs[(j - 1) * HEADS + h]
        inner = jnp.sum(weights * dweights, axis=0, keepdims=True)
        dscores = (weights * (dweights - inner)).astype(BF16)
        held_back[j, h] = (dscores, weights.astype(BF16))

    def gather_back(j, h):
        r = j - 1
        dscores, weights = held_back.pop((j, h))
        found = [key_sum(dscores, row_of(qbuf, j, h)), key_sum(weights, row_of(gbuf, j, h))]
        if j > 1:
            there = slice((r - 1) * WINDOW, r * WINDOW)
            for part, (before, _) in enumerate(found):
                total = unfinished[part, h] + before
                at = (part + 1) * D + h * HEAD_DIM
                dqkv[there, at : at + HEAD_DIM] = (total if part else total * SCALE).astype(BF16)
        for part, (_, current_part) in enumerate(found):
            unfinished[part, h] = current_part
        if j <= rows:
            dqkv[r * WINDOW : (r + 1) * WINDOW, columns[h]] = (
                window_sum(dscores, kbuf, j, h) * SCALE
            ).astype(BF16)

    def project_back(i):
        at = i * step
        here = slice(at, at + step)
        there = slice(at + WINDOW, at + WINDOW + step)
        grads = dqkv[here, :]
        part = dot_rows(normed[there, :], grads)
        if at:
            acc_qkv[...] += part
        else:
            acc_qkv[...] = part
        g1 = dot_lanes(grads, wqkv[...])
        scaled = xhat[there, :]
        acc_vec[0:1, :D] += column_sums(g1 * scaled)
        acc_vec[1:2, :D] += column_sums(g1)
        in_grad_buf[here, :] = (
            mid_grad[here, :] + normalize_back(g1 * gain1_ref[...], scaled, inv[there, :])
        ).astype(BF16)
        copy = pltpu.make_async_copy(
            in_grad_buf.at[pl.ds(at, step)], in_grad_ref.at[pl.ds(at, step)], out_sem.at[1, i]
        )
        copy.start()
        leaving.append(copy)

    def do(jobs):
        for job in jobs:
            job()

    def staggered(first, last, *kinds):
        units = [(j, h) for j in range(first, last + 1) for h in range(HEADS)]
        jobs = []
        for t in range(len(units) + LAG * (len(kinds) - 1)):
            for k, kind in enumerate(kinds):
                if 0 <= t - LAG * k < len(units):
                    jobs.append(functools.partial(kind, *units[t - LAG * k]))
        return jobs

    def forward(first, last):
        return staggered(first, last, score, soften, gather)

    def backward(first, last):
        return staggered(first, last, weigh_grads, soften_back, gather_back)

    for i in range(steps):
        arriving["x", i].wait()
        project(i * CHUNK + (1 if i else 0), CHUNK + (0 if i else 1))
    project(rows + 1, 1)
    do(forward(1, rows + 1))
    for name in ("up", "down", "cot"):
        arriving[name].wait()
    down_ref[...] = (down_ref[...].astype(F32) * 0.5).astype(BF16)
    for i in range(steps):
        do(feed_forward(i * CHUNK, CHUNK, True))
    do(feed_forward(rows, 1, False))
    do(backward(1, rows + 1))
    for i in range(steps):
        project_back(i)

    for s, (n, cols) in enumerate(vector_slots(FF, D)):
        vec_rows[s : s + 1, :] = acc_vec[n : n + 1, cols]
    core = (place & 2) // 2
    wide = FF // 2
    for c, ref in ((core, keep_ref), (1 - core, send_ref)):
        base = 0
        for f in range(0, wide, D):
            at = pl.ds(pl.multiple_of(c * wide + f, D), D)
            block = (acc_down[:, at] * 0.5).astype(BF16).T
            for half in range(D // HEAD_DIM):
                ref[half * wide + f : half * wide + f + D, :] = block[
                    :, half * HEAD_DIM : (half + 1) * HEAD_DIM
                ]
        base = D // HEAD_DIM * wide
        for f in range(0, wide, HEAD_DIM):
            at = pl.ds(pl.multiple_of(c * wide + f, HEAD_DIM), HEAD_DIM)
            ref[base : base + D, :] = acc_up[:, at].astype(BF16)
            base += D
        mine = pl.ds(pl.multiple_of(c * HEAD_DIM, HEAD_DIM), HEAD_DIM)
        for h in range(HEADS):
            for part in range(3):
                at = part * D + h * HEAD_DIM
                ref[base : base + HEAD_DIM, :] = acc_qkv[mine, at : at + HEAD_DIM].astype(BF16)
                base += HEAD_DIM
            ref[base : base + HEAD_DIM, :] = acc_out[
                h * HEAD_DIM : (h + 1) * HEAD_DIM, mine
            ].astype(BF16)
            base += HEAD_DIM
        flat = vec_rows[pl.ds(pl.multiple_of(c * 16, 16), 16), :].astype(BF16)
        ref[base:, :] = jnp.concatenate([flat] * (VECTOR_ROWS // 16))
    for copy in leaving:
        copy.wait()


def layer(
    tokens, cotangent, rim, image_rows, image_fill, gain1, shift1, weights, other, gain2, shift2, up,
    up_bias, down, down_bias
):
    own, D = tokens.shape
    FF = up.shape[1]
    rows = own // WINDOW
    count = own + 2 * WINDOW
    half = half_rows(FF, D)
    in_vmem = functools.partial(pltpu.with_memory_space_constraint, memory_space=pltpu.VMEM)
    rim, other = in_vmem(rim), in_vmem(other)
    vmem = pl.BlockSpec(memory_space=pltpu.VMEM)
    anywhere = pl.BlockSpec(memory_space=pl.ANY)
    steps = rows // CHUNK
    mark_rows = -(-(rows + 1) // 8) * 8
    return pl.pallas_call(
        functools.partial(layer_kernel, rows),
        out_shape=(
            jax.ShapeDtypeStruct((own, D), BF16),
            jax.ShapeDtypeStruct((own, D), BF16),
            pltpu.VMEM((half, HEAD_DIM), BF16),
            pltpu.VMEM((half, HEAD_DIM), BF16),
        ),
        in_specs=[anywhere, anywhere] + [vmem] * 12 + [anywhere, vmem, anywhere, vmem],
        out_specs=(anywhere, anywhere, vmem, vmem),
        scratch_shapes=[
            pltpu.VMEM((count, D), BF16),
            pltpu.VMEM((count - WINDOW, D), BF16),
            pltpu.VMEM((D, FF), BF16),
            pltpu.VMEM((FF, D), BF16),
            pltpu.VMEM((D, 3 * D), BF16),
            pltpu.VMEM((D, D), BF16),
            pltpu.VMEM((mark_rows, 128), jnp.int32),
            pltpu.VMEM((mark_rows, 128), jnp.int32),
            pltpu.VMEM((count, D), BF16),
            pltpu.VMEM((count, D), F32),
            pltpu.VMEM((count, 1), F32),
            pltpu.VMEM((count, D), BF16),
            pltpu.VMEM((count, D), BF16),
            pltpu.VMEM((count, D), BF16),
            pltpu.VMEM((count, D), BF16),
            pltpu.VMEM((count - WINDOW, D), BF16),
            pltpu.VMEM(((rows + 1) * HEADS, WINDOW, WINDOW), F32),
            pltpu.VMEM((own, D), F32),
            pltpu.VMEM((own, 3 * D), BF16),
            pltpu.VMEM((CHUNK * WINDOW, FF), BF16),
            pltpu.VMEM((CHUNK * WINDOW, FF), BF16),
            pltpu.VMEM((own, D), BF16),
            pltpu.VMEM((own, D), BF16),
            pltpu.VMEM((D, FF), F32),
            pltpu.VMEM((D, FF), F32),
            pltpu.VMEM((D, 3 * D), F32),
            pltpu.VMEM((D, D), F32),
            pltpu.VMEM((16, FF), F32),
            pltpu.VMEM((32, HEAD_DIM), F32),
            pltpu.SemaphoreType.DMA((steps + 3,)),
            pltpu.SemaphoreType.DMA((2, steps)),
        ],
        compiler_params=pltpu.CompilerParams(vmem_limit_bytes=56 * 1024 * 1024),
        name="layer",
    )(
        tokens, cotangent, rim, image_rows, image_fill, gain1, shift1, *weights, other, gain2, shift2, up,
        up_bias, down, down_bias
    )


def pack_kernel(query_ref, key_ref, value_ref, out_ref, tok_ref, cot_ref, near_ref, far_ref, sem):
    D = query_ref.shape[0]
    own = tok_ref.shape[0]
    head = lax.axis_index("head")
    moves = [
        (ref, near_ref.at[pl.ds(part * D, D)]) for part, ref in enumerate((query_ref, key_ref, value_ref))
    ]
    last = own - WINDOW
    near_from = pl.multiple_of((1 - head) * last, WINDOW)
    far_from = pl.multiple_of(head * last, WINDOW)
    for half in range(D // HEAD_DIM):
        cols = pl.ds(half * HEAD_DIM, HEAD_DIM)
        moves.append((out_ref.at[:, cols], near_ref.at[pl.ds(3 * D + half * HEAD_DIM, HEAD_DIM)]))
        for k, ref in enumerate((tok_ref, cot_ref)):
            at = (half * 2 + k) * WINDOW
            moves.append((ref.at[pl.ds(near_from, WINDOW), cols], near_ref.at[pl.ds(4 * D + at, WINDOW)]))
            moves.append((ref.at[pl.ds(far_from, WINDOW), cols], far_ref.at[pl.ds(at, WINDOW)]))
    copies = [pltpu.make_async_copy(a, b, sem.at[n]) for n, (a, b) in enumerate(moves)]
    for copy in copies:
        copy.start()
    for copy in copies:
        copy.wait()


def pack(query_weight, key_weight, value_weight, out_weight, tokens, cotangent):
    D = query_weight.shape[0]
    rim = 2 * WINDOW * D // HEAD_DIM
    anywhere = pl.BlockSpec(memory_space=pl.ANY)
    vmem = pl.BlockSpec(memory_space=pltpu.VMEM)
    return pl.pallas_call(
        pack_kernel,
        out_shape=(pltpu.VMEM((4 * D + rim, HEAD_DIM), BF16), pltpu.VMEM((rim, HEAD_DIM), BF16)),
        in_specs=[anywhere] * 6,
        out_specs=(vmem, vmem),
        scratch_shapes=[pltpu.SemaphoreType.DMA((3 + 5 * (D // HEAD_DIM),))],
        name="pack",
    )(query_weight, key_weight, value_weight, out_weight, tokens, cotangent)


def finish_kernel(FF, D, mine_ref, other_ref, *refs):
    outs, (down_buf, up_buf, vec_rows, sem) = refs[:12], refs[12:]
    gain1, shift1, query, key, value, out, gain2, shift2, up, up_bias, down, down_bias = outs
    core = lax.axis_index("seq") % 2
    head = lax.axis_index("head")
    halves = ((core, mine_ref), (1 - core, other_ref))
    wide = FF // 2
    for c, ref in halves:
        rows = pl.ds(pl.multiple_of(c * wide, wide), wide)
        for half in range(D // HEAD_DIM):
            down_buf[rows, half * HEAD_DIM : (half + 1) * HEAD_DIM] = ref[
                half * wide : (half + 1) * wide, :
            ].astype(F32)
    copies = [pltpu.make_async_copy(down_buf, down, sem.at[0])]
    copies[0].start()
    start = D // HEAD_DIM * wide
    for c, ref in halves:
        for n, f in enumerate(range(0, wide, HEAD_DIM)):
            at = pl.ds(pl.multiple_of(c * wide + f, HEAD_DIM), HEAD_DIM)
            up_buf[:, at] = ref[start + n * D : start + (n + 1) * D, :].astype(F32)
    copies.append(pltpu.make_async_copy(up_buf, up, sem.at[1]))
    copies[1].start()
    start += wide // HEAD_DIM * D
    for c, ref in halves:
        mine = pl.ds(pl.multiple_of(c * HEAD_DIM, HEAD_DIM), HEAD_DIM)
        base = start + head * (4 * HEAD_DIM)
        for part, made in enumerate((query, key, value)):
            at = pl.multiple_of(base + part * HEAD_DIM, HEAD_DIM)
            made[mine, :] = ref[pl.ds(at, HEAD_DIM), :].astype(F32)
        at = pl.multiple_of(base + 3 * HEAD_DIM, HEAD_DIM)
        out[:, mine] = ref[pl.ds(at, HEAD_DIM), :].astype(F32)
        base = start + 8 * HEAD_DIM
        vec_rows[pl.ds(pl.multiple_of(c * 16, 16), 16), :] = ref[base : base + 16, :].astype(F32)
    vectors = (gain1, shift1, gain2, shift2, down_bias)
    for s, (n, cols) in enumerate(vector_slots(FF, D)):
        made = up_bias if n == 8 else vectors[n]
        made[cols] = vec_rows[s, :]
    for copy in copies:
        copy.wait()


def finish(mine, other, FF, D):
    vmem = pl.BlockSpec(memory_space=pltpu.VMEM)
    anywhere = pl.BlockSpec(memory_space=pl.ANY)
    shapes = [(D,), (D,)] + [(D, HEAD_DIM)] * 3 + [(HEAD_DIM, D), (D,), (D,), (D, FF), (FF,), (FF, D), (D,)]
    in_vmem = functools.partial(pltpu.with_memory_space_constraint, memory_space=pltpu.VMEM)
    return pl.pallas_call(
        functools.partial(finish_kernel, FF, D),
        out_shape=tuple(jax.ShapeDtypeStruct(shape, F32) for shape in shapes),
        in_specs=[vmem, vmem],
        out_specs=tuple(anywhere if n in (8, 10) else vmem for n in range(len(shapes))),
        scratch_shapes=[
            pltpu.VMEM((FF, D), F32),
            pltpu.VMEM((D, FF), F32),
            pltpu.VMEM((32, HEAD_DIM), F32),
            pltpu.SemaphoreType.DMA((2,)),
        ],
        name="finish",
    )(in_vmem(mine), in_vmem(other))


def spans(masks):
    found = [0]
    for mask in masks:
        found = found + [f ^ mask for f in found]
    return found


def stages(count):
    bits = [1 << b for b in range(count.bit_length() - 1)]
    plane, rest = [bits[0], bits[2]], bits[3:]
    found = [plane] + [rest[i : i + 2] for i in range(0, len(rest), 2)]
    if len(found) > 1 and len(found[1]) == 2:
        return [(found[0], found[1]), (found[1], found[0])] + [(masks, masks) for masks in found[2:]]
    return [(masks, masks) for masks in found]


def partners(value, masks, k):
    count = lax.axis_size("seq") * lax.axis_size("head")
    hops = [spans(side)[k] for side in masks]
    return lax.ppermute(value, BOTH, [(i, i ^ hops[i // 2 % 2]) for i in range(count)])


def all_sum(value):
    count = lax.axis_size("seq") * lax.axis_size("head")
    place = lax.axis_index("seq") * lax.axis_size("head") + lax.axis_index("head")
    width = value.shape[1]
    steps = []
    for masks in stages(count):
        code, other_code = (
            sum(((place & mask) // mask) << j for j, mask in enumerate(side)) for side in masks
        )
        steps.append((masks, jnp.where(place & 2 == 0, code, other_code)))
    for masks, code in steps:
        parts = value.reshape(1 << len(masks[0]), -1, width)
        total = lax.dynamic_index_in_dim(parts, code, 0, False).astype(F32)
        arrived = [
            partners(lax.dynamic_index_in_dim(parts, code ^ k, 0, False), masks, k)
            for k in range(1, parts.shape[0])
        ]
        for part in arrived:
            total = total + part.astype(F32)
        value = total.astype(BF16)
    for masks, code in steps[::-1]:
        parts = 1 << len(masks[0])
        found = [value] + [partners(value, masks, k) for k in range(1, parts)]
        whole = jnp.zeros((parts,) + value.shape, value.dtype)
        for k, part in enumerate(found):
            whole = lax.dynamic_update_index_in_dim(whole, part, code ^ k, 0)
        value = whole.reshape(-1, width)
    return value


def across_cores(value):
    return partners(value, ([2], [2]), 1)


def shards(
    tokens,
    cotangent,
    image_rows,
    image_fill,
    first_gain,
    first_shift,
    query_weight,
    key_weight,
    value_weight,
    out_weight,
    second_gain,
    second_shift,
    up_weight,
    up_bias,
    down_weight,
    down_bias,
):
    own, D = tokens.shape
    FF = up_weight.shape[1]
    devices = lax.axis_size("seq") * lax.axis_size("head")
    near, far = pack(query_weight, key_weight, value_weight, out_weight, tokens, cotangent)
    other = lax.ppermute(near, "head", [(0, 1), (1, 0)])
    pairs = [(i, i + 1) for i in range(1, devices - 1, 2)]
    rim = lax.ppermute(far, BOTH, pairs + [(b, a) for a, b in pairs])
    mixed, input_grad, keep, send = layer(
        tokens,
        cotangent,
        rim,
        image_rows[None],
        image_fill[None],
        first_gain[None],
        first_shift[None],
        (query_weight, key_weight, value_weight, out_weight),
        other,
        second_gain[None],
        second_shift[None],
        up_weight,
        up_bias[None],
        down_weight,
        down_bias[None],
    )
    summed = (keep.astype(F32) + across_cores(send).astype(F32)).astype(BF16)
    mine = all_sum(summed)
    return (mixed, input_grad, *finish(mine, across_cores(mine), FF, D))


def solution(mesh):
    stream = P(("seq", "head"), None)
    columns = P(None, "head")
    in_specs = (stream, stream) + (P(),) * 4 + (columns,) * 3 + (P("head", None),) + (P(),) * 6
    out_specs = (
        (stream, stream) + (P(),) * 2 + (columns,) * 3 + (P("head", None),) + (P(),) * 6
    )
    return jax.shard_map(shards, mesh=mesh, in_specs=in_specs, out_specs=out_specs, check_vma=False)
```

```python
import functools

import jax
import jax.numpy as jnp
from jax import lax
from jax.experimental import pallas as pl
from jax.experimental.pallas import tpu as pltpu
from jax.sharding import PartitionSpec as P

HEAD_DIM = 128
HEADS = 2
WINDOW = 96
BOTH = ("seq", "head")

EPSILON = 1e-05
MASKED = -1000000000.0
LOG2E = 1.4426950408889634
SCALE = HEAD_DIM ** (-0.5)

F32 = jnp.float32
BF16 = jnp.bfloat16
LANES = (((1,), (1,)), ((), ()))
ROWS = (((0,), (0,)), ((), ()))

CHUNK = 8
LAG = 4


def dot(a, b):
    return jnp.dot(a, b, preferred_element_type=F32)


def split_dot(a, b, how=None):
    how = how or dot
    half = a.shape[0] // 2
    if half % 16:
        return how(a, b)
    return jnp.concatenate([how(a[:half], b), how(a[half:], b)])


def dot_lanes(a, b):
    return lax.dot_general(a, b, LANES, preferred_element_type=F32)


def dot_rows(a, b):
    return lax.dot_general(a, b, ROWS, preferred_element_type=F32)


def standardize(inputs):
    center = inputs - jnp.mean(inputs, axis=1, keepdims=True)
    spread = jnp.mean(center * center, axis=1, keepdims=True)
    inverse = lax.rsqrt(spread + EPSILON)
    return center * inverse, inverse


def normalize_back(weighted, scaled, inverse):
    return inverse * (
        weighted
        - jnp.mean(weighted, axis=1, keepdims=True)
        - scaled * jnp.mean(weighted * scaled, axis=1, keepdims=True)
    )


def twice_gelu(x):
    z = x * 0.7071067811865476
    below = 1.0 + lax.erf(z)
    bell = jnp.exp2(z * z * -LOG2E)
    return x * below, below + x * bell * 0.7978845608028654


def column_sums(value):
    return jnp.sum(value, axis=0, keepdims=True)


def merge(*lists):
    marked = [
        ((n + 0.5) / len(work), k, n, job) for k, work in enumerate(lists) for n, job in enumerate(work)
    ]
    return [job for *_, job in sorted(marked, key=lambda item: item[:3])]


VECTOR_ROWS = 128


def half_rows(FF, D):
    return (2 * FF * D + 4 * D * D) // (2 * HEAD_DIM) + VECTOR_ROWS


def vector_slots(FF, D):
    found = [
        (n, slice(c, c + HEAD_DIM)) for n in range(5) for c in range(0, D, HEAD_DIM)
    ]
    return found + [(8, slice(c, c + HEAD_DIM)) for c in range(0, FF, HEAD_DIM)]


def masks():
    key_id = lax.broadcasted_iota(jnp.int32, (WINDOW, WINDOW), 0)
    query_id = lax.broadcasted_iota(jnp.int32, (WINDOW, WINDOW), 1)
    current = key_id <= query_id
    return current, key_id >= query_id, jnp.where(current, key_id, key_id - WINDOW)


def merged_scores(keys, query, current):
    raw = dot_lanes(keys, query)
    return jnp.where(current, raw[WINDOW:], raw[:WINDOW])


def soft_weights(scores, offset, low, fill):
    keep = (offset >= low) & (offset < fill)
    scores = jnp.where(keep, scores * (SCALE * LOG2E), MASKED * LOG2E)
    lifted = jnp.exp2(scores - jnp.max(scores, axis=0, keepdims=True))
    return lifted * (1.0 / jnp.sum(lifted, axis=0, keepdims=True))


def window_sum(weights, values, current_t):
    turned = weights.T
    zero = jnp.zeros_like(turned)
    return dot(jnp.where(current_t, zero, turned), values[:WINDOW]) + dot(
        jnp.where(current_t, turned, zero), values[WINDOW:]
    )


def staggered(units, *kinds):
    jobs = []
    for t in range(len(units) + LAG * (len(kinds) - 1)):
        for k, kind in enumerate(kinds):
            if 0 <= t - LAG * k < len(units):
                jobs.append(functools.partial(kind, *units[t - LAG * k]))
    return jobs


def do(jobs):
    for job in jobs:
        job()


def local_kernel(
    rows,
    x_ref,
    cot_in_ref,
    down_in_ref,
    image_rows_ref,
    image_fill_ref,
    gain1_ref,
    shift1_ref,
    query_ref,
    key_ref,
    value_ref,
    xhat,
    inv,
    qbuf,
    kbuf,
    vbuf,
    probs,
    att,
    low_mark,
    fill_mark,
    normed_t,
    cot_t,
    cot_ref,
    down_ref,
    weight,
    in_sem,
):
    own = rows * WINDOW
    step = CHUNK * WINDOW
    place = lax.axis_index("seq") * lax.axis_size("head") + lax.axis_index("head")
    for part, ref in enumerate((query_ref, key_ref, value_ref)):
        weight[:, part * HEAD_DIM : (part + 1) * HEAD_DIM] = ref[...]
    later = [
        pltpu.make_async_copy(a, b, in_sem.at[n])
        for n, (a, b) in enumerate(((cot_in_ref, cot_ref), (down_in_ref, down_ref)))
    ]
    for copy in later:
        copy.start()

    images = image_rows_ref.shape[1]
    earlier = lax.broadcasted_iota(jnp.int32, (images, images), 0) <= lax.broadcasted_iota(
        jnp.int32, (images, images), 1
    )
    counts = jnp.broadcast_to(image_rows_ref[...], (8, images)).astype(F32)
    ends = dot(counts.astype(BF16), jnp.where(earlier, 1.0, 0.0).astype(BF16))[:1]
    starts = ends - counts[:1]
    mark_rows = low_mark.shape[0]
    row = (place * rows + lax.broadcasted_iota(jnp.int32, (mark_rows, 1), 0)).astype(F32)
    opens = jnp.sum(jnp.where(starts == row, 1.0, 0.0), axis=1, keepdims=True)
    opens = jnp.where(row >= ends[:, images - 1 :], 1.0, opens)
    missing = WINDOW - image_fill_ref[...].astype(F32)
    short = jnp.sum(jnp.where(ends == row + 1.0, missing, 0.0), axis=1, keepdims=True)
    low_mark[...] = jnp.broadcast_to(
        jnp.where(opens > 0.0, 0.0, -1.0 * WINDOW), low_mark.shape
    ).astype(jnp.int32)
    fill_mark[...] = jnp.broadcast_to(WINDOW - short, fill_mark.shape).astype(jnp.int32)

    for i in range(rows // CHUNK):
        here = slice(i * step, (i + 1) * step)
        scaled, inverse = standardize(x_ref[here, :].astype(F32))
        xhat[here, :] = scaled
        inv[here, :] = inverse
        value = (scaled * gain1_ref[...] + shift1_ref[...]).astype(BF16)
        normed_t[:, here] = value.T
        made = dot(value, weight[...]).astype(BF16)
        for part, buf in enumerate((qbuf, kbuf, vbuf)):
            buf[here, :] = made[:, part * HEAD_DIM : (part + 1) * HEAD_DIM]

    current, current_t, offset = masks()
    held = {}

    def score(r):
        held[r] = merged_scores(
            kbuf[(r - 1) * WINDOW : (r + 1) * WINDOW, :], qbuf[r * WINDOW : (r + 1) * WINDOW, :], current
        )

    def soften(r):
        weights = soft_weights(
            held[r], offset, low_mark[r : r + 1, :WINDOW], fill_mark[r : r + 1, :WINDOW]
        )
        probs[r] = weights
        held[r] = weights.astype(BF16)

    def gather(r):
        values = vbuf[(r - 1) * WINDOW : (r + 1) * WINDOW, :]
        att[r * WINDOW : (r + 1) * WINDOW, :] = window_sum(held.pop(r), values, current_t).astype(BF16)

    do(staggered([(r,) for r in range(1, rows)], score, soften, gather))
    for copy in later:
        copy.wait()
    cot_t[...] = cot_ref[...].T
    down_ref[...] = (down_ref[...].astype(F32) * 0.5).astype(BF16)


def in_vmem(array):
    return pltpu.with_memory_space_constraint(array, pltpu.VMEM)


def in_hbm(array):
    return pltpu.with_memory_space_constraint(array, pltpu.HBM)


def local(tokens, cotangent, down, image_rows, image_fill, gain1, shift1, weights):
    own, D = tokens.shape
    rows = own // WINDOW
    mark_rows = -(-(rows + 1) // 8) * 8
    vmem = pl.BlockSpec(memory_space=pltpu.VMEM)
    return pl.pallas_call(
        functools.partial(local_kernel, rows),
        out_shape=(
            pltpu.VMEM((own, D), F32),
            pltpu.VMEM((own, 1), F32),
            pltpu.VMEM((own, HEAD_DIM), BF16),
            pltpu.VMEM((own, HEAD_DIM), BF16),
            pltpu.VMEM((own, HEAD_DIM), BF16),
            pltpu.VMEM((rows, WINDOW, WINDOW), F32),
            pltpu.VMEM((own, HEAD_DIM), BF16),
            pltpu.VMEM((mark_rows, 128), jnp.int32),
            pltpu.VMEM((mark_rows, 128), jnp.int32),
            pltpu.VMEM((D, own), BF16),
            pltpu.VMEM((D, own), BF16),
            pltpu.VMEM((own, D), BF16),
            pltpu.VMEM(down.shape, BF16),
        ),
        in_specs=[vmem] + [pl.BlockSpec(memory_space=pltpu.HBM)] * 2 + [vmem] * 7,
        out_specs=(vmem,) * 13,
        scratch_shapes=[
            pltpu.VMEM((D, 3 * HEAD_DIM), BF16),
            pltpu.SemaphoreType.DMA((2,)),
        ],
        compiler_params=pltpu.CompilerParams(vmem_limit_bytes=24 * 1024 * 1024),
        name="local",
    )(
        in_vmem(tokens), in_hbm(cotangent), in_hbm(down), image_rows, image_fill, gain1, shift1, *weights[:3]
    )


def layer_kernel(
    rows,
    rim_ref,
    xhat,
    inv,
    own_q,
    own_k,
    own_v,
    own_probs,
    own_att,
    low_mark,
    fill_mark,
    normed_t,
    cot_t,
    cot_ref,
    down_ref,
    x_ref,
    up_ref,
    gain1_ref,
    shift1_ref,
    query_ref,
    key_ref,
    value_ref,
    out_ref,
    heads_ref,
    gain2_ref,
    shift2_ref,
    up_bias_ref,
    down_bias_ref,
    mixed_ref,
    in_grad_ref,
    keep_ref,
    send_ref,
    rim_x,
    rim_cot,
    halo_grad,
    wqkv,
    wother,
    wout,
    rim_q,
    rim_k,
    rim_v,
    qbuf,
    kbuf,
    vbuf,
    gbuf,
    att,
    probs,
    mid_grad,
    dqkv,
    act,
    hid_grad,
    mixed_buf,
    in_grad_buf,
    acc_down,
    acc_up,
    acc_qkv,
    acc_out,
    acc_vec,
    vec_rows,
    out_sem,
):
    D = x_ref.shape[1]
    FF = up_ref.shape[1]
    own = rows * WINDOW
    head = lax.axis_index("head")
    place = lax.axis_index("seq") * lax.axis_size("head") + head
    step = CHUNK * WINDOW
    steps = rows // CHUNK
    sent = {}

    for part, ref in enumerate((query_ref, key_ref, value_ref)):
        wqkv[:, part * D : part * D + HEAD_DIM] = ref[...]
        wqkv[:, part * D + HEAD_DIM : (part + 1) * D] = heads_ref[part * D : (part + 1) * D, :]
        wother[:, part * HEAD_DIM : (part + 1) * HEAD_DIM] = heads_ref[part * D : (part + 1) * D, :]
    wout[:HEAD_DIM, :] = out_ref[...]
    for half in range(D // HEAD_DIM):
        wout[HEAD_DIM:, half * HEAD_DIM : (half + 1) * HEAD_DIM] = heads_ref[
            3 * D + half * HEAD_DIM : 3 * D + (half + 1) * HEAD_DIM, :
        ]
    acc_vec[...] = jnp.zeros_like(acc_vec)

    for half in range(D // HEAD_DIM):
        cols = slice(half * HEAD_DIM, (half + 1) * HEAD_DIM)
        near = heads_ref[4 * D + half * 2 * WINDOW : 4 * D + (half + 1) * 2 * WINDOW, :]
        far = rim_ref[half * 2 * WINDOW : (half + 1) * 2 * WINDOW, :]
        rim_x[:WINDOW, cols] = jnp.where(head == 0, far[:WINDOW], near[:WINDOW])
        rim_x[WINDOW:, cols] = jnp.where(head == 0, near[:WINDOW], far[:WINDOW])
        rim_cot[:, cols] = jnp.where(head == 0, near[WINDOW:], far[WINDOW:])

    att[WINDOW:own, :HEAD_DIM] = own_att[WINDOW:, :]
    queries = (own_q, rim_q, qbuf)
    keys = (own_k, rim_k, kbuf)
    values = (own_v, rim_v, vbuf)

    def project_rim(j):
        here = slice(j * WINDOW, (j + 1) * WINDOW)
        there = slice(WINDOW, 2 * WINDOW) if j else slice(0, WINDOW)
        scaled, _ = standardize(rim_x[there, :].astype(F32))
        value = (scaled * gain1_ref[...] + shift1_ref[...]).astype(BF16)
        made = dot(value, wqkv[...]).astype(BF16)
        for part, (_, rim, other) in enumerate((queries, keys, values)):
            rim[there, :] = made[:, part * D : part * D + HEAD_DIM]
            other[here, :] = made[:, part * D + HEAD_DIM : (part + 1) * D]

    def project(i):
        here = slice(WINDOW + i * step, WINDOW + (i + 1) * step)
        value = xhat[i * step : (i + 1) * step, :] * gain1_ref[...] + shift1_ref[...]
        made = dot(value.astype(BF16), wother[...]).astype(BF16)
        for part, (_, _, other) in enumerate((queries, keys, values)):
            other[here, :] = made[:, part * HEAD_DIM : (part + 1) * HEAD_DIM]

    current, current_t, offset = masks()
    columns = [slice(h * HEAD_DIM, (h + 1) * HEAD_DIM) for h in range(HEADS)]
    held = {}

    def row_of(bufs, j, h):
        mine, rim, other = bufs
        if h:
            return other[j * WINDOW : (j + 1) * WINDOW, :]
        if 1 <= j <= rows:
            return mine[(j - 1) * WINDOW : j * WINDOW, :]
        return rim[WINDOW:, :] if j else rim[:WINDOW, :]

    def pair(bufs, j, h):
        if h:
            return bufs[2][(j - 1) * WINDOW : (j + 1) * WINDOW, :]
        if 1 < j <= rows:
            return bufs[0][(j - 2) * WINDOW : j * WINDOW, :]
        return jnp.concatenate([row_of(bufs, j - 1, 0), row_of(bufs, j, 0)])

    def grad_of(j, h):
        return gbuf[j * WINDOW : (j + 1) * WINDOW, columns[h]]

    def probs_of(j, h):
        if h:
            return probs.at[j - 1]
        return own_probs.at[j - 1] if 1 < j <= rows else probs.at[rows + 1 + (j > 1)]

    def key_sum(weights, queries):
        zero = jnp.zeros_like(weights)
        both = jnp.concatenate([jnp.where(current, zero, weights), jnp.where(current, weights, zero)])
        made = dot(both, queries)
        return made[:WINDOW], made[WINDOW:]

    def score(j, h):
        held[j, h] = merged_scores(pair(keys, j, h), row_of(queries, j, h), current)

    def soften(j, h):
        r = j - 1
        weights = soft_weights(
            held[j, h], offset, low_mark[r : r + 1, :WINDOW], fill_mark[r : r + 1, :WINDOW]
        )
        probs_of(j, h)[...] = weights
        held[j, h] = weights.astype(BF16)

    def gather(j, h):
        r = j - 1
        att[r * WINDOW : (r + 1) * WINDOW, columns[h]] = window_sum(
            held.pop((j, h)), pair(values, j, h), current_t
        ).astype(BF16)

    def feed_forward(first, count, own_rows):
        at = first * WINDOW
        size = count * WINDOW
        here = slice(at, at + size)
        held = {}
        block = 256
        slot = at // step % 2
        grads = hid_grad.at[slot] if own_rows else halo_grad
        xs, cots = (x_ref, cot_ref) if own_rows else (rim_x.at[pl.ds(WINDOW, WINDOW)], rim_cot)
        there = here if own_rows else slice(0, size)

        def enter():
            attended = att[here, :]
            middle = xs[there, :].astype(F32) + split_dot(attended, wout[...])
            scaled, inverse = standardize(middle)
            held.update(middle=middle, scaled=scaled, inverse=inverse)
            held["normed"] = (scaled * gain2_ref[...] + shift2_ref[...]).astype(BF16)

        def hide(f):
            cols = slice(f * block, (f + 1) * block)
            cot = cots[there, :]
            hidden = dot(held["normed"], up_ref[:, cols]) + up_bias_ref[:, cols]
            active, slope = twice_gelu(hidden)
            grad = dot_lanes(cot, down_ref[cols, :]) * slope
            grads[:size, cols] = grad.astype(BF16)
            if own_rows:
                act[slot, :size, cols] = active.astype(BF16)
                acc_vec[8:9, cols] += column_sums(grad)

        def weigh(f):
            cols = slice(f * block, (f + 1) * block)
            down_part = dot(cot_t[:, here], act[slot, :size, cols])
            up_part = dot_rows(held["normed"], grads[:size, cols])
            if at:
                acc_down[:, cols] += down_part
                acc_up[:, cols] += up_part
            else:
                acc_down[:, cols] = down_part
                acc_up[:, cols] = up_part

        def mix():
            if at >= 2 * step:
                sent["mixed", at // step - 2].wait()
            mixed_buf[slot, :, :] = (
                held["middle"] + split_dot(act[slot, :size], down_ref[...]) + down_bias_ref[...]
            ).astype(BF16)
            copy = pltpu.make_async_copy(
                mixed_buf.at[slot], mixed_ref.at[pl.ds(at, size)], out_sem.at[0, at // size]
            )
            copy.start()
            sent["mixed", at // step] = copy

        def back():
            scaled = held["scaled"]
            g2 = split_dot(grads[:size, :], up_ref[...], dot_lanes)
            cot32 = cots[there, :].astype(F32)
            middle_grad = cot32 + normalize_back(g2 * gain2_ref[...], scaled, held["inverse"])
            mixing_grad = middle_grad.astype(BF16)
            if own_rows:
                mid_grad[here, :] = middle_grad
                acc_vec[2:3, :D] += column_sums(g2 * scaled)
                acc_vec[3:4, :D] += column_sums(g2)
                acc_vec[4:5, :D] += column_sums(cot32)
                out_part = dot_rows(att[here, :], mixing_grad)
                if at:
                    acc_out[...] += out_part
                else:
                    acc_out[...] = out_part
            made = split_dot(mixing_grad, wout[...], dot_lanes).astype(BF16)
            for g in range(count):
                j = first + 1 + g
                gbuf[j * WINDOW : (j + 1) * WINDOW, :] = made[g * WINDOW : (g + 1) * WINDOW]

        call = functools.partial
        parts = FF // block
        hides = [call(hide, f) for f in range(parts)]
        weighs = [call(weigh, f) for f in range(parts)] if own_rows else []
        return enter, hides, weighs, mix, back

    held_back = {}
    unfinished = {}

    def weigh_grads(j, h):
        held_back[j, h] = merged_scores(pair(values, j, h), grad_of(j, h), current)

    def soften_back(j, h):
        dweights = held_back.pop((j, h))
        weights = probs_of(j, h)[...]
        inner = jnp.sum(weights * dweights, axis=0, keepdims=True)
        dscores = (weights * (dweights - inner)).astype(BF16)
        held_back[j, h] = (dscores, weights.astype(BF16))

    def gather_back(j, h):
        r = j - 1
        dscores, weights = held_back.pop((j, h))
        found = [key_sum(dscores, row_of(queries, j, h)), key_sum(weights, grad_of(j, h))]
        if j > 1:
            there = slice((r - 1) * WINDOW, r * WINDOW)
            for part, (before, _) in enumerate(found):
                total = unfinished[part, h] + before
                at = (part + 1) * D + h * HEAD_DIM
                dqkv[there, at : at + HEAD_DIM] = (total if part else total * SCALE).astype(BF16)
        for part, (_, current_part) in enumerate(found):
            unfinished[part, h] = current_part
        if j <= rows:
            dqkv[r * WINDOW : (r + 1) * WINDOW, columns[h]] = (
                window_sum(dscores, pair(keys, j, h), current_t) * SCALE
            ).astype(BF16)

    def project_back(i):
        at = i * step
        here = slice(at, at + step)
        found = {}

        def multiply():
            grads = dqkv[here, :]
            part = dot(normed_t[:, here], grads)
            acc_qkv[...] = (acc_qkv[...] + part) if at else part
            found["g1"] = split_dot(grads, wqkv[...], dot_lanes)

        def back():
            g1 = found["g1"]
            scaled = xhat[here, :]
            acc_vec[0:1, :D] += column_sums(g1 * scaled)
            acc_vec[1:2, :D] += column_sums(g1)
            if i > 1:
                sent["grad", i - 2].wait()
            in_grad_buf[i % 2, :, :] = (
                mid_grad[here, :] + normalize_back(g1 * gain1_ref[...], scaled, inv[here, :])
            ).astype(BF16)
            copy = pltpu.make_async_copy(
                in_grad_buf.at[i % 2], in_grad_ref.at[pl.ds(at, step)], out_sem.at[1, i]
            )
            copy.start()
            sent["grad", i] = copy

        return multiply, back

    def units(first, last):
        return [(j, h) for j in range(first, last + 1) for h in range(HEADS)]

    project_rim(0)
    project_rim(rows + 1)
    for i in range(steps):
        project(i)
    forward = [(j, h) for j, h in units(1, rows + 1) if h or not 1 < j <= rows]
    do(staggered(forward, score, soften, gather))
    feeds = [feed_forward(i * CHUNK, CHUNK, True) for i in range(steps)]
    halo_enter, halo_hides, _, _, halo_back = feed_forward(rows, 1, False)
    halo = [halo_enter] + halo_hides + [halo_back]
    enter, hides, weighs, mix, back = feeds[0]
    do([enter, halo.pop(0), hides[0], hides[1], weighs[0]])
    for i in range(steps):
        enter, hides, weighs, mix, back = feeds[i]
        for f in range(2, len(hides)):
            do([hides[f], weighs[f - 1]] + halo[:1])
            halo = halo[1:]
        if i + 1 < steps:
            later = feeds[i + 1]
            do([later[0], weighs[-1], later[1][0], mix, later[1][1], back, later[2][0]] + halo[:1])
            halo = halo[1:]
        else:
            do([weighs[-1]] + halo + [mix, back])

    core = (place & 2) // 2
    wide = FF // 2
    halves = ((core, keep_ref), (1 - core, send_ref))
    after_down = D // HEAD_DIM * wide
    after_up = after_down + wide // HEAD_DIM * D

    def export_down(c, ref, f):
        at = pl.ds(pl.multiple_of(c * wide + f, D), D)
        block = (acc_down[:, at] * 0.5).astype(BF16).T
        for half in range(D // HEAD_DIM):
            ref[half * wide + f : half * wide + f + D, :] = block[
                :, half * HEAD_DIM : (half + 1) * HEAD_DIM
            ]

    def export_up(c, ref, n):
        at = pl.ds(pl.multiple_of(c * wide + n * HEAD_DIM, HEAD_DIM), HEAD_DIM)
        ref[after_down + n * D : after_down + (n + 1) * D, :] = acc_up[:, at].astype(BF16)

    def export_heads(c, ref, h, part):
        mine = pl.ds(pl.multiple_of(c * HEAD_DIM, HEAD_DIM), HEAD_DIM)
        true_head = head if h == 0 else 1 - head
        if part < 3:
            at = part * D + h * HEAD_DIM
            block = acc_qkv[mine, at : at + HEAD_DIM]
        else:
            block = acc_out[h * HEAD_DIM : (h + 1) * HEAD_DIM, mine]
        at = after_up + (true_head * 4 + part) * HEAD_DIM
        ref[pl.ds(pl.multiple_of(at, HEAD_DIM), HEAD_DIM), :] = block.astype(BF16)

    def export_vectors(c, ref):
        flat = vec_rows[pl.ds(pl.multiple_of(c * 16, 16), 16), :].astype(BF16)
        ref[after_up + 8 * HEAD_DIM :, :] = jnp.concatenate([flat] * (VECTOR_ROWS // 16))

    call = functools.partial
    exports = [call(export_down, c, ref, f) for c, ref in halves for f in range(0, wide, D)]
    exports += [call(export_up, c, ref, n) for c, ref in halves for n in range(wide // HEAD_DIM)]
    exports += [call(export_heads, c, ref, h, 3) for c, ref in halves for h in range(HEADS)]
    ends = [project_back(i) for i in range(steps)]
    backs = staggered(units(1, rows + 1), weigh_grads, soften_back, gather_back)
    marks = []
    for i in range(steps):
        done = [n for n, job in enumerate(backs) if job.func is gather_back and job.args == ((i + 1) * CHUNK + 1, 1)]
        marks.append(done[0] + 1)
    exports = merge(exports, list(range(0)))
    share = -(-len(exports) // marks[0])
    do(merge(backs[: marks[0]], exports))
    for i in range(1, steps):
        ends[i - 1][0]()
        do(merge(backs[marks[i - 1] : marks[i]], [ends[i - 1][1]]))
    do(backs[marks[-1] :])
    ends[-1][0]()
    ends[-1][1]()

    for c, ref in halves:
        do([call(export_heads, c, ref, h, part) for h in range(HEADS) for part in range(3)])
    for n, (row, cols) in enumerate(vector_slots(FF, D)):
        vec_rows[n : n + 1, :] = acc_vec[row : row + 1, cols]
    for c, ref in halves:
        export_vectors(c, ref)
    for kind in ("mixed", "grad"):
        for i in range(max(steps - 2, 0), steps):
            sent[kind, i].wait()


def layer(
    rim, made, tokens, up, gain1, shift1, weights, other, gain2, shift2, up_bias, down_bias
):
    own, D = tokens.shape
    FF = up.shape[1]
    rows = own // WINDOW
    count = own + 2 * WINDOW
    half = half_rows(FF, D)
    tokens, up, rim, other = in_vmem(tokens), in_vmem(up), in_vmem(rim), in_vmem(other)
    made = [in_vmem(array) for array in made]
    vmem = pl.BlockSpec(memory_space=pltpu.VMEM)
    anywhere = pl.BlockSpec(memory_space=pl.ANY)
    steps = rows // CHUNK
    return pl.pallas_call(
        functools.partial(layer_kernel, rows),
        out_shape=(
            jax.ShapeDtypeStruct((own, D), BF16),
            jax.ShapeDtypeStruct((own, D), BF16),
            pltpu.VMEM((half, HEAD_DIM), BF16),
            pltpu.VMEM((half, HEAD_DIM), BF16),
        ),
        in_specs=[vmem] * 27,
        out_specs=(anywhere, anywhere, vmem, vmem),
        scratch_shapes=[
            pltpu.VMEM((2 * WINDOW, D), BF16),
            pltpu.VMEM((WINDOW, D), BF16),
            pltpu.VMEM((WINDOW, FF), BF16),
            pltpu.VMEM((D, 3 * D), BF16),
            pltpu.VMEM((D, 3 * HEAD_DIM), BF16),
            pltpu.VMEM((D, D), BF16),
            pltpu.VMEM((2 * WINDOW, HEAD_DIM), BF16),
            pltpu.VMEM((2 * WINDOW, HEAD_DIM), BF16),
            pltpu.VMEM((2 * WINDOW, HEAD_DIM), BF16),
            pltpu.VMEM((count, HEAD_DIM), BF16),
            pltpu.VMEM((count, HEAD_DIM), BF16),
            pltpu.VMEM((count, HEAD_DIM), BF16),
            pltpu.VMEM((count, D), BF16),
            pltpu.VMEM((count - WINDOW, D), BF16),
            pltpu.VMEM((rows + 3, WINDOW, WINDOW), F32),
            pltpu.VMEM((own, D), F32),
            pltpu.VMEM((own, 3 * D), BF16),
            pltpu.VMEM((2, CHUNK * WINDOW, FF), BF16),
            pltpu.VMEM((2, CHUNK * WINDOW, FF), BF16),
            pltpu.VMEM((2, CHUNK * WINDOW, D), BF16),
            pltpu.VMEM((2, CHUNK * WINDOW, D), BF16),
            pltpu.VMEM((D, FF), F32),
            pltpu.VMEM((D, FF), F32),
            pltpu.VMEM((D, 3 * D), F32),
            pltpu.VMEM((D, D), F32),
            pltpu.VMEM((16, FF), F32),
            pltpu.VMEM((32, HEAD_DIM), F32),
            pltpu.SemaphoreType.DMA((2, steps)),
        ],
        compiler_params=pltpu.CompilerParams(vmem_limit_bytes=34 * 1024 * 1024),
        name="layer",
    )(
        rim, *made, tokens, up, gain1, shift1, *weights, other, gain2, shift2, up_bias, down_bias
    )


def pack_kernel(query_ref, key_ref, value_ref, out_ref, tok_ref, cot_ref, near_ref, far_ref, sem):
    D = query_ref.shape[0]
    own = tok_ref.shape[0]
    head = lax.axis_index("head")
    moves = [
        (ref, near_ref.at[pl.ds(part * D, D)]) for part, ref in enumerate((query_ref, key_ref, value_ref))
    ]
    last = own - WINDOW
    near_from = pl.multiple_of((1 - head) * last, WINDOW)
    far_from = pl.multiple_of(head * last, WINDOW)
    for half in range(D // HEAD_DIM):
        cols = pl.ds(half * HEAD_DIM, HEAD_DIM)
        moves.append((out_ref.at[:, cols], near_ref.at[pl.ds(3 * D + half * HEAD_DIM, HEAD_DIM)]))
        for k, ref in enumerate((tok_ref, cot_ref)):
            at = (half * 2 + k) * WINDOW
            moves.append((ref.at[pl.ds(near_from, WINDOW), cols], near_ref.at[pl.ds(4 * D + at, WINDOW)]))
            moves.append((ref.at[pl.ds(far_from, WINDOW), cols], far_ref.at[pl.ds(at, WINDOW)]))
    copies = [pltpu.make_async_copy(a, b, sem.at[n]) for n, (a, b) in enumerate(moves)]
    for copy in copies:
        copy.start()
    for copy in copies:
        copy.wait()


def pack(query_weight, key_weight, value_weight, out_weight, tokens, cotangent):
    D = query_weight.shape[0]
    rim = 2 * WINDOW * D // HEAD_DIM
    anywhere = pl.BlockSpec(memory_space=pl.ANY)
    vmem = pl.BlockSpec(memory_space=pltpu.VMEM)
    return pl.pallas_call(
        pack_kernel,
        out_shape=(pltpu.VMEM((4 * D + rim, HEAD_DIM), BF16), pltpu.VMEM((rim, HEAD_DIM), BF16)),
        in_specs=[anywhere] * 6,
        out_specs=(vmem, vmem),
        scratch_shapes=[pltpu.SemaphoreType.DMA((3 + 5 * (D // HEAD_DIM),))],
        name="pack",
    )(query_weight, key_weight, value_weight, out_weight, tokens, cotangent)


def finish_kernel(FF, D, mine_ref, other_ref, *refs):
    outs, (down_buf, up_buf, vec_rows, sem) = refs[:12], refs[12:]
    gain1, shift1, query, key, value, out, gain2, shift2, up, up_bias, down, down_bias = outs
    core = lax.axis_index("seq") % 2
    head = lax.axis_index("head")
    halves = ((core, mine_ref), (1 - core, other_ref))
    wide = FF // 2
    for c, ref in halves:
        rows = pl.ds(pl.multiple_of(c * wide, wide), wide)
        for half in range(D // HEAD_DIM):
            down_buf[rows, half * HEAD_DIM : (half + 1) * HEAD_DIM] = ref[
                half * wide : (half + 1) * wide, :
            ].astype(F32)
    copies = [pltpu.make_async_copy(down_buf, down, sem.at[0])]
    copies[0].start()
    start = D // HEAD_DIM * wide
    for c, ref in halves:
        for n, f in enumerate(range(0, wide, HEAD_DIM)):
            at = pl.ds(pl.multiple_of(c * wide + f, HEAD_DIM), HEAD_DIM)
            up_buf[:, at] = ref[start + n * D : start + (n + 1) * D, :].astype(F32)
    copies.append(pltpu.make_async_copy(up_buf, up, sem.at[1]))
    copies[1].start()
    start += wide // HEAD_DIM * D
    for c, ref in halves:
        mine = pl.ds(pl.multiple_of(c * HEAD_DIM, HEAD_DIM), HEAD_DIM)
        base = start + head * (4 * HEAD_DIM)
        for part, made in enumerate((query, key, value)):
            at = pl.multiple_of(base + part * HEAD_DIM, HEAD_DIM)
            made[mine, :] = ref[pl.ds(at, HEAD_DIM), :].astype(F32)
        at = pl.multiple_of(base + 3 * HEAD_DIM, HEAD_DIM)
        out[:, mine] = ref[pl.ds(at, HEAD_DIM), :].astype(F32)
        base = start + 8 * HEAD_DIM
        vec_rows[pl.ds(pl.multiple_of(c * 16, 16), 16), :] = ref[base : base + 16, :].astype(F32)
    vectors = (gain1, shift1, gain2, shift2, down_bias)
    for s, (n, cols) in enumerate(vector_slots(FF, D)):
        made = up_bias if n == 8 else vectors[n]
        made[cols] = vec_rows[s, :]
    for copy in copies:
        copy.wait()


def finish(mine, other, FF, D):
    vmem = pl.BlockSpec(memory_space=pltpu.VMEM)
    anywhere = pl.BlockSpec(memory_space=pl.ANY)
    shapes = [(D,), (D,)] + [(D, HEAD_DIM)] * 3 + [(HEAD_DIM, D), (D,), (D,), (D, FF), (FF,), (FF, D), (D,)]
    return pl.pallas_call(
        functools.partial(finish_kernel, FF, D),
        out_shape=tuple(jax.ShapeDtypeStruct(shape, F32) for shape in shapes),
        in_specs=[vmem, vmem],
        out_specs=tuple(anywhere if n in (8, 10) else vmem for n in range(len(shapes))),
        scratch_shapes=[
            pltpu.VMEM((FF, D), F32),
            pltpu.VMEM((D, FF), F32),
            pltpu.VMEM((32, HEAD_DIM), F32),
            pltpu.SemaphoreType.DMA((2,)),
        ],
        name="finish",
    )(in_vmem(mine), in_vmem(other))


def spans(masks):
    found = [0]
    for mask in masks:
        found = found + [f ^ mask for f in found]
    return found


def stages(count):
    bits = [1 << b for b in range(count.bit_length() - 1)]
    plane, rest = [bits[0], bits[2]], bits[3:]
    found = [plane] + [rest[i : i + 2] for i in range(0, len(rest), 2)]
    if len(found) > 1 and len(found[1]) == 2:
        return [(found[0], found[1]), (found[1], found[0])] + [(masks, masks) for masks in found[2:]]
    return [(masks, masks) for masks in found]


def partners(value, masks, k):
    count = lax.axis_size("seq") * lax.axis_size("head")
    hops = [spans(side)[k] for side in masks]
    return lax.ppermute(value, BOTH, [(i, i ^ hops[i // 2 % 2]) for i in range(count)])


def all_sum(value):
    count = lax.axis_size("seq") * lax.axis_size("head")
    place = lax.axis_index("seq") * lax.axis_size("head") + lax.axis_index("head")
    width = value.shape[1]
    steps = []
    for masks in stages(count):
        code, other_code = (
            sum(((place & mask) // mask) << j for j, mask in enumerate(side)) for side in masks
        )
        steps.append((masks, jnp.where(place & 2 == 0, code, other_code)))
    def spread(value, masks, code):
        parts = 1 << len(masks[0])
        found = [value] + [partners(value, masks, k) for k in range(1, parts)]
        whole = jnp.zeros((parts,) + value.shape, value.dtype)
        for k, part in enumerate(found):
            whole = lax.dynamic_update_index_in_dim(whole, part, code ^ k, 0)
        return whole

    for masks, code in steps[:-1]:
        parts = value.reshape(1 << len(masks[0]), -1, width)
        total = lax.dynamic_index_in_dim(parts, code, 0, False).astype(F32)
        arrived = [
            partners(lax.dynamic_index_in_dim(parts, code ^ k, 0, False), masks, k)
            for k in range(1, parts.shape[0])
        ]
        for part in arrived:
            total = total + part.astype(F32)
        value = total.astype(BF16)
    whole = spread(value, *steps[-1])
    total = whole[0].astype(F32)
    for part in whole[1:]:
        total = total + part.astype(F32)
    value = total.astype(BF16)
    for masks, code in steps[-2::-1]:
        value = spread(value, masks, code).reshape(-1, width)
    return value


def across_cores(value):
    return partners(value, ([2], [2]), 1)


def shards(
    tokens,
    cotangent,
    image_rows,
    image_fill,
    first_gain,
    first_shift,
    query_weight,
    key_weight,
    value_weight,
    out_weight,
    second_gain,
    second_shift,
    up_weight,
    up_bias,
    down_weight,
    down_bias,
):
    own, D = tokens.shape
    FF = up_weight.shape[1]
    devices = lax.axis_size("seq") * lax.axis_size("head")
    near, far = pack(query_weight, key_weight, value_weight, out_weight, tokens, cotangent)
    other = lax.ppermute(near, "head", [(0, 1), (1, 0)])
    pairs = [(i, i + 1) for i in range(1, devices - 1, 2)]
    rim = lax.ppermute(far, BOTH, pairs + [(b, a) for a, b in pairs])
    weights = (query_weight, key_weight, value_weight, out_weight)
    gain1, shift1 = first_gain[None], first_shift[None]
    made = local(tokens, cotangent, down_weight, image_rows[None], image_fill[None], gain1, shift1, weights)
    mixed, input_grad, keep, send = layer(
        rim,
        made,
        tokens,
        up_weight,
        gain1,
        shift1,
        weights,
        other,
        second_gain[None],
        second_shift[None],
        up_bias[None],
        down_bias[None],
    )
    summed = (keep.astype(F32) + across_cores(send).astype(F32)).astype(BF16)
    mine = all_sum(summed)
    return (mixed, input_grad, *finish(mine, across_cores(mine), FF, D))


def solution(mesh):
    stream = P(("seq", "head"), None)
    columns = P(None, "head")
    in_specs = (stream, stream) + (P(),) * 4 + (columns,) * 3 + (P("head", None),) + (P(),) * 6
    out_specs = (
        (stream, stream) + (P(),) * 2 + (columns,) * 3 + (P("head", None),) + (P(),) * 6
    )
    return jax.shard_map(shards, mesh=mesh, in_specs=in_specs, out_specs=out_specs, check_vma=False)
```

```python
import functools

import jax
import jax.numpy as jnp
from jax import lax
from jax.experimental import pallas as pl
from jax.experimental.pallas import tpu as pltpu
from jax.sharding import PartitionSpec as P

HEAD_DIM = 128
HEADS = 2
WINDOW = 96
BOTH = ("seq", "head")

EPSILON = 1e-05
MASKED = -1000000000.0
LOG2E = 1.4426950408889634
SCALE = HEAD_DIM ** (-0.5)

F32 = jnp.float32
BF16 = jnp.bfloat16
LANES = (((1,), (1,)), ((), ()))
ROWS = (((0,), (0,)), ((), ()))

CHUNK = 8
LAG = 4


def dot(a, b):
    return jnp.dot(a, b, preferred_element_type=F32)


def split_dot(a, b, how=None):
    how = how or dot
    half = a.shape[0] // 2
    if half % 16:
        return how(a, b)
    return jnp.concatenate([how(a[:half], b), how(a[half:], b)])


def dot_lanes(a, b):
    return lax.dot_general(a, b, LANES, preferred_element_type=F32)


def dot_rows(a, b):
    return lax.dot_general(a, b, ROWS, preferred_element_type=F32)


def standardize(inputs):
    center = inputs - jnp.mean(inputs, axis=1, keepdims=True)
    spread = jnp.mean(center * center, axis=1, keepdims=True)
    inverse = lax.rsqrt(spread + EPSILON)
    return center * inverse, inverse


def normalize_back(weighted, scaled, inverse):
    return inverse * (
        weighted
        - jnp.mean(weighted, axis=1, keepdims=True)
        - scaled * jnp.mean(weighted * scaled, axis=1, keepdims=True)
    )


def twice_gelu(x):
    z = x * 0.7071067811865476
    below = 1.0 + lax.erf(z)
    bell = jnp.exp2(z * z * -LOG2E)
    return x * below, below + x * bell * 0.7978845608028654


def column_sums(value):
    return jnp.sum(value, axis=0, keepdims=True)


def merge(*lists):
    marked = [
        ((n + 0.5) / len(work), k, n, job) for k, work in enumerate(lists) for n, job in enumerate(work)
    ]
    return [job for *_, job in sorted(marked, key=lambda item: item[:3])]


VECTOR_ROWS = 128


def half_rows(FF, D):
    return (2 * FF * D + 4 * D * D) // (2 * HEAD_DIM) + VECTOR_ROWS


def vector_slots(FF, D):
    found = [
        (n, slice(c, c + HEAD_DIM)) for n in range(5) for c in range(0, D, HEAD_DIM)
    ]
    return found + [(8, slice(c, c + HEAD_DIM)) for c in range(0, FF, HEAD_DIM)]


def masks():
    key_id = lax.broadcasted_iota(jnp.int32, (WINDOW, WINDOW), 0)
    query_id = lax.broadcasted_iota(jnp.int32, (WINDOW, WINDOW), 1)
    current = key_id <= query_id
    return current, key_id >= query_id, jnp.where(current, key_id, key_id - WINDOW)


def merged_scores(keys, query, current):
    raw = dot_lanes(keys, query)
    return jnp.where(current, raw[WINDOW:], raw[:WINDOW])


def soft_weights(scores, offset, low, fill):
    keep = (offset >= low) & (offset < fill)
    scores = jnp.where(keep, scores * (SCALE * LOG2E), MASKED * LOG2E)
    lifted = jnp.exp2(scores - jnp.max(scores, axis=0, keepdims=True))
    return lifted * (1.0 / jnp.sum(lifted, axis=0, keepdims=True))


def window_sum(weights, values, current_t):
    turned = weights.T
    zero = jnp.zeros_like(turned)
    return dot(jnp.where(current_t, zero, turned), values[:WINDOW]) + dot(
        jnp.where(current_t, turned, zero), values[WINDOW:]
    )


def staggered(units, *kinds):
    jobs = []
    for t in range(len(units) + LAG * (len(kinds) - 1)):
        for k, kind in enumerate(kinds):
            if 0 <= t - LAG * k < len(units):
                jobs.append(functools.partial(kind, *units[t - LAG * k]))
    return jobs


def do(jobs):
    for job in jobs:
        job()


def local_kernel(
    rows,
    x_ref,
    cot_in_ref,
    down_in_ref,
    image_rows_ref,
    image_fill_ref,
    gain1_ref,
    shift1_ref,
    query_ref,
    key_ref,
    value_ref,
    normed,
    qbuf,
    kbuf,
    vbuf,
    probs,
    att,
    low_mark,
    fill_mark,
    xhat_t,
    cot_t,
    cot_ref,
    down_ref,
    cot_sum,
    weight,
    in_sem,
):
    D = x_ref.shape[1]
    step = CHUNK * WINDOW
    xhat_t[D:, :] = jnp.ones((16, rows * WINDOW), BF16)
    place = lax.axis_index("seq") * lax.axis_size("head") + lax.axis_index("head")
    for part, ref in enumerate((query_ref, key_ref, value_ref)):
        weight[:, part * HEAD_DIM : (part + 1) * HEAD_DIM] = ref[...]
    later = [
        pltpu.make_async_copy(a, b, in_sem.at[n])
        for n, (a, b) in enumerate(((cot_in_ref, cot_ref), (down_in_ref, down_ref)))
    ]
    for copy in later:
        copy.start()

    images = image_rows_ref.shape[1]
    earlier = lax.broadcasted_iota(jnp.int32, (images, images), 0) <= lax.broadcasted_iota(
        jnp.int32, (images, images), 1
    )
    counts = jnp.broadcast_to(image_rows_ref[...], (8, images)).astype(F32)
    ends = dot(counts.astype(BF16), jnp.where(earlier, 1.0, 0.0).astype(BF16))[:1]
    starts = ends - counts[:1]
    mark_rows = low_mark.shape[0]
    row = (place * rows + lax.broadcasted_iota(jnp.int32, (mark_rows, 1), 0)).astype(F32)
    opens = jnp.sum(jnp.where(starts == row, 1.0, 0.0), axis=1, keepdims=True)
    opens = jnp.where(row >= ends[:, images - 1 :], 1.0, opens)
    missing = WINDOW - image_fill_ref[...].astype(F32)
    short = jnp.sum(jnp.where(ends == row + 1.0, missing, 0.0), axis=1, keepdims=True)
    low_mark[...] = jnp.broadcast_to(
        jnp.where(opens > 0.0, 0.0, -1.0 * WINDOW), low_mark.shape
    ).astype(jnp.int32)
    fill_mark[...] = jnp.broadcast_to(WINDOW - short, fill_mark.shape).astype(jnp.int32)

    for i in range(rows // CHUNK):
        here = slice(i * step, (i + 1) * step)
        scaled, _ = standardize(x_ref[here, :].astype(F32))
        xhat_t[:D, here] = scaled.astype(BF16).T
        value = (scaled * gain1_ref[...] + shift1_ref[...]).astype(BF16)
        normed[here, :] = value
        made = dot(value, weight[...]).astype(BF16)
        for part, buf in enumerate((qbuf, kbuf, vbuf)):
            buf[here, :] = made[:, part * HEAD_DIM : (part + 1) * HEAD_DIM]

    current, current_t, offset = masks()
    held = {}

    def score(r):
        held[r] = merged_scores(
            kbuf[(r - 1) * WINDOW : (r + 1) * WINDOW, :], qbuf[r * WINDOW : (r + 1) * WINDOW, :], current
        )

    def soften(r):
        weights = soft_weights(
            held[r], offset, low_mark[r : r + 1, :WINDOW], fill_mark[r : r + 1, :WINDOW]
        )
        probs[r] = weights
        held[r] = weights.astype(BF16)

    def gather(r):
        values = vbuf[(r - 1) * WINDOW : (r + 1) * WINDOW, :]
        att[r * WINDOW : (r + 1) * WINDOW, :] = window_sum(held.pop(r), values, current_t).astype(BF16)

    do(staggered([(r,) for r in range(1, rows)], score, soften, gather))
    for copy in later:
        copy.wait()
    cot_t[...] = cot_ref[...].T
    down_ref[...] = (down_ref[...].astype(F32) * 0.5).astype(BF16)
    total = jnp.zeros((8, D), F32)
    for i in range(rows // CHUNK):
        total += jnp.sum(cot_ref[i * step : (i + 1) * step, :].astype(F32).reshape(step // 8, 8, D), axis=0)
    cot_sum[...] = total


def in_vmem(array):
    return pltpu.with_memory_space_constraint(array, pltpu.VMEM)


def in_hbm(array):
    return pltpu.with_memory_space_constraint(array, pltpu.HBM)


def local(tokens, cotangent, down, image_rows, image_fill, gain1, shift1, weights):
    own, D = tokens.shape
    rows = own // WINDOW
    mark_rows = -(-(rows + 1) // 8) * 8
    vmem = pl.BlockSpec(memory_space=pltpu.VMEM)
    return pl.pallas_call(
        functools.partial(local_kernel, rows),
        out_shape=(
            pltpu.VMEM((own, D), BF16),
            pltpu.VMEM((own, HEAD_DIM), BF16),
            pltpu.VMEM((own, HEAD_DIM), BF16),
            pltpu.VMEM((own, HEAD_DIM), BF16),
            pltpu.VMEM((rows, WINDOW, WINDOW), F32),
            pltpu.VMEM((own, HEAD_DIM), BF16),
            pltpu.VMEM((mark_rows, 128), jnp.int32),
            pltpu.VMEM((mark_rows, 128), jnp.int32),
            pltpu.VMEM((D + 16, own), BF16),
            pltpu.VMEM((D, own), BF16),
            pltpu.VMEM((own, D), BF16),
            pltpu.VMEM(down.shape, BF16),
            pltpu.VMEM((8, D), F32),
        ),
        in_specs=[vmem] + [pl.BlockSpec(memory_space=pltpu.HBM)] * 2 + [vmem] * 7,
        out_specs=(vmem,) * 13,
        scratch_shapes=[
            pltpu.VMEM((D, 3 * HEAD_DIM), BF16),
            pltpu.SemaphoreType.DMA((2,)),
        ],
        compiler_params=pltpu.CompilerParams(vmem_limit_bytes=24 * 1024 * 1024),
        name="local",
    )(
        in_vmem(tokens), in_hbm(cotangent), in_hbm(down), image_rows, image_fill, gain1, shift1, *weights[:3]
    )


def layer_kernel(
    rows,
    rim_ref,
    normed,
    own_q,
    own_k,
    own_v,
    own_probs,
    own_att,
    low_mark,
    fill_mark,
    xhat_t,
    cot_t,
    cot_ref,
    down_ref,
    cot_sum,
    x_ref,
    up_ref,
    gain1_ref,
    shift1_ref,
    query_ref,
    key_ref,
    value_ref,
    out_ref,
    heads_ref,
    gain2_ref,
    shift2_ref,
    up_bias_ref,
    keep_ref,
    send_ref,
    act_out,
    att_out,
    mid_grad_out,
    dqkv_out,
    wqkv_out,
    wout_out,
    act,
    att,
    mid_grad,
    dqkv,
    wqkv,
    wout,
    rim_x,
    rim_cot,
    halo_grad,
    halo_att,
    wother,
    rim_q,
    rim_k,
    rim_v,
    qbuf,
    kbuf,
    vbuf,
    gbuf,
    probs,
    hid_grad,
    acc_down,
    acc_up,
    acc_qkv,
    acc_out,
    acc_vec,
    vec_rows,
    out_sem,
):
    D = x_ref.shape[1]
    FF = up_ref.shape[1]
    own = rows * WINDOW
    head = lax.axis_index("head")
    place = lax.axis_index("seq") * lax.axis_size("head") + head
    step = CHUNK * WINDOW
    steps = rows // CHUNK
    leaving = {}

    def leave(kind, n, source, target):
        leaving[kind, n] = pltpu.make_async_copy(source, target, out_sem.at[kind, n])
        leaving[kind, n].start()

    for part, ref in enumerate((query_ref, key_ref, value_ref)):
        wqkv[:, part * D : part * D + HEAD_DIM] = ref[...]
        wqkv[:, part * D + HEAD_DIM : (part + 1) * D] = heads_ref[part * D : (part + 1) * D, :]
        wother[:, part * HEAD_DIM : (part + 1) * HEAD_DIM] = heads_ref[part * D : (part + 1) * D, :]
    wout[:HEAD_DIM, :] = out_ref[...]
    for half in range(D // HEAD_DIM):
        wout[HEAD_DIM:, half * HEAD_DIM : (half + 1) * HEAD_DIM] = heads_ref[
            3 * D + half * HEAD_DIM : 3 * D + (half + 1) * HEAD_DIM, :
        ]
    leave(4, 0, wqkv, wqkv_out)
    leave(4, 1, wout, wout_out)
    acc_vec[...] = jnp.zeros_like(acc_vec)

    for half in range(D // HEAD_DIM):
        cols = slice(half * HEAD_DIM, (half + 1) * HEAD_DIM)
        near = heads_ref[4 * D + half * 2 * WINDOW : 4 * D + (half + 1) * 2 * WINDOW, :]
        far = rim_ref[half * 2 * WINDOW : (half + 1) * 2 * WINDOW, :]
        rim_x[:WINDOW, cols] = jnp.where(head == 0, far[:WINDOW], near[:WINDOW])
        rim_x[WINDOW:, cols] = jnp.where(head == 0, near[:WINDOW], far[:WINDOW])
        rim_cot[:, cols] = jnp.where(head == 0, near[WINDOW:], far[WINDOW:])

    att[WINDOW:, :HEAD_DIM] = own_att[WINDOW:, :]
    queries = (own_q, rim_q, qbuf)
    keys = (own_k, rim_k, kbuf)
    values = (own_v, rim_v, vbuf)

    def project_rim(j):
        here = slice(j * WINDOW, (j + 1) * WINDOW)
        there = slice(WINDOW, 2 * WINDOW) if j else slice(0, WINDOW)
        scaled, _ = standardize(rim_x[there, :].astype(F32))
        value = (scaled * gain1_ref[...] + shift1_ref[...]).astype(BF16)
        made = dot(value, wqkv[...]).astype(BF16)
        for part, (_, rim, other) in enumerate((queries, keys, values)):
            rim[there, :] = made[:, part * D : part * D + HEAD_DIM]
            other[here, :] = made[:, part * D + HEAD_DIM : (part + 1) * D]

    def project(i):
        here = slice(WINDOW + i * step, WINDOW + (i + 1) * step)
        made = dot(normed[i * step : (i + 1) * step, :], wother[...]).astype(BF16)
        for part, (_, _, other) in enumerate((queries, keys, values)):
            other[here, :] = made[:, part * HEAD_DIM : (part + 1) * HEAD_DIM]

    current, current_t, offset = masks()
    columns = [slice(h * HEAD_DIM, (h + 1) * HEAD_DIM) for h in range(HEADS)]
    held = {}

    def row_of(bufs, j, h):
        mine, rim, other = bufs
        if h:
            return other[j * WINDOW : (j + 1) * WINDOW, :]
        if 1 <= j <= rows:
            return mine[(j - 1) * WINDOW : j * WINDOW, :]
        return rim[WINDOW:, :] if j else rim[:WINDOW, :]

    def pair(bufs, j, h):
        if h:
            return bufs[2][(j - 1) * WINDOW : (j + 1) * WINDOW, :]
        if 1 < j <= rows:
            return bufs[0][(j - 2) * WINDOW : j * WINDOW, :]
        return jnp.concatenate([row_of(bufs, j - 1, 0), row_of(bufs, j, 0)])

    def grad_of(j, h):
        return gbuf[j * WINDOW : (j + 1) * WINDOW, columns[h]]

    def probs_of(j, h):
        if h:
            return probs.at[j - 1]
        return own_probs.at[j - 1] if 1 < j <= rows else probs.at[rows + 1 + (j > 1)]

    def key_sum(weights, queries):
        zero = jnp.zeros_like(weights)
        both = jnp.concatenate([jnp.where(current, zero, weights), jnp.where(current, weights, zero)])
        made = dot(both, queries)
        return made[:WINDOW], made[WINDOW:]

    def score(j, h):
        held[j, h] = merged_scores(pair(keys, j, h), row_of(queries, j, h), current)

    def soften(j, h):
        r = j - 1
        weights = soft_weights(
            held[j, h], offset, low_mark[r : r + 1, :WINDOW], fill_mark[r : r + 1, :WINDOW]
        )
        probs_of(j, h)[...] = weights
        held[j, h] = weights.astype(BF16)

    def gather(j, h):
        r = j - 1
        made = window_sum(held.pop((j, h)), pair(values, j, h), current_t).astype(BF16)
        if r < rows:
            att[r * WINDOW : (r + 1) * WINDOW, columns[h]] = made
        else:
            halo_att[:, columns[h]] = made

    def feed_forward(first, count, own_rows):
        at = first * WINDOW
        size = count * WINDOW
        here = slice(at, at + size)
        held = {}
        block = 256
        slot = at // step % 2
        grads = hid_grad.at[slot] if own_rows else halo_grad
        xs, cots, atts = (x_ref, cot_ref, att) if own_rows else (rim_x.at[pl.ds(WINDOW, WINDOW)], rim_cot, halo_att)
        there = here if own_rows else slice(0, size)

        def enter():
            if own_rows:
                if at >= 2 * step:
                    leaving[0, at // step - 2].wait()
                    leaving[2, at // step - 2].wait()
                leave(1, at // step, att.at[pl.ds(at, size)], att_out.at[pl.ds(at, size)])
            attended = atts[there, :]
            middle = xs[there, :].astype(F32) + split_dot(attended, wout[...])
            scaled, inverse = standardize(middle)
            held.update(scaled=scaled, inverse=inverse)
            held["normed"] = (scaled * gain2_ref[...] + shift2_ref[...]).astype(BF16)

        def hide(f):
            cols = slice(f * block, (f + 1) * block)
            hidden = dot(held["normed"], up_ref[:, cols]) + up_bias_ref[:, cols]
            active, slope = twice_gelu(hidden)
            grad = dot_lanes(cots[there, :], down_ref[cols, :]) * slope
            grads[:size, cols] = grad.astype(BF16)
            if own_rows:
                act[slot, :size, cols] = active.astype(BF16)
                acc_vec[8:9, cols] += column_sums(grad)

        def weigh(f):
            cols = slice(f * block, (f + 1) * block)
            down_part = dot(cot_t[:, here], act[slot, :size, cols])
            up_part = dot_rows(held["normed"], grads[:size, cols])
            if at:
                acc_down[:, cols] += down_part
                acc_up[:, cols] += up_part
            else:
                acc_down[:, cols] = down_part
                acc_up[:, cols] = up_part

        def back():
            if own_rows:
                leave(0, at // step, act.at[slot], act_out.at[pl.ds(at, size)])
            scaled = held["scaled"]
            g2 = split_dot(grads[:size, :], up_ref[...], dot_lanes)
            cot32 = cots[there, :].astype(F32)
            middle_grad = cot32 + normalize_back(g2 * gain2_ref[...], scaled, held["inverse"])
            mixing_grad = middle_grad.astype(BF16)
            if own_rows:
                mid_grad[slot, :, :] = middle_grad
                leave(2, at // step, mid_grad.at[slot], mid_grad_out.at[pl.ds(at, size)])
                acc_vec[2:3, :D] += column_sums(g2 * scaled)
                acc_vec[3:4, :D] += column_sums(g2)
                out_part = dot_rows(atts[there, :], mixing_grad)
                if at:
                    acc_out[...] += out_part
                else:
                    acc_out[...] = out_part
            made = split_dot(mixing_grad, wout[...], dot_lanes).astype(BF16)
            for g in range(count):
                j = first + 1 + g
                gbuf[j * WINDOW : (j + 1) * WINDOW, :] = made[g * WINDOW : (g + 1) * WINDOW]

        call = functools.partial
        parts = FF // block
        hides = [call(hide, f) for f in range(parts)]
        weighs = [call(weigh, f) for f in range(parts)] if own_rows else []
        return enter, hides, weighs, back

    held_back = {}
    unfinished = {}

    def weigh_grads(j, h):
        held_back[j, h] = merged_scores(pair(values, j, h), grad_of(j, h), current)

    def soften_back(j, h):
        dweights = held_back.pop((j, h))
        weights = probs_of(j, h)[...]
        inner = jnp.sum(weights * dweights, axis=0, keepdims=True)
        dscores = (weights * (dweights - inner)).astype(BF16)
        held_back[j, h] = (dscores, weights.astype(BF16))

    def gather_back(j, h):
        r = j - 1
        dscores, weights = held_back.pop((j, h))
        found = [key_sum(dscores, row_of(queries, j, h)), key_sum(weights, grad_of(j, h))]
        if j > 1:
            there = slice((r - 1) * WINDOW, r * WINDOW)
            for part, (before, _) in enumerate(found):
                total = unfinished[part, h] + before
                at = (part + 1) * D + h * HEAD_DIM
                dqkv[there, at : at + HEAD_DIM] = (total if part else total * SCALE).astype(BF16)
        for part, (_, current_part) in enumerate(found):
            unfinished[part, h] = current_part
        if j <= rows:
            dqkv[r * WINDOW : (r + 1) * WINDOW, columns[h]] = (
                window_sum(dscores, pair(keys, j, h), current_t) * SCALE
            ).astype(BF16)

    def project_back(i):
        at = i * step
        leave(3, i, dqkv.at[pl.ds(at, step)], dqkv_out.at[pl.ds(at, step)])
        made = dot(xhat_t[:, at : at + step], dqkv[at : at + step, :])
        acc_qkv[...] = (acc_qkv[...] + made) if at else made

    def units(first, last):
        return [(j, h) for j in range(first, last + 1) for h in range(HEADS)]

    project_rim(0)
    project_rim(rows + 1)
    for i in range(steps):
        project(i)
    forward = [(j, h) for j, h in units(1, rows + 1) if h or not 1 < j <= rows]
    do(staggered(forward, score, soften, gather))
    feeds = [feed_forward(i * CHUNK, CHUNK, True) for i in range(steps)]
    halo_enter, halo_hides, _, halo_back = feed_forward(rows, 1, False)
    halo = [halo_enter] + halo_hides + [halo_back]
    enter, hides, weighs, back = feeds[0]
    do([enter, halo.pop(0), hides[0], hides[1], weighs[0]])
    for i in range(steps):
        enter, hides, weighs, back = feeds[i]
        for f in range(2, len(hides)):
            do([hides[f], weighs[f - 1]] + halo[:1])
            halo = halo[1:]
        if i + 1 < steps:
            later = feeds[i + 1]
            do([later[0], weighs[-1], later[1][0], back, later[1][1], later[2][0]] + halo[:1])
            halo = halo[1:]
        else:
            do([weighs[-1]] + halo + [back])

    core = (place & 2) // 2
    wide = FF // 2
    halves = ((core, keep_ref), (1 - core, send_ref))
    after_down = D // HEAD_DIM * wide
    after_up = after_down + wide // HEAD_DIM * D

    def export_down(c, ref, f):
        at = pl.ds(pl.multiple_of(c * wide + f, D), D)
        block = (acc_down[:, at] * 0.5).astype(BF16).T
        for half in range(D // HEAD_DIM):
            ref[half * wide + f : half * wide + f + D, :] = block[
                :, half * HEAD_DIM : (half + 1) * HEAD_DIM
            ]

    def export_up(c, ref, n):
        at = pl.ds(pl.multiple_of(c * wide + n * HEAD_DIM, HEAD_DIM), HEAD_DIM)
        ref[after_down + n * D : after_down + (n + 1) * D, :] = acc_up[:, at].astype(BF16)

    def export_heads(c, ref, h, part):
        mine = pl.ds(pl.multiple_of(c * HEAD_DIM, HEAD_DIM), HEAD_DIM)
        true_head = head if h == 0 else 1 - head
        if part < 3:
            at = part * D + h * HEAD_DIM
            block = acc_qkv[mine, at : at + HEAD_DIM]
        else:
            block = acc_out[h * HEAD_DIM : (h + 1) * HEAD_DIM, mine]
        at = after_up + (true_head * 4 + part) * HEAD_DIM
        ref[pl.ds(pl.multiple_of(at, HEAD_DIM), HEAD_DIM), :] = block.astype(BF16)

    def export_vectors(c, ref):
        flat = vec_rows[pl.ds(pl.multiple_of(c * 16, 16), 16), :].astype(BF16)
        ref[after_up + 8 * HEAD_DIM :, :] = jnp.concatenate([flat] * (VECTOR_ROWS // 16))

    call = functools.partial
    exports = [call(export_down, c, ref, f) for c, ref in halves for f in range(0, wide, D)]
    exports += [call(export_up, c, ref, n) for c, ref in halves for n in range(wide // HEAD_DIM)]
    exports += [call(export_heads, c, ref, h, 3) for c, ref in halves for h in range(HEADS)]
    backs = staggered(units(1, rows + 1), weigh_grads, soften_back, gather_back)
    marks = []
    for i in range(steps):
        done = [n for n, job in enumerate(backs) if job.func is gather_back and job.args == ((i + 1) * CHUNK + 1, 1)]
        marks.append(done[0] + 1)
    do(merge(backs[: marks[0]], exports))
    for i in range(1, steps):
        project_back(i - 1)
        do(backs[marks[i - 1] : marks[i]])
    do(backs[marks[-1] :])
    project_back(steps - 1)

    gain_t = jnp.broadcast_to(gain1_ref[...], (HEAD_DIM, D)).T
    shift_t = jnp.broadcast_to(shift1_ref[...], (HEAD_DIM, D)).T
    gain_sum = jnp.zeros((D, HEAD_DIM), F32)
    shift_sum = jnp.zeros((D, HEAD_DIM), F32)
    for n in range(3 * D // HEAD_DIM):
        cols = slice(n * HEAD_DIM, (n + 1) * HEAD_DIM)
        product = acc_qkv[:D, cols]
        total = acc_qkv[D : D + 1, cols]
        weight = wqkv[:, cols].astype(F32)
        gain_sum += weight * product
        shift_sum += weight * total
        acc_qkv[:D, cols] = gain_t * product + shift_t * total
    acc_vec[0:1, :D] = column_sums(gain_sum.T)
    acc_vec[1:2, :D] = column_sums(shift_sum.T)
    acc_vec[4:5, :D] = column_sums(cot_sum[...])

    for c, ref in halves:
        do([call(export_heads, c, ref, h, part) for h in range(HEADS) for part in range(3)])
    for n, (row, cols) in enumerate(vector_slots(FF, D)):
        vec_rows[n : n + 1, :] = acc_vec[row : row + 1, cols]
    for c, ref in halves:
        export_vectors(c, ref)
    for (kind, n), copy in leaving.items():
        if kind not in (0, 2) or n >= steps - 2:
            copy.wait()


def layer(rim, made, tokens, up, gain1, shift1, weights, other, gain2, shift2, up_bias):
    own, D = tokens.shape
    FF = up.shape[1]
    rows = own // WINDOW
    count = own + 2 * WINDOW
    half = half_rows(FF, D)
    tokens, up, rim, other = in_vmem(tokens), in_vmem(up), in_vmem(rim), in_vmem(other)
    made = [in_vmem(array) for array in made]
    vmem = pl.BlockSpec(memory_space=pltpu.VMEM)
    return pl.pallas_call(
        functools.partial(layer_kernel, rows),
        out_shape=(
            pltpu.VMEM((half, HEAD_DIM), BF16),
            pltpu.VMEM((half, HEAD_DIM), BF16),
            pltpu.HBM((own, FF), BF16),
            pltpu.HBM((own, D), BF16),
            pltpu.HBM((own, D), F32),
            pltpu.HBM((own, 3 * D), BF16),
            pltpu.HBM((D, 3 * D), BF16),
            pltpu.HBM((D, D), BF16),
        ),
        in_specs=[vmem] * (1 + len(made) + 2 + 2 + 4 + 1 + 3),
        out_specs=(vmem, vmem) + (pl.BlockSpec(memory_space=pltpu.HBM),) * 6,
        scratch_shapes=[
            pltpu.VMEM((2, CHUNK * WINDOW, FF), BF16),
            pltpu.VMEM((own, D), BF16),
            pltpu.VMEM((2, CHUNK * WINDOW, D), F32),
            pltpu.VMEM((own, 3 * D), BF16),
            pltpu.VMEM((D, 3 * D), BF16),
            pltpu.VMEM((D, D), BF16),
            pltpu.VMEM((2 * WINDOW, D), BF16),
            pltpu.VMEM((WINDOW, D), BF16),
            pltpu.VMEM((WINDOW, FF), BF16),
            pltpu.VMEM((WINDOW, D), BF16),
            pltpu.VMEM((D, 3 * HEAD_DIM), BF16),
            pltpu.VMEM((2 * WINDOW, HEAD_DIM), BF16),
            pltpu.VMEM((2 * WINDOW, HEAD_DIM), BF16),
            pltpu.VMEM((2 * WINDOW, HEAD_DIM), BF16),
            pltpu.VMEM((count, HEAD_DIM), BF16),
            pltpu.VMEM((count, HEAD_DIM), BF16),
            pltpu.VMEM((count, HEAD_DIM), BF16),
            pltpu.VMEM((count, D), BF16),
            pltpu.VMEM((rows + 3, WINDOW, WINDOW), F32),
            pltpu.VMEM((2, CHUNK * WINDOW, FF), BF16),
            pltpu.VMEM((D, FF), F32),
            pltpu.VMEM((D, FF), F32),
            pltpu.VMEM((D + 16, 3 * D), F32),
            pltpu.VMEM((D, D), F32),
            pltpu.VMEM((16, FF), F32),
            pltpu.VMEM((32, HEAD_DIM), F32),
            pltpu.SemaphoreType.DMA((5, max(rows // CHUNK, 2))),
        ],
        compiler_params=pltpu.CompilerParams(vmem_limit_bytes=34 * 1024 * 1024),
        name="layer",
    )(rim, *made, tokens, up, gain1, shift1, *weights, other, gain2, shift2, up_bias)


def token_chunks(streams, out_ref, buf, in_sem, out_sem, fixed, work):
    step = CHUNK * WINDOW
    arriving = [pltpu.make_async_copy(a, b, in_sem.at[0, n]) for n, (a, b) in enumerate(fixed)]
    steps = buf.shape[0] // step
    chunks = []
    for i in range(steps):
        here = pl.ds(i * step, step)
        chunks.append(
            [pltpu.make_async_copy(a.at[here], b.at[here], in_sem.at[i + 1, n]) for n, (a, b) in enumerate(streams)]
        )
    for copy in arriving + [copy for chunk in chunks for copy in chunk]:
        copy.start()
    for copy in arriving:
        copy.wait()
    leaving = []
    for i in range(steps):
        for copy in chunks[i]:
            copy.wait()
        work(slice(i * step, (i + 1) * step))
        here = pl.ds(i * step, step)
        leaving.append(pltpu.make_async_copy(buf.at[here], out_ref.at[here], out_sem.at[i]))
        leaving[-1].start()
    for copy in leaving:
        copy.wait()


def input_grad_kernel(
    x_in, mid_in, dqkv_in, wqkv_in, gain1_ref, out_ref, buf, in_sem, out_sem, x_ref, mid_grad, dqkv, wqkv
):
    def work(here):
        scaled, inverse = standardize(x_ref[here, :].astype(F32))
        g1 = split_dot(dqkv[here, :], wqkv[...], dot_lanes)
        buf[here, :] = (
            mid_grad[here, :] + normalize_back(g1 * gain1_ref[...], scaled, inverse)
        ).astype(BF16)

    streams = ((x_in, x_ref), (mid_in, mid_grad), (dqkv_in, dqkv))
    token_chunks(streams, out_ref, buf, in_sem, out_sem, ((wqkv_in, wqkv),), work)


def mixed_kernel(
    x_in, att_in, act_in, wout_in, down_in, down_bias_ref, out_ref, buf, in_sem, out_sem, x_ref, att, act, wout, down
):
    def work(here):
        middle = x_ref[here, :].astype(F32) + split_dot(att[here, :], wout[...])
        mixed = middle + split_dot(act[here, :], down[...]) * 0.5 + down_bias_ref[...]
        buf[here, :] = mixed.astype(BF16)

    streams = ((x_in, x_ref), (att_in, att), (act_in, act))
    token_chunks(streams, out_ref, buf, in_sem, out_sem, ((wout_in, wout), (down_in, down)), work)


def late(kernel, name, arrays, small):
    own, D = arrays[0].shape
    steps = own // (CHUNK * WINDOW)
    hbm = pl.BlockSpec(memory_space=pltpu.HBM)
    return pl.pallas_call(
        kernel,
        out_shape=pltpu.HBM((own, D), BF16),
        in_specs=[hbm] * len(arrays) + [pl.BlockSpec(memory_space=pltpu.VMEM)],
        out_specs=hbm,
        scratch_shapes=[
            pltpu.VMEM((own, D), BF16),
            pltpu.SemaphoreType.DMA((steps + 1, 3)),
            pltpu.SemaphoreType.DMA((steps,)),
        ]
        + [pltpu.VMEM(array.shape, array.dtype) for array in arrays],
        compiler_params=pltpu.CompilerParams(vmem_limit_bytes=32 * 1024 * 1024),
        name=name,
    )(*[in_hbm(array) for array in arrays], small)


def pack_kernel(query_ref, key_ref, value_ref, out_ref, tok_ref, cot_ref, near_ref, far_ref, sem):
    D = query_ref.shape[0]
    own = tok_ref.shape[0]
    head = lax.axis_index("head")
    moves = [
        (ref, near_ref.at[pl.ds(part * D, D)]) for part, ref in enumerate((query_ref, key_ref, value_ref))
    ]
    last = own - WINDOW
    near_from = pl.multiple_of((1 - head) * last, WINDOW)
    far_from = pl.multiple_of(head * last, WINDOW)
    for half in range(D // HEAD_DIM):
        cols = pl.ds(half * HEAD_DIM, HEAD_DIM)
        moves.append((out_ref.at[:, cols], near_ref.at[pl.ds(3 * D + half * HEAD_DIM, HEAD_DIM)]))
        for k, ref in enumerate((tok_ref, cot_ref)):
            at = (half * 2 + k) * WINDOW
            moves.append((ref.at[pl.ds(near_from, WINDOW), cols], near_ref.at[pl.ds(4 * D + at, WINDOW)]))
            moves.append((ref.at[pl.ds(far_from, WINDOW), cols], far_ref.at[pl.ds(at, WINDOW)]))
    copies = [pltpu.make_async_copy(a, b, sem.at[n]) for n, (a, b) in enumerate(moves)]
    for copy in copies:
        copy.start()
    for copy in copies:
        copy.wait()


def pack(query_weight, key_weight, value_weight, out_weight, tokens, cotangent):
    D = query_weight.shape[0]
    rim = 2 * WINDOW * D // HEAD_DIM
    anywhere = pl.BlockSpec(memory_space=pl.ANY)
    vmem = pl.BlockSpec(memory_space=pltpu.VMEM)
    return pl.pallas_call(
        pack_kernel,
        out_shape=(pltpu.VMEM((4 * D + rim, HEAD_DIM), BF16), pltpu.VMEM((rim, HEAD_DIM), BF16)),
        in_specs=[anywhere] * 6,
        out_specs=(vmem, vmem),
        scratch_shapes=[pltpu.SemaphoreType.DMA((3 + 5 * (D // HEAD_DIM),))],
        name="pack",
    )(query_weight, key_weight, value_weight, out_weight, tokens, cotangent)


def finish_kernel(FF, D, mine_ref, other_ref, *refs):
    outs, (down_buf, up_buf, vec_rows, sem) = refs[:12], refs[12:]
    gain1, shift1, query, key, value, out, gain2, shift2, up, up_bias, down, down_bias = outs
    core = lax.axis_index("seq") % 2
    head = lax.axis_index("head")
    halves = ((core, mine_ref), (1 - core, other_ref))
    wide = FF // 2
    for c, ref in halves:
        rows = pl.ds(pl.multiple_of(c * wide, wide), wide)
        for half in range(D // HEAD_DIM):
            down_buf[rows, half * HEAD_DIM : (half + 1) * HEAD_DIM] = ref[
                half * wide : (half + 1) * wide, :
            ].astype(F32)
    copies = [pltpu.make_async_copy(down_buf, down, sem.at[0])]
    copies[0].start()
    start = D // HEAD_DIM * wide
    for c, ref in halves:
        for n, f in enumerate(range(0, wide, HEAD_DIM)):
            at = pl.ds(pl.multiple_of(c * wide + f, HEAD_DIM), HEAD_DIM)
            up_buf[:, at] = ref[start + n * D : start + (n + 1) * D, :].astype(F32)
    copies.append(pltpu.make_async_copy(up_buf, up, sem.at[1]))
    copies[1].start()
    start += wide // HEAD_DIM * D
    for c, ref in halves:
        mine = pl.ds(pl.multiple_of(c * HEAD_DIM, HEAD_DIM), HEAD_DIM)
        base = start + head * (4 * HEAD_DIM)
        for part, made in enumerate((query, key, value)):
            at = pl.multiple_of(base + part * HEAD_DIM, HEAD_DIM)
            made[mine, :] = ref[pl.ds(at, HEAD_DIM), :].astype(F32)
        at = pl.multiple_of(base + 3 * HEAD_DIM, HEAD_DIM)
        out[:, mine] = ref[pl.ds(at, HEAD_DIM), :].astype(F32)
        base = start + 8 * HEAD_DIM
        vec_rows[pl.ds(pl.multiple_of(c * 16, 16), 16), :] = ref[base : base + 16, :].astype(F32)
    vectors = (gain1, shift1, gain2, shift2, down_bias)
    for s, (n, cols) in enumerate(vector_slots(FF, D)):
        made = up_bias if n == 8 else vectors[n]
        made[cols] = vec_rows[s, :]
    for copy in copies:
        copy.wait()


def finish(mine, other, FF, D):
    vmem = pl.BlockSpec(memory_space=pltpu.VMEM)
    anywhere = pl.BlockSpec(memory_space=pl.ANY)
    shapes = [(D,), (D,)] + [(D, HEAD_DIM)] * 3 + [(HEAD_DIM, D), (D,), (D,), (D, FF), (FF,), (FF, D), (D,)]
    return pl.pallas_call(
        functools.partial(finish_kernel, FF, D),
        out_shape=tuple(jax.ShapeDtypeStruct(shape, F32) for shape in shapes),
        in_specs=[vmem, vmem],
        out_specs=tuple(anywhere if n in (8, 10) else vmem for n in range(len(shapes))),
        scratch_shapes=[
            pltpu.VMEM((FF, D), F32),
            pltpu.VMEM((D, FF), F32),
            pltpu.VMEM((32, HEAD_DIM), F32),
            pltpu.SemaphoreType.DMA((2,)),
        ],
        name="finish",
    )(in_vmem(mine), in_vmem(other))


def spans(masks):
    found = [0]
    for mask in masks:
        found = found + [f ^ mask for f in found]
    return found


def stages(count):
    bits = [1 << b for b in range(count.bit_length() - 1)]
    plane, rest = [bits[0], bits[2]], bits[3:]
    found = [plane] + [rest[i : i + 2] for i in range(0, len(rest), 2)]
    if len(found) > 1 and len(found[1]) == 2:
        return [(found[0], found[1]), (found[1], found[0])] + [(masks, masks) for masks in found[2:]]
    return [(masks, masks) for masks in found]


def partners(value, masks, k):
    count = lax.axis_size("seq") * lax.axis_size("head")
    hops = [spans(side)[k] for side in masks]
    return lax.ppermute(value, BOTH, [(i, i ^ hops[i // 2 % 2]) for i in range(count)])


def all_sum(value, side):
    count = lax.axis_size("seq") * lax.axis_size("head")
    place = lax.axis_index("seq") * lax.axis_size("head") + lax.axis_index("head")
    width = value.shape[1]
    made = []
    steps = []
    for masks in stages(count):
        code, other_code = (
            sum(((place & mask) // mask) << j for j, mask in enumerate(bits)) for bits in masks
        )
        steps.append((masks, jnp.where(place & 2 == 0, code, other_code)))

    def exchange(value, send, masks, number):
        if number >= len(side):
            return [partners(send(value, k), masks, k) for k in range(1, 1 << len(masks[0]))]
        work, small = side[number]
        value, small = lax.optimization_barrier((value, small))
        arrived = [partners(send(value, k), masks, k) for k in range(1, 1 << len(masks[0]))]
        arrived, done = lax.optimization_barrier((arrived, work(small)))
        made.append(done)
        return arrived

    def spread(value, masks, code, number):
        found = [value] + exchange(value, lambda v, k: v, masks, number)
        whole = jnp.zeros((len(found),) + value.shape, value.dtype)
        for k, part in enumerate(found):
            whole = lax.dynamic_update_index_in_dim(whole, part, code ^ k, 0)
        return whole

    for number, (masks, code) in enumerate(steps[:-1]):
        parts = value.reshape(1 << len(masks[0]), -1, width)
        total = lax.dynamic_index_in_dim(parts, code, 0, False).astype(F32)
        pick = lambda parts, k, code=code: lax.dynamic_index_in_dim(parts, code ^ k, 0, False)
        for part in exchange(parts, pick, masks, number):
            total = total + part.astype(F32)
        value = total.astype(BF16)
    whole = spread(value, *steps[-1], len(steps) - 1)
    total = whole[0].astype(F32)
    for part in whole[1:]:
        total = total + part.astype(F32)
    value = total.astype(BF16)
    for masks, code in steps[-2::-1]:
        value = spread(value, masks, code, len(side)).reshape(-1, width)
    return value, made


def across_cores(value):
    return partners(value, ([2], [2]), 1)


def shards(
    tokens,
    cotangent,
    image_rows,
    image_fill,
    first_gain,
    first_shift,
    query_weight,
    key_weight,
    value_weight,
    out_weight,
    second_gain,
    second_shift,
    up_weight,
    up_bias,
    down_weight,
    down_bias,
):
    own, D = tokens.shape
    FF = up_weight.shape[1]
    devices = lax.axis_size("seq") * lax.axis_size("head")
    near, far = pack(query_weight, key_weight, value_weight, out_weight, tokens, cotangent)
    other = lax.ppermute(near, "head", [(0, 1), (1, 0)])
    pairs = [(i, i + 1) for i in range(1, devices - 1, 2)]
    rim = lax.ppermute(far, BOTH, pairs + [(b, a) for a, b in pairs])
    weights = (query_weight, key_weight, value_weight, out_weight)
    gain1, shift1 = first_gain[None], first_shift[None]
    made = local(tokens, cotangent, down_weight, image_rows[None], image_fill[None], gain1, shift1, weights)
    keep, send, act, att, mid_grad, dqkv, wqkv, wout = layer(
        rim,
        made,
        tokens,
        up_weight,
        gain1,
        shift1,
        weights,
        other,
        second_gain[None],
        second_shift[None],
        up_bias[None],
    )
    side = [
        (lambda small: late(input_grad_kernel, "input_grad", (tokens, mid_grad, dqkv, wqkv), small), gain1),
        (lambda small: late(mixed_kernel, "mixed", (tokens, att, act, wout, down_weight), small), down_bias[None]),
    ]
    summed = (keep.astype(F32) + across_cores(send).astype(F32)).astype(BF16)
    mine, (input_grad, mixed) = all_sum(summed, side)
    return (mixed, input_grad, *finish(mine, across_cores(mine), FF, D))


def solution(mesh):
    stream = P(("seq", "head"), None)
    columns = P(None, "head")
    in_specs = (stream, stream) + (P(),) * 4 + (columns,) * 3 + (P("head", None),) + (P(),) * 6
    out_specs = (
        (stream, stream) + (P(),) * 2 + (columns,) * 3 + (P("head", None),) + (P(),) * 6
    )
    return jax.shard_map(shards, mesh=mesh, in_specs=in_specs, out_specs=out_specs, check_vma=False)
```

```python
import functools

import jax
import jax.numpy as jnp
from jax import lax
from jax.experimental import pallas as pl
from jax.experimental.pallas import tpu as pltpu
from jax.sharding import PartitionSpec as P

HEAD_DIM = 128
HEADS = 2
WINDOW = 96
BOTH = ("seq", "head")

EPSILON = 1e-05
MASKED = -1000000000.0
LOG2E = 1.4426950408889634
SCALE = HEAD_DIM ** (-0.5)

F32 = jnp.float32
BF16 = jnp.bfloat16
LANES = (((1,), (1,)), ((), ()))
ROWS = (((0,), (0,)), ((), ()))

CHUNK = 8
LAG = 4


def dot(a, b):
    return jnp.dot(a, b, preferred_element_type=F32)


def split_dot(a, b, how=None):
    how = how or dot
    half = a.shape[0] // 2
    if half % 16:
        return how(a, b)
    return jnp.concatenate([how(a[:half], b), how(a[half:], b)])


def dot_lanes(a, b):
    return lax.dot_general(a, b, LANES, preferred_element_type=F32)


def dot_rows(a, b):
    return lax.dot_general(a, b, ROWS, preferred_element_type=F32)


def standardize(inputs):
    center = inputs - jnp.mean(inputs, axis=1, keepdims=True)
    spread = jnp.mean(center * center, axis=1, keepdims=True)
    inverse = lax.rsqrt(spread + EPSILON)
    return center * inverse, inverse


def normalize_back(weighted, scaled, inverse):
    return inverse * (
        weighted
        - jnp.mean(weighted, axis=1, keepdims=True)
        - scaled * jnp.mean(weighted * scaled, axis=1, keepdims=True)
    )


def twice_gelu(x):
    z = x * 0.7071067811865476
    below = 1.0 + lax.erf(z)
    bell = jnp.exp2(z * z * -LOG2E)
    return x * below, below + x * bell * 0.7978845608028654


def column_sums(value):
    return jnp.sum(value, axis=0, keepdims=True)


def merge(*lists):
    marked = [
        ((n + 0.5) / len(work), k, n, job) for k, work in enumerate(lists) for n, job in enumerate(work)
    ]
    return [job for *_, job in sorted(marked, key=lambda item: item[:3])]


VECTOR_ROWS = 64


def half_rows(FF, D):
    return (2 * FF * D + 4 * D * D) // (2 * HEAD_DIM) + VECTOR_ROWS


def vector_slots(FF, D):
    found = [
        (n, slice(c, c + HEAD_DIM)) for n in range(5) for c in range(0, D, HEAD_DIM)
    ]
    return found + [(8, slice(c, c + HEAD_DIM)) for c in range(0, FF, HEAD_DIM)]


def masks():
    key_id = lax.broadcasted_iota(jnp.int32, (WINDOW, WINDOW), 0)
    query_id = lax.broadcasted_iota(jnp.int32, (WINDOW, WINDOW), 1)
    current = key_id <= query_id
    return current, key_id >= query_id, jnp.where(current, key_id, key_id - WINDOW)


def merged_scores(keys, query, current):
    raw = dot_lanes(keys, query)
    return jnp.where(current, raw[WINDOW:], raw[:WINDOW])


def soft_weights(scores, offset, low, fill):
    keep = (offset >= low) & (offset < fill)
    scores = jnp.where(keep, scores * (SCALE * LOG2E), MASKED * LOG2E)
    lifted = jnp.exp2(scores - jnp.max(scores, axis=0, keepdims=True))
    return lifted * (1.0 / jnp.sum(lifted, axis=0, keepdims=True))


def window_sum(weights, values, current_t):
    turned = weights.T
    zero = jnp.zeros_like(turned)
    return dot(jnp.where(current_t, zero, turned), values[:WINDOW]) + dot(
        jnp.where(current_t, turned, zero), values[WINDOW:]
    )


def staggered(units, *kinds):
    jobs = []
    for t in range(len(units) + LAG * (len(kinds) - 1)):
        for k, kind in enumerate(kinds):
            if 0 <= t - LAG * k < len(units):
                jobs.append(functools.partial(kind, *units[t - LAG * k]))
    return jobs


def do(jobs):
    for job in jobs:
        job()


def local_kernel(
    rows,
    x_ref,
    cot_in_ref,
    down_in_ref,
    image_rows_ref,
    image_fill_ref,
    gain1_ref,
    shift1_ref,
    query_ref,
    key_ref,
    value_ref,
    normed,
    qbuf,
    kbuf,
    vbuf,
    probs,
    att,
    low_mark,
    fill_mark,
    xhat_t,
    cot_t,
    cot_ref,
    down_ref,
    cot_sum,
    weight,
    in_sem,
):
    D = x_ref.shape[1]
    step = CHUNK * WINDOW
    xhat_t[D:, :] = jnp.ones((16, rows * WINDOW), BF16)
    place = lax.axis_index("seq") * lax.axis_size("head") + lax.axis_index("head")
    for part, ref in enumerate((query_ref, key_ref, value_ref)):
        weight[:, part * HEAD_DIM : (part + 1) * HEAD_DIM] = ref[...]
    later = [
        pltpu.make_async_copy(a, b, in_sem.at[n])
        for n, (a, b) in enumerate(((cot_in_ref, cot_ref), (down_in_ref, down_ref)))
    ]
    for copy in later:
        copy.start()

    images = image_rows_ref.shape[1]
    earlier = lax.broadcasted_iota(jnp.int32, (images, images), 0) <= lax.broadcasted_iota(
        jnp.int32, (images, images), 1
    )
    counts = jnp.broadcast_to(image_rows_ref[...], (8, images)).astype(F32)
    ends = dot(counts.astype(BF16), jnp.where(earlier, 1.0, 0.0).astype(BF16))[:1]
    starts = ends - counts[:1]
    mark_rows = low_mark.shape[0]
    row = (place * rows + lax.broadcasted_iota(jnp.int32, (mark_rows, 1), 0)).astype(F32)
    opens = jnp.sum(jnp.where(starts == row, 1.0, 0.0), axis=1, keepdims=True)
    opens = jnp.where(row >= ends[:, images - 1 :], 1.0, opens)
    missing = WINDOW - image_fill_ref[...].astype(F32)
    short = jnp.sum(jnp.where(ends == row + 1.0, missing, 0.0), axis=1, keepdims=True)
    low_mark[...] = jnp.broadcast_to(
        jnp.where(opens > 0.0, 0.0, -1.0 * WINDOW), low_mark.shape
    ).astype(jnp.int32)
    fill_mark[...] = jnp.broadcast_to(WINDOW - short, fill_mark.shape).astype(jnp.int32)

    for i in range(rows // CHUNK):
        here = slice(i * step, (i + 1) * step)
        scaled, _ = standardize(x_ref[here, :].astype(F32))
        xhat_t[:D, here] = scaled.astype(BF16).T
        value = (scaled * gain1_ref[...] + shift1_ref[...]).astype(BF16)
        normed[here, :] = value
        made = dot(value, weight[...]).astype(BF16)
        for part, buf in enumerate((qbuf, kbuf, vbuf)):
            buf[here, :] = made[:, part * HEAD_DIM : (part + 1) * HEAD_DIM]

    current, current_t, offset = masks()
    held = {}

    def score(r):
        held[r] = merged_scores(
            kbuf[(r - 1) * WINDOW : (r + 1) * WINDOW, :], qbuf[r * WINDOW : (r + 1) * WINDOW, :], current
        )

    def soften(r):
        weights = soft_weights(
            held[r], offset, low_mark[r : r + 1, :WINDOW], fill_mark[r : r + 1, :WINDOW]
        )
        probs[r] = weights
        held[r] = weights.astype(BF16)

    def gather(r):
        values = vbuf[(r - 1) * WINDOW : (r + 1) * WINDOW, :]
        att[r * WINDOW : (r + 1) * WINDOW, :] = window_sum(held.pop(r), values, current_t).astype(BF16)

    do(staggered([(r,) for r in range(1, rows)], score, soften, gather))
    for copy in later:
        copy.wait()
    cot_t[...] = cot_ref[...].T
    down_ref[...] = (down_ref[...].astype(F32) * 0.5).astype(BF16)
    total = jnp.zeros((8, D), F32)
    for i in range(rows // CHUNK):
        total += jnp.sum(cot_ref[i * step : (i + 1) * step, :].astype(F32).reshape(step // 8, 8, D), axis=0)
    cot_sum[...] = total


def in_vmem(array):
    return pltpu.with_memory_space_constraint(array, pltpu.VMEM)


def in_hbm(array):
    return pltpu.with_memory_space_constraint(array, pltpu.HBM)


def local(tokens, cotangent, down, image_rows, image_fill, gain1, shift1, weights):
    own, D = tokens.shape
    rows = own // WINDOW
    mark_rows = -(-(rows + 1) // 8) * 8
    vmem = pl.BlockSpec(memory_space=pltpu.VMEM)
    return pl.pallas_call(
        functools.partial(local_kernel, rows),
        out_shape=(
            pltpu.VMEM((own, D), BF16),
            pltpu.VMEM((own, HEAD_DIM), BF16),
            pltpu.VMEM((own, HEAD_DIM), BF16),
            pltpu.VMEM((own, HEAD_DIM), BF16),
            pltpu.VMEM((rows, WINDOW, WINDOW), F32),
            pltpu.VMEM((own, HEAD_DIM), BF16),
            pltpu.VMEM((mark_rows, 128), jnp.int32),
            pltpu.VMEM((mark_rows, 128), jnp.int32),
            pltpu.VMEM((D + 16, own), BF16),
            pltpu.VMEM((D, own), BF16),
            pltpu.VMEM((own, D), BF16),
            pltpu.VMEM(down.shape, BF16),
            pltpu.VMEM((8, D), F32),
        ),
        in_specs=[vmem] + [pl.BlockSpec(memory_space=pltpu.HBM)] * 2 + [vmem] * 7,
        out_specs=(vmem,) * 13,
        scratch_shapes=[
            pltpu.VMEM((D, 3 * HEAD_DIM), BF16),
            pltpu.SemaphoreType.DMA((2,)),
        ],
        compiler_params=pltpu.CompilerParams(vmem_limit_bytes=24 * 1024 * 1024),
        name="local",
    )(
        in_vmem(tokens), in_hbm(cotangent), in_hbm(down), image_rows, image_fill, gain1, shift1, *weights[:3]
    )


def layer_kernel(
    rows,
    near_rim,
    far_rim,
    normed,
    own_q,
    own_k,
    own_v,
    own_probs,
    own_att,
    low_mark,
    fill_mark,
    xhat_t,
    cot_t,
    cot_ref,
    down_ref,
    cot_sum,
    x_ref,
    up_ref,
    gain1_ref,
    shift1_ref,
    query_ref,
    key_ref,
    value_ref,
    out_ref,
    half_ref,
    other_half_ref,
    gain2_ref,
    shift2_ref,
    up_bias_ref,
    keep_ref,
    send_ref,
    act_out,
    att_out,
    mid_grad_out,
    dqkv_out,
    wqkv_out,
    wout_out,
    act,
    att,
    mid_grad,
    dqkv,
    wqkv,
    wout,
    rim_x,
    rim_cot,
    halo_grad,
    halo_att,
    wother,
    rim_q,
    rim_k,
    rim_v,
    qbuf,
    kbuf,
    vbuf,
    gbuf,
    probs,
    hid_grad,
    acc_down,
    acc_up,
    acc_qkv,
    acc_out,
    acc_vec,
    vec_rows,
    out_sem,
):
    D = x_ref.shape[1]
    FF = up_ref.shape[1]
    own = rows * WINDOW
    head = lax.axis_index("head")
    place = lax.axis_index("seq") * lax.axis_size("head") + head
    core = (place & 2) // 2
    step = CHUNK * WINDOW
    steps = rows // CHUNK
    leaving = {}

    def leave(kind, n, source, target):
        leaving[kind, n] = pltpu.make_async_copy(source, target, out_sem.at[kind, n])
        leaving[kind, n].start()

    def theirs(at, size):
        half, at = at // (2 * D), at % (2 * D)
        here, there = half_ref[at : at + size, :], other_half_ref[at : at + size, :]
        return jnp.where(core == half, here, there)

    for part, ref in enumerate((query_ref, key_ref, value_ref)):
        wqkv[:, part * D : part * D + HEAD_DIM] = ref[...]
        wqkv[:, part * D + HEAD_DIM : (part + 1) * D] = theirs(part * D, D)
        wother[:, part * HEAD_DIM : (part + 1) * HEAD_DIM] = theirs(part * D, D)
    wout[:HEAD_DIM, :] = out_ref[...]
    for half in range(D // HEAD_DIM):
        wout[HEAD_DIM:, half * HEAD_DIM : (half + 1) * HEAD_DIM] = theirs(
            3 * D + half * HEAD_DIM, HEAD_DIM
        )
    leave(4, 0, wqkv, wqkv_out)
    leave(4, 1, wout, wout_out)
    acc_vec[...] = jnp.zeros_like(acc_vec)

    for half in range(D // HEAD_DIM):
        cols = slice(half * HEAD_DIM, (half + 1) * HEAD_DIM)
        near = near_rim[half * 2 * WINDOW : (half + 1) * 2 * WINDOW, :]
        far = far_rim[half * 2 * WINDOW : (half + 1) * 2 * WINDOW, :]
        rim_x[:WINDOW, cols] = jnp.where(head == 0, far[:WINDOW], near[:WINDOW])
        rim_x[WINDOW:, cols] = jnp.where(head == 0, near[:WINDOW], far[:WINDOW])
        rim_cot[:, cols] = jnp.where(head == 0, near[WINDOW:], far[WINDOW:])

    att[WINDOW:, :HEAD_DIM] = own_att[WINDOW:, :]
    queries = (own_q, rim_q, qbuf)
    keys = (own_k, rim_k, kbuf)
    values = (own_v, rim_v, vbuf)

    def project_rim(j):
        here = slice(j * WINDOW, (j + 1) * WINDOW)
        there = slice(WINDOW, 2 * WINDOW) if j else slice(0, WINDOW)
        scaled, _ = standardize(rim_x[there, :].astype(F32))
        value = (scaled * gain1_ref[...] + shift1_ref[...]).astype(BF16)
        made = dot(value, wqkv[...]).astype(BF16)
        for part, (_, rim, other) in enumerate((queries, keys, values)):
            rim[there, :] = made[:, part * D : part * D + HEAD_DIM]
            other[here, :] = made[:, part * D + HEAD_DIM : (part + 1) * D]

    def project(i):
        here = slice(WINDOW + i * step, WINDOW + (i + 1) * step)
        made = dot(normed[i * step : (i + 1) * step, :], wother[...]).astype(BF16)
        for part, (_, _, other) in enumerate((queries, keys, values)):
            other[here, :] = made[:, part * HEAD_DIM : (part + 1) * HEAD_DIM]

    current, current_t, offset = masks()
    columns = [slice(h * HEAD_DIM, (h + 1) * HEAD_DIM) for h in range(HEADS)]
    held = {}

    def row_of(bufs, j, h):
        mine, rim, other = bufs
        if h:
            return other[j * WINDOW : (j + 1) * WINDOW, :]
        if 1 <= j <= rows:
            return mine[(j - 1) * WINDOW : j * WINDOW, :]
        return rim[WINDOW:, :] if j else rim[:WINDOW, :]

    def pair(bufs, j, h):
        if h:
            return bufs[2][(j - 1) * WINDOW : (j + 1) * WINDOW, :]
        if 1 < j <= rows:
            return bufs[0][(j - 2) * WINDOW : j * WINDOW, :]
        return jnp.concatenate([row_of(bufs, j - 1, 0), row_of(bufs, j, 0)])

    def grad_of(j, h):
        return gbuf[j * WINDOW : (j + 1) * WINDOW, columns[h]]

    def probs_of(j, h):
        if h:
            return probs.at[j - 1]
        return own_probs.at[j - 1] if 1 < j <= rows else probs.at[rows + 1 + (j > 1)]

    def key_sum(weights, queries):
        zero = jnp.zeros_like(weights)
        both = jnp.concatenate([jnp.where(current, zero, weights), jnp.where(current, weights, zero)])
        made = dot(both, queries)
        return made[:WINDOW], made[WINDOW:]

    def score(j, h):
        held[j, h] = merged_scores(pair(keys, j, h), row_of(queries, j, h), current)

    def soften(j, h):
        r = j - 1
        weights = soft_weights(
            held[j, h], offset, low_mark[r : r + 1, :WINDOW], fill_mark[r : r + 1, :WINDOW]
        )
        probs_of(j, h)[...] = weights
        held[j, h] = weights.astype(BF16)

    def gather(j, h):
        r = j - 1
        made = window_sum(held.pop((j, h)), pair(values, j, h), current_t).astype(BF16)
        if r < rows:
            att[r * WINDOW : (r + 1) * WINDOW, columns[h]] = made
        else:
            halo_att[:, columns[h]] = made

    def feed_forward(first, count, own_rows):
        at = first * WINDOW
        size = count * WINDOW
        here = slice(at, at + size)
        held = {}
        block = 256
        slot = at // step % 2
        grads = hid_grad.at[slot] if own_rows else halo_grad
        xs, cots, atts = (x_ref, cot_ref, att) if own_rows else (rim_x.at[pl.ds(WINDOW, WINDOW)], rim_cot, halo_att)
        there = here if own_rows else slice(0, size)

        def enter():
            if own_rows:
                if at >= 2 * step:
                    leaving[0, at // step - 2].wait()
                    leaving[2, at // step - 2].wait()
                leave(1, at // step, att.at[pl.ds(at, size)], att_out.at[pl.ds(at, size)])
            attended = atts[there, :]
            middle = xs[there, :].astype(F32) + split_dot(attended, wout[...])
            scaled, inverse = standardize(middle)
            held.update(scaled=scaled, inverse=inverse)
            held["normed"] = (scaled * gain2_ref[...] + shift2_ref[...]).astype(BF16)

        def hide(f):
            cols = slice(f * block, (f + 1) * block)
            hidden = dot(held["normed"], up_ref[:, cols]) + up_bias_ref[:, cols]
            active, slope = twice_gelu(hidden)
            grad = dot_lanes(cots[there, :], down_ref[cols, :]) * slope
            grads[:size, cols] = grad.astype(BF16)
            if own_rows:
                act[slot, :size, cols] = active.astype(BF16)
                acc_vec[8:9, cols] += column_sums(grad)

        def weigh(f):
            cols = slice(f * block, (f + 1) * block)
            down_part = dot(cot_t[:, here], act[slot, :size, cols])
            up_part = dot_rows(held["normed"], grads[:size, cols])
            if at:
                acc_down[:, cols] += down_part
                acc_up[:, cols] += up_part
            else:
                acc_down[:, cols] = down_part
                acc_up[:, cols] = up_part

        def back():
            if own_rows:
                leave(0, at // step, act.at[slot], act_out.at[pl.ds(at, size)])
            scaled = held["scaled"]
            g2 = split_dot(grads[:size, :], up_ref[...], dot_lanes)
            cot32 = cots[there, :].astype(F32)
            middle_grad = cot32 + normalize_back(g2 * gain2_ref[...], scaled, held["inverse"])
            mixing_grad = middle_grad.astype(BF16)
            if own_rows:
                mid_grad[slot, :, :] = middle_grad
                leave(2, at // step, mid_grad.at[slot], mid_grad_out.at[pl.ds(at, size)])
                acc_vec[2:3, :D] += column_sums(g2 * scaled)
                acc_vec[3:4, :D] += column_sums(g2)
                out_part = dot_rows(atts[there, :], mixing_grad)
                if at:
                    acc_out[...] += out_part
                else:
                    acc_out[...] = out_part
            made = split_dot(mixing_grad, wout[...], dot_lanes).astype(BF16)
            for g in range(count):
                j = first + 1 + g
                gbuf[j * WINDOW : (j + 1) * WINDOW, :] = made[g * WINDOW : (g + 1) * WINDOW]

        call = functools.partial
        parts = FF // block
        hides = [call(hide, f) for f in range(parts)]
        weighs = [call(weigh, f) for f in range(parts)] if own_rows else []
        return enter, hides, weighs, back

    held_back = {}
    unfinished = {}

    def weigh_grads(j, h):
        held_back[j, h] = merged_scores(pair(values, j, h), grad_of(j, h), current)

    def soften_back(j, h):
        dweights = held_back.pop((j, h))
        weights = probs_of(j, h)[...]
        inner = jnp.sum(weights * dweights, axis=0, keepdims=True)
        dscores = (weights * (dweights - inner)).astype(BF16)
        held_back[j, h] = (dscores, weights.astype(BF16))

    def gather_back(j, h):
        r = j - 1
        dscores, weights = held_back.pop((j, h))
        found = [key_sum(dscores, row_of(queries, j, h)), key_sum(weights, grad_of(j, h))]
        if j > 1:
            there = slice((r - 1) * WINDOW, r * WINDOW)
            for part, (before, _) in enumerate(found):
                total = unfinished[part, h] + before
                at = (part + 1) * D + h * HEAD_DIM
                dqkv[there, at : at + HEAD_DIM] = (total if part else total * SCALE).astype(BF16)
        for part, (_, current_part) in enumerate(found):
            unfinished[part, h] = current_part
        if j <= rows:
            dqkv[r * WINDOW : (r + 1) * WINDOW, columns[h]] = (
                window_sum(dscores, pair(keys, j, h), current_t) * SCALE
            ).astype(BF16)

    def project_back(i):
        at = i * step
        leave(3, i, dqkv.at[pl.ds(at, step)], dqkv_out.at[pl.ds(at, step)])
        made = dot(xhat_t[:, at : at + step], dqkv[at : at + step, :])
        acc_qkv[...] = (acc_qkv[...] + made) if at else made

    def units(first, last):
        return [(j, h) for j in range(first, last + 1) for h in range(HEADS)]

    project_rim(0)
    project_rim(rows + 1)
    for i in range(steps):
        project(i)
    forward = [(j, h) for j, h in units(1, rows + 1) if h or not 1 < j <= rows]
    do(staggered(forward, score, soften, gather))
    feeds = [feed_forward(i * CHUNK, CHUNK, True) for i in range(steps)]
    halo_enter, halo_hides, _, halo_back = feed_forward(rows, 1, False)
    halo = [halo_enter] + halo_hides + [halo_back]
    enter, hides, weighs, back = feeds[0]
    do([enter, halo.pop(0), hides[0], hides[1], weighs[0]])
    for i in range(steps):
        enter, hides, weighs, back = feeds[i]
        for f in range(2, len(hides)):
            do([hides[f], weighs[f - 1]] + halo[:1])
            halo = halo[1:]
        if i + 1 < steps:
            later = feeds[i + 1]
            do([later[0], weighs[-1], later[1][0], back, later[1][1], later[2][0]] + halo[:1])
            halo = halo[1:]
        else:
            do([weighs[-1]] + halo + [back])

    wide = FF // 2
    halves = ((core, keep_ref), (1 - core, send_ref))
    after_down = D // HEAD_DIM * wide
    after_up = after_down + wide // HEAD_DIM * D

    def export_down(c, ref, f):
        at = pl.ds(pl.multiple_of(c * wide + f, D), D)
        block = (acc_down[:, at] * 0.5).astype(BF16).T
        for half in range(D // HEAD_DIM):
            ref[half * wide + f : half * wide + f + D, :] = block[
                :, half * HEAD_DIM : (half + 1) * HEAD_DIM
            ]

    def export_up(c, ref, n):
        at = pl.ds(pl.multiple_of(c * wide + n * HEAD_DIM, HEAD_DIM), HEAD_DIM)
        ref[after_down + n * D : after_down + (n + 1) * D, :] = acc_up[:, at].astype(BF16)

    def export_heads(c, ref, h, part):
        mine = pl.ds(pl.multiple_of(c * HEAD_DIM, HEAD_DIM), HEAD_DIM)
        true_head = head if h == 0 else 1 - head
        if part < 3:
            at = part * D + h * HEAD_DIM
            block = acc_qkv[mine, at : at + HEAD_DIM]
        else:
            block = acc_out[h * HEAD_DIM : (h + 1) * HEAD_DIM, mine]
        at = after_up + (true_head * 4 + part) * HEAD_DIM
        ref[pl.ds(pl.multiple_of(at, HEAD_DIM), HEAD_DIM), :] = block.astype(BF16)

    def export_vectors(c, ref):
        flat = vec_rows[pl.ds(pl.multiple_of(c * 16, 16), 16), :].astype(BF16)
        ref[after_up + 8 * HEAD_DIM :, :] = jnp.concatenate([flat] * (VECTOR_ROWS // 16))

    call = functools.partial
    exports = [call(export_down, c, ref, f) for c, ref in halves for f in range(0, wide, D)]
    exports += [call(export_up, c, ref, n) for c, ref in halves for n in range(wide // HEAD_DIM)]
    exports += [call(export_heads, c, ref, h, 3) for c, ref in halves for h in range(HEADS)]
    backs = staggered(units(1, rows + 1), weigh_grads, soften_back, gather_back)
    marks = []
    for i in range(steps):
        done = [n for n, job in enumerate(backs) if job.func is gather_back and job.args == ((i + 1) * CHUNK + 1, 1)]
        marks.append(done[0] + 1)
    do(merge(backs[: marks[0]], exports))
    for i in range(1, steps):
        project_back(i - 1)
        do(backs[marks[i - 1] : marks[i]])
    do(backs[marks[-1] :])
    project_back(steps - 1)

    gain_t = jnp.broadcast_to(gain1_ref[...], (HEAD_DIM, D)).T
    shift_t = jnp.broadcast_to(shift1_ref[...], (HEAD_DIM, D)).T
    gain_sum = jnp.zeros((D, HEAD_DIM), F32)
    shift_sum = jnp.zeros((D, HEAD_DIM), F32)
    for n in range(3 * D // HEAD_DIM):
        cols = slice(n * HEAD_DIM, (n + 1) * HEAD_DIM)
        product = acc_qkv[:D, cols]
        total = acc_qkv[D : D + 1, cols]
        weight = wqkv[:, cols].astype(F32)
        gain_sum += weight * product
        shift_sum += weight * total
        acc_qkv[:D, cols] = gain_t * product + shift_t * total
    acc_vec[0:1, :D] = column_sums(gain_sum.T)
    acc_vec[1:2, :D] = column_sums(shift_sum.T)
    acc_vec[4:5, :D] = column_sums(cot_sum[...])

    for c, ref in halves:
        do([call(export_heads, c, ref, h, part) for h in range(HEADS) for part in range(3)])
    for n, (row, cols) in enumerate(vector_slots(FF, D)):
        vec_rows[n : n + 1, :] = acc_vec[row : row + 1, cols]
    for c, ref in halves:
        export_vectors(c, ref)
    for (kind, n), copy in leaving.items():
        if kind not in (0, 2) or n >= steps - 2:
            copy.wait()


def layer(rims, made, tokens, up, gain1, shift1, weights, others, gain2, shift2, up_bias):
    own, D = tokens.shape
    FF = up.shape[1]
    rows = own // WINDOW
    count = own + 2 * WINDOW
    half = half_rows(FF, D)
    tokens, up = in_vmem(tokens), in_vmem(up)
    rims, made, others = ([in_vmem(array) for array in arrays] for arrays in (rims, made, others))
    vmem = pl.BlockSpec(memory_space=pltpu.VMEM)
    return pl.pallas_call(
        functools.partial(layer_kernel, rows),
        out_shape=(
            pltpu.VMEM((half, HEAD_DIM), BF16),
            pltpu.VMEM((half, HEAD_DIM), BF16),
            pltpu.HBM((own, FF), BF16),
            pltpu.HBM((own, D), BF16),
            pltpu.HBM((own, D), F32),
            pltpu.HBM((own, 3 * D), BF16),
            pltpu.HBM((D, 3 * D), BF16),
            pltpu.HBM((D, D), BF16),
        ),
        in_specs=[vmem] * (2 + len(made) + 2 + 2 + 4 + 2 + 3),
        out_specs=(vmem, vmem) + (pl.BlockSpec(memory_space=pltpu.HBM),) * 6,
        scratch_shapes=[
            pltpu.VMEM((2, CHUNK * WINDOW, FF), BF16),
            pltpu.VMEM((own, D), BF16),
            pltpu.VMEM((2, CHUNK * WINDOW, D), F32),
            pltpu.VMEM((own, 3 * D), BF16),
            pltpu.VMEM((D, 3 * D), BF16),
            pltpu.VMEM((D, D), BF16),
            pltpu.VMEM((2 * WINDOW, D), BF16),
            pltpu.VMEM((WINDOW, D), BF16),
            pltpu.VMEM((WINDOW, FF), BF16),
            pltpu.VMEM((WINDOW, D), BF16),
            pltpu.VMEM((D, 3 * HEAD_DIM), BF16),
            pltpu.VMEM((2 * WINDOW, HEAD_DIM), BF16),
            pltpu.VMEM((2 * WINDOW, HEAD_DIM), BF16),
            pltpu.VMEM((2 * WINDOW, HEAD_DIM), BF16),
            pltpu.VMEM((count, HEAD_DIM), BF16),
            pltpu.VMEM((count, HEAD_DIM), BF16),
            pltpu.VMEM((count, HEAD_DIM), BF16),
            pltpu.VMEM((count, D), BF16),
            pltpu.VMEM((rows + 3, WINDOW, WINDOW), F32),
            pltpu.VMEM((2, CHUNK * WINDOW, FF), BF16),
            pltpu.VMEM((D, FF), F32),
            pltpu.VMEM((D, FF), F32),
            pltpu.VMEM((D + 16, 3 * D), F32),
            pltpu.VMEM((D, D), F32),
            pltpu.VMEM((16, FF), F32),
            pltpu.VMEM((32, HEAD_DIM), F32),
            pltpu.SemaphoreType.DMA((5, max(rows // CHUNK, 2))),
        ],
        compiler_params=pltpu.CompilerParams(vmem_limit_bytes=34 * 1024 * 1024),
        name="layer",
    )(*rims, *made, tokens, up, gain1, shift1, *weights, *others, gain2, shift2, up_bias)


def token_chunks(streams, out_ref, buf, in_sem, out_sem, fixed, work):
    step = CHUNK * WINDOW
    arriving = [pltpu.make_async_copy(a, b, in_sem.at[0, n]) for n, (a, b) in enumerate(fixed)]
    steps = buf.shape[0] // step
    chunks = []
    for i in range(steps):
        here = pl.ds(i * step, step)
        chunks.append(
            [pltpu.make_async_copy(a.at[here], b.at[here], in_sem.at[i + 1, n]) for n, (a, b) in enumerate(streams)]
        )
    for copy in arriving + [copy for chunk in chunks for copy in chunk]:
        copy.start()
    for copy in arriving:
        copy.wait()
    leaving = []
    for i in range(steps):
        for copy in chunks[i]:
            copy.wait()
        work(slice(i * step, (i + 1) * step))
        here = pl.ds(i * step, step)
        leaving.append(pltpu.make_async_copy(buf.at[here], out_ref.at[here], out_sem.at[i]))
        leaving[-1].start()
    for copy in leaving:
        copy.wait()


def input_grad_kernel(
    x_in, mid_in, dqkv_in, wqkv_in, gain1_ref, out_ref, buf, in_sem, out_sem, x_ref, mid_grad, dqkv, wqkv
):
    def work(here):
        scaled, inverse = standardize(x_ref[here, :].astype(F32))
        g1 = split_dot(dqkv[here, :], wqkv[...], dot_lanes)
        buf[here, :] = (
            mid_grad[here, :] + normalize_back(g1 * gain1_ref[...], scaled, inverse)
        ).astype(BF16)

    streams = ((x_in, x_ref), (mid_in, mid_grad), (dqkv_in, dqkv))
    token_chunks(streams, out_ref, buf, in_sem, out_sem, ((wqkv_in, wqkv),), work)


def mixed_kernel(
    x_in, att_in, act_in, wout_in, down_in, down_bias_ref, out_ref, buf, in_sem, out_sem, x_ref, att, act, wout, down
):
    def work(here):
        middle = x_ref[here, :].astype(F32) + split_dot(att[here, :], wout[...])
        mixed = middle + split_dot(act[here, :], down[...]) * 0.5 + down_bias_ref[...]
        buf[here, :] = mixed.astype(BF16)

    streams = ((x_in, x_ref), (att_in, att), (act_in, act))
    token_chunks(streams, out_ref, buf, in_sem, out_sem, ((wout_in, wout), (down_in, down)), work)


def late(kernel, name, arrays, small):
    own, D = arrays[0].shape
    steps = own // (CHUNK * WINDOW)
    hbm = pl.BlockSpec(memory_space=pltpu.HBM)
    return pl.pallas_call(
        kernel,
        out_shape=pltpu.HBM((own, D), BF16),
        in_specs=[hbm] * len(arrays) + [pl.BlockSpec(memory_space=pltpu.VMEM)],
        out_specs=hbm,
        scratch_shapes=[
            pltpu.VMEM((own, D), BF16),
            pltpu.SemaphoreType.DMA((steps + 1, 3)),
            pltpu.SemaphoreType.DMA((steps,)),
        ]
        + [pltpu.VMEM(array.shape, array.dtype) for array in arrays],
        compiler_params=pltpu.CompilerParams(vmem_limit_bytes=32 * 1024 * 1024),
        name=name,
    )(*[in_hbm(array) for array in arrays], small)


def pack_kernel(query_ref, key_ref, value_ref, out_ref, tok_ref, cot_ref, half_ref, near_ref, far_ref, sem):
    D = query_ref.shape[0]
    own = tok_ref.shape[0]
    head = lax.axis_index("head")
    core = lax.axis_index("seq") % 2
    last = own - WINDOW
    near_from = pl.multiple_of((1 - head) * last, WINDOW)
    far_from = pl.multiple_of(head * last, WINDOW)
    moves = []
    for half in range(D // HEAD_DIM):
        cols = pl.ds(half * HEAD_DIM, HEAD_DIM)
        for k, ref in enumerate((tok_ref, cot_ref)):
            at = (half * 2 + k) * WINDOW
            moves.append((ref.at[pl.ds(near_from, WINDOW), cols], near_ref.at[pl.ds(at, WINDOW)]))
            moves.append((ref.at[pl.ds(far_from, WINDOW), cols], far_ref.at[pl.ds(at, WINDOW)]))
    copies = [pltpu.make_async_copy(a, b, sem.at[n]) for n, (a, b) in enumerate(moves)]
    for copy in copies:
        copy.start()

    def weights(moves):
        sent = [pltpu.make_async_copy(a, b, sem.at[len(copies) + n]) for n, (a, b) in enumerate(moves)]
        for copy in sent:
            copy.start()
        for copy in sent:
            copy.wait()

    @pl.when(core == 0)
    def _():
        weights([(query_ref, half_ref.at[pl.ds(0, D)]), (key_ref, half_ref.at[pl.ds(D, D)])])

    @pl.when(core == 1)
    def _():
        outs = [
            (
                out_ref.at[:, pl.ds(half * HEAD_DIM, HEAD_DIM)],
                half_ref.at[pl.ds(D + half * HEAD_DIM, HEAD_DIM)],
            )
            for half in range(D // HEAD_DIM)
        ]
        weights([(value_ref, half_ref.at[pl.ds(0, D)])] + outs)

    for copy in copies:
        copy.wait()


def pack(query_weight, key_weight, value_weight, out_weight, tokens, cotangent):
    D = query_weight.shape[0]
    rim = 2 * WINDOW * D // HEAD_DIM
    vmem = pl.BlockSpec(memory_space=pltpu.VMEM)
    return pl.pallas_call(
        pack_kernel,
        out_shape=(
            pltpu.VMEM((2 * D, HEAD_DIM), BF16),
            pltpu.VMEM((rim, HEAD_DIM), BF16),
            pltpu.VMEM((rim, HEAD_DIM), BF16),
        ),
        in_specs=[pl.BlockSpec(memory_space=pl.ANY)] * 6,
        out_specs=(vmem, vmem, vmem),
        scratch_shapes=[pltpu.SemaphoreType.DMA((6 * (D // HEAD_DIM) + 1,))],
        name="pack",
    )(query_weight, key_weight, value_weight, out_weight, tokens, cotangent)


def finish_kernel(FF, D, second, mine_ref, *refs):
    if second:
        vectors, refs = (refs[0], refs[7:13]), refs[13:]
    outs, (down_buf, up_buf, heads_buf, vec_rows, sem) = refs[:6], refs[6:]
    query, key, value, out, up, down = outs
    core = lax.axis_index("seq") % 2
    head = lax.axis_index("head")
    c = 1 - core if second else core
    wide = FF // 2
    copies = []

    def leave(source, target):
        copies.append(pltpu.make_async_copy(source, target, sem.at[len(copies)]))
        copies[-1].start()

    for half in range(D // HEAD_DIM):
        down_buf[:, half * HEAD_DIM : (half + 1) * HEAD_DIM] = mine_ref[
            half * wide : (half + 1) * wide, :
        ].astype(F32)
    leave(down_buf, down.at[pl.ds(pl.multiple_of(c * wide, wide), wide)])
    start = D // HEAD_DIM * wide
    for n, f in enumerate(range(0, wide, HEAD_DIM)):
        up_buf[:, f : f + HEAD_DIM] = mine_ref[start + n * D : start + (n + 1) * D, :].astype(F32)
    leave(up_buf, up.at[:, pl.ds(pl.multiple_of(c * wide, wide), wide)])
    start += wide // HEAD_DIM * D
    own = pl.ds(pl.multiple_of(c * HEAD_DIM, HEAD_DIM), HEAD_DIM)
    for part, made in enumerate((query, key, value, out)):
        at = pl.multiple_of(start + (head * 4 + part) * HEAD_DIM, HEAD_DIM)
        heads_buf[part] = mine_ref[pl.ds(at, HEAD_DIM), :].astype(F32)
        leave(heads_buf.at[part], made.at[:, own] if part == 3 else made.at[own])
    if second:
        other_ref, made = vectors
        at = start + 8 * HEAD_DIM
        for k, ref in ((c, mine_ref), (core, other_ref)):
            vec_rows[pl.ds(pl.multiple_of(k * 16, 16), 16), :] = ref[at : at + 16, :].astype(F32)
        for s, (n, cols) in enumerate(vector_slots(FF, D)):
            made[5 if n == 8 else n][cols] = vec_rows[s, :]
    for copy in copies:
        copy.wait()


def finish(mine, FF, D, first=None):
    vmem = pl.BlockSpec(memory_space=pltpu.VMEM)
    hbm = pl.BlockSpec(memory_space=pltpu.HBM)
    arrays = [(D, HEAD_DIM)] * 3 + [(HEAD_DIM, D), (D, FF), (FF, D)]
    vectors = [(D,)] * 5 + [(FF,)] if first else []
    wide = FF // 2
    given = (in_vmem(first[0]), *[in_hbm(array) for array in first[1]]) if first else ()
    return pl.pallas_call(
        functools.partial(finish_kernel, FF, D, bool(first)),
        out_shape=tuple(jax.ShapeDtypeStruct(shape, F32) for shape in vectors)
        + tuple(pltpu.HBM(shape, F32) for shape in arrays),
        in_specs=[vmem] + ([vmem] + [hbm] * 6 if first else []),
        out_specs=(vmem,) * len(vectors) + (hbm,) * 6,
        input_output_aliases={2 + n: 6 + n for n in range(6)} if first else {},
        scratch_shapes=[
            pltpu.VMEM((wide, D), F32),
            pltpu.VMEM((D, wide), F32),
            pltpu.VMEM((4, HEAD_DIM, HEAD_DIM), F32),
            pltpu.VMEM((32, HEAD_DIM), F32),
            pltpu.SemaphoreType.DMA((6,)),
        ],
        name="finish_rest" if first else "finish",
    )(in_vmem(mine), *given)


def spans(masks):
    found = [0]
    for mask in masks:
        found = found + [f ^ mask for f in found]
    return found


def stages(count):
    bits = [1 << b for b in range(count.bit_length() - 1)]
    plane, rest = [bits[0], bits[2]], bits[3:]
    found = [plane] + [rest[i : i + 2] for i in range(0, len(rest), 2)]
    if len(found) > 1 and len(found[1]) == 2:
        return [(found[0], found[1]), (found[1], found[0])] + [(masks, masks) for masks in found[2:]]
    return [(masks, masks) for masks in found]


def partners(value, masks, k):
    count = lax.axis_size("seq") * lax.axis_size("head")
    hops = [spans(side)[k] for side in masks]
    return lax.ppermute(value, BOTH, [(i, i ^ hops[i // 2 % 2]) for i in range(count)])


def all_sum(value, side):
    count = lax.axis_size("seq") * lax.axis_size("head")
    place = lax.axis_index("seq") * lax.axis_size("head") + lax.axis_index("head")
    width = value.shape[1]
    made = []
    steps = []
    for masks in stages(count):
        code, other_code = (
            sum(((place & mask) // mask) << j for j, mask in enumerate(bits)) for bits in masks
        )
        steps.append((masks, jnp.where(place & 2 == 0, code, other_code)))

    def exchange(value, send, masks, number):
        if number >= len(side):
            return [partners(send(value, k), masks, k) for k in range(1, 1 << len(masks[0]))]
        work, small = side[number]
        value, small = lax.optimization_barrier((value, small))
        arrived = [partners(send(value, k), masks, k) for k in range(1, 1 << len(masks[0]))]
        arrived, done = lax.optimization_barrier((arrived, work(small)))
        made.append(done)
        return arrived

    def spread(value, masks, code, number):
        found = [value] + exchange(value, lambda v, k: v, masks, number)
        whole = jnp.zeros((len(found),) + value.shape, value.dtype)
        for k, part in enumerate(found):
            whole = lax.dynamic_update_index_in_dim(whole, part, code ^ k, 0)
        return whole

    for number, (masks, code) in enumerate(steps[:-1]):
        parts = value.reshape(1 << len(masks[0]), -1, width)
        total = lax.dynamic_index_in_dim(parts, code, 0, False).astype(F32)
        pick = lambda parts, k, code=code: lax.dynamic_index_in_dim(parts, code ^ k, 0, False)
        for part in exchange(parts, pick, masks, number):
            total = total + part.astype(F32)
        value = total.astype(BF16)
    whole = spread(value, *steps[-1], len(steps) - 1)
    total = whole[0].astype(F32)
    for part in whole[1:]:
        total = total + part.astype(F32)
    value = total.astype(BF16)
    for masks, code in steps[-2::-1]:
        value = spread(value, masks, code, len(side)).reshape(-1, width)
    return value, made


def across_cores(value):
    return partners(value, ([2], [2]), 1)


def shards(
    tokens,
    cotangent,
    image_rows,
    image_fill,
    first_gain,
    first_shift,
    query_weight,
    key_weight,
    value_weight,
    out_weight,
    second_gain,
    second_shift,
    up_weight,
    up_bias,
    down_weight,
    down_bias,
):
    own, D = tokens.shape
    FF = up_weight.shape[1]
    devices = lax.axis_size("seq") * lax.axis_size("head")
    half, near, far = pack(query_weight, key_weight, value_weight, out_weight, tokens, cotangent)
    half = lax.ppermute(half, "head", [(0, 1), (1, 0)])
    pairs = [(i, i + 1) for i in range(1, devices - 1, 2)]
    far = lax.ppermute(far, BOTH, pairs + [(b, a) for a, b in pairs])
    near = lax.ppermute(near, "head", [(0, 1), (1, 0)])
    weights = (query_weight, key_weight, value_weight, out_weight)
    gain1, shift1 = first_gain[None], first_shift[None]
    made = local(tokens, cotangent, down_weight, image_rows[None], image_fill[None], gain1, shift1, weights)
    half, near, far, mark = lax.optimization_barrier((half, near, far, made[6]))
    made = (*made[:6], mark, *made[7:])
    keep, send, act, att, mid_grad, dqkv, wqkv, wout = layer(
        (near, far),
        made,
        tokens,
        up_weight,
        gain1,
        shift1,
        weights,
        (half, across_cores(half)),
        second_gain[None],
        second_shift[None],
        up_bias[None],
    )
    side = [
        (lambda small: late(input_grad_kernel, "input_grad", (tokens, mid_grad, dqkv, wqkv), small), gain1),
        (lambda small: late(mixed_kernel, "mixed", (tokens, att, act, wout, down_weight), small), down_bias[None]),
    ]
    summed = (keep.astype(F32) + across_cores(send).astype(F32)).astype(BF16)
    mine, (input_grad, mixed) = all_sum(summed, side)
    arrays = finish(mine, FF, D)
    gain1_grad, shift1_grad, gain2_grad, shift2_grad, down_bias_grad, up_bias_grad, *arrays = finish(
        across_cores(mine), FF, D, (mine, arrays)
    )
    query_grad, key_grad, value_grad, out_grad, up_grad, down_grad = arrays
    return (
        mixed,
        input_grad,
        gain1_grad,
        shift1_grad,
        query_grad,
        key_grad,
        value_grad,
        out_grad,
        gain2_grad,
        shift2_grad,
        up_grad,
        up_bias_grad,
        down_grad,
        down_bias_grad,
    )


def solution(mesh):
    stream = P(("seq", "head"), None)
    columns = P(None, "head")
    in_specs = (stream, stream) + (P(),) * 4 + (columns,) * 3 + (P("head", None),) + (P(),) * 6
    out_specs = (
        (stream, stream) + (P(),) * 2 + (columns,) * 3 + (P("head", None),) + (P(),) * 6
    )
    return jax.shard_map(shards, mesh=mesh, in_specs=in_specs, out_specs=out_specs, check_vma=False)
```

```python
import functools

import jax
import jax.numpy as jnp
from jax import lax
from jax.experimental import pallas as pl
from jax.experimental.pallas import tpu as pltpu
from jax.sharding import PartitionSpec as P

HEAD_DIM = 128
HEADS = 2
WINDOW = 96
BOTH = ("seq", "head")

EPSILON = 1e-05
MASKED = -1000000000.0
LOG2E = 1.4426950408889634
SCALE = HEAD_DIM ** (-0.5)

F32 = jnp.float32
BF16 = jnp.bfloat16
LANES = (((1,), (1,)), ((), ()))
ROWS = (((0,), (0,)), ((), ()))

CHUNK = 8
LAG = 4


def dot(a, b):
    return jnp.dot(a, b, preferred_element_type=F32)


def split_dot(a, b, how=None):
    how = how or dot
    half = a.shape[0] // 2
    if half % 16:
        return how(a, b)
    return jnp.concatenate([how(a[:half], b), how(a[half:], b)])


def dot_lanes(a, b):
    return lax.dot_general(a, b, LANES, preferred_element_type=F32)


def dot_rows(a, b):
    return lax.dot_general(a, b, ROWS, preferred_element_type=F32)


def standardize(inputs):
    center = inputs - jnp.mean(inputs, axis=1, keepdims=True)
    spread = jnp.mean(center * center, axis=1, keepdims=True)
    inverse = lax.rsqrt(spread + EPSILON)
    return center * inverse, inverse


def normalize_back(weighted, scaled, inverse):
    return inverse * (
        weighted
        - jnp.mean(weighted, axis=1, keepdims=True)
        - scaled * jnp.mean(weighted * scaled, axis=1, keepdims=True)
    )


def twice_gelu(x):
    z = x * 0.7071067811865476
    below = 1.0 + lax.erf(z)
    bell = jnp.exp2(z * z * -LOG2E)
    return x * below, below + x * bell * 0.7978845608028654


def column_sums(value):
    return jnp.sum(value, axis=0, keepdims=True)


def merge(*lists):
    marked = [
        ((n + 0.5) / len(work), k, n, job) for k, work in enumerate(lists) for n, job in enumerate(work)
    ]
    return [job for *_, job in sorted(marked, key=lambda item: item[:3])]


VECTOR_ROWS = 16


def piece_rows(FF, D):
    return 2 * FF * D // (8 * HEAD_DIM) + VECTOR_ROWS, 4 * D * D // (8 * HEAD_DIM)


def half_rows(FF, D):
    return 4 * sum(piece_rows(FF, D))


def vector_slots(FF, D):
    found = [
        (n, slice(c, c + HEAD_DIM)) for n in range(5) for c in range(0, D, HEAD_DIM)
    ]
    return found + [(8, slice(c, c + HEAD_DIM)) for c in range(0, FF, HEAD_DIM)]


def masks():
    key_id = lax.broadcasted_iota(jnp.int32, (WINDOW, WINDOW), 0)
    query_id = lax.broadcasted_iota(jnp.int32, (WINDOW, WINDOW), 1)
    current = key_id <= query_id
    return current, key_id >= query_id, jnp.where(current, key_id, key_id - WINDOW)


def merged_scores(keys, query, current):
    raw = dot_lanes(keys, query)
    return jnp.where(current, raw[WINDOW:], raw[:WINDOW])


def soft_weights(scores, offset, low, fill):
    keep = (offset >= low) & (offset < fill)
    scores = jnp.where(keep, scores * (SCALE * LOG2E), MASKED * LOG2E)
    lifted = jnp.exp2(scores - jnp.max(scores, axis=0, keepdims=True))
    return lifted * (1.0 / jnp.sum(lifted, axis=0, keepdims=True))


def window_sum(weights, values, current_t):
    turned = weights.T
    zero = jnp.zeros_like(turned)
    return dot(jnp.where(current_t, zero, turned), values[:WINDOW]) + dot(
        jnp.where(current_t, turned, zero), values[WINDOW:]
    )


def staggered(units, *kinds):
    jobs = []
    for t in range(len(units) + LAG * (len(kinds) - 1)):
        for k, kind in enumerate(kinds):
            if 0 <= t - LAG * k < len(units):
                jobs.append(functools.partial(kind, *units[t - LAG * k]))
    return jobs


def do(jobs):
    for job in jobs:
        job()


def local_kernel(
    rows,
    x_ref,
    cot_in_ref,
    down_in_ref,
    image_rows_ref,
    image_fill_ref,
    gain1_ref,
    shift1_ref,
    query_ref,
    key_ref,
    value_ref,
    normed,
    qbuf,
    kbuf,
    vbuf,
    probs,
    att,
    low_mark,
    fill_mark,
    xhat_t,
    cot_t,
    cot_ref,
    down_ref,
    cot_sum,
    weight,
    in_sem,
):
    D = x_ref.shape[1]
    step = CHUNK * WINDOW
    xhat_t[D:, :] = jnp.ones((16, rows * WINDOW), BF16)
    place = lax.axis_index("seq") * lax.axis_size("head") + lax.axis_index("head")
    for part, ref in enumerate((query_ref, key_ref, value_ref)):
        weight[:, part * HEAD_DIM : (part + 1) * HEAD_DIM] = ref[...]
    later = [
        pltpu.make_async_copy(a, b, in_sem.at[n])
        for n, (a, b) in enumerate(((cot_in_ref, cot_ref), (down_in_ref, down_ref)))
    ]
    for copy in later:
        copy.start()

    images = image_rows_ref.shape[1]
    earlier = lax.broadcasted_iota(jnp.int32, (images, images), 0) <= lax.broadcasted_iota(
        jnp.int32, (images, images), 1
    )
    counts = jnp.broadcast_to(image_rows_ref[...], (8, images)).astype(F32)
    ends = dot(counts.astype(BF16), jnp.where(earlier, 1.0, 0.0).astype(BF16))[:1]
    starts = ends - counts[:1]
    mark_rows = low_mark.shape[0]
    row = (place * rows + lax.broadcasted_iota(jnp.int32, (mark_rows, 1), 0)).astype(F32)
    opens = jnp.sum(jnp.where(starts == row, 1.0, 0.0), axis=1, keepdims=True)
    opens = jnp.where(row >= ends[:, images - 1 :], 1.0, opens)
    missing = WINDOW - image_fill_ref[...].astype(F32)
    short = jnp.sum(jnp.where(ends == row + 1.0, missing, 0.0), axis=1, keepdims=True)
    low_mark[...] = jnp.broadcast_to(
        jnp.where(opens > 0.0, 0.0, -1.0 * WINDOW), low_mark.shape
    ).astype(jnp.int32)
    fill_mark[...] = jnp.broadcast_to(WINDOW - short, fill_mark.shape).astype(jnp.int32)

    for i in range(rows // CHUNK):
        here = slice(i * step, (i + 1) * step)
        scaled, _ = standardize(x_ref[here, :].astype(F32))
        xhat_t[:D, here] = scaled.astype(BF16).T
        value = (scaled * gain1_ref[...] + shift1_ref[...]).astype(BF16)
        normed[here, :] = value
        made = dot(value, weight[...]).astype(BF16)
        for part, buf in enumerate((qbuf, kbuf, vbuf)):
            buf[here, :] = made[:, part * HEAD_DIM : (part + 1) * HEAD_DIM]

    current, current_t, offset = masks()
    held = {}

    def score(r):
        held[r] = merged_scores(
            kbuf[(r - 1) * WINDOW : (r + 1) * WINDOW, :], qbuf[r * WINDOW : (r + 1) * WINDOW, :], current
        )

    def soften(r):
        weights = soft_weights(
            held[r], offset, low_mark[r : r + 1, :WINDOW], fill_mark[r : r + 1, :WINDOW]
        )
        probs[r] = weights
        held[r] = weights.astype(BF16)

    def gather(r):
        values = vbuf[(r - 1) * WINDOW : (r + 1) * WINDOW, :]
        att[r * WINDOW : (r + 1) * WINDOW, :] = window_sum(held.pop(r), values, current_t).astype(BF16)

    do(staggered([(r,) for r in range(1, rows)], score, soften, gather))
    for copy in later:
        copy.wait()
    cot_t[...] = cot_ref[...].T
    down_ref[...] = (down_ref[...].astype(F32) * 0.5).astype(BF16)
    total = jnp.zeros((8, D), F32)
    for i in range(rows // CHUNK):
        total += jnp.sum(cot_ref[i * step : (i + 1) * step, :].astype(F32).reshape(step // 8, 8, D), axis=0)
    cot_sum[...] = total


def in_vmem(array):
    return pltpu.with_memory_space_constraint(array, pltpu.VMEM)


def in_hbm(array):
    return pltpu.with_memory_space_constraint(array, pltpu.HBM)


def local(tokens, cotangent, down, image_rows, image_fill, gain1, shift1, weights):
    own, D = tokens.shape
    rows = own // WINDOW
    mark_rows = -(-(rows + 1) // 8) * 8
    vmem = pl.BlockSpec(memory_space=pltpu.VMEM)
    return pl.pallas_call(
        functools.partial(local_kernel, rows),
        out_shape=(
            pltpu.VMEM((own, D), BF16),
            pltpu.VMEM((own, HEAD_DIM), BF16),
            pltpu.VMEM((own, HEAD_DIM), BF16),
            pltpu.VMEM((own, HEAD_DIM), BF16),
            pltpu.VMEM((rows, WINDOW, WINDOW), F32),
            pltpu.VMEM((own, HEAD_DIM), BF16),
            pltpu.VMEM((mark_rows, 128), jnp.int32),
            pltpu.VMEM((mark_rows, 128), jnp.int32),
            pltpu.VMEM((D + 16, own), BF16),
            pltpu.VMEM((D, own), BF16),
            pltpu.VMEM((own, D), BF16),
            pltpu.VMEM(down.shape, BF16),
            pltpu.VMEM((8, D), F32),
        ),
        in_specs=[vmem] + [pl.BlockSpec(memory_space=pltpu.HBM)] * 2 + [vmem] * 7,
        out_specs=(vmem,) * 13,
        scratch_shapes=[
            pltpu.VMEM((D, 3 * HEAD_DIM), BF16),
            pltpu.SemaphoreType.DMA((2,)),
        ],
        compiler_params=pltpu.CompilerParams(vmem_limit_bytes=24 * 1024 * 1024),
        name="local",
    )(
        in_vmem(tokens), in_hbm(cotangent), in_hbm(down), image_rows, image_fill, gain1, shift1, *weights[:3]
    )


def layer_kernel(
    rows,
    near_rim,
    far_rim,
    normed,
    own_q,
    own_k,
    own_v,
    own_probs,
    own_att,
    low_mark,
    fill_mark,
    xhat_t,
    cot_t,
    cot_ref,
    down_ref,
    cot_sum,
    x_ref,
    up_ref,
    gain1_ref,
    shift1_ref,
    query_ref,
    key_ref,
    value_ref,
    out_ref,
    half_ref,
    other_half_ref,
    gain2_ref,
    shift2_ref,
    up_bias_ref,
    keep_ref,
    send_ref,
    act_out,
    att_out,
    mid_grad_out,
    dqkv_out,
    wqkv_out,
    wout_out,
    act,
    att,
    mid_grad,
    dqkv,
    wqkv,
    wout,
    rim_x,
    rim_cot,
    halo_grad,
    halo_att,
    wother,
    rim_q,
    rim_k,
    rim_v,
    qbuf,
    kbuf,
    vbuf,
    gbuf,
    probs,
    hid_grad,
    acc_down,
    acc_up,
    acc_qkv,
    acc_out,
    acc_vec,
    vec_rows,
    out_sem,
):
    D = x_ref.shape[1]
    FF = up_ref.shape[1]
    own = rows * WINDOW
    head = lax.axis_index("head")
    place = lax.axis_index("seq") * lax.axis_size("head") + head
    core = (place & 2) // 2
    step = CHUNK * WINDOW
    steps = rows // CHUNK
    leaving = {}

    def leave(kind, n, source, target):
        leaving[kind, n] = pltpu.make_async_copy(source, target, out_sem.at[kind, n])
        leaving[kind, n].start()

    def theirs(at, size):
        half, at = at // (2 * D), at % (2 * D)
        here, there = half_ref[at : at + size, :], other_half_ref[at : at + size, :]
        return jnp.where(core == half, here, there)

    for part, ref in enumerate((query_ref, key_ref, value_ref)):
        wqkv[:, part * D : part * D + HEAD_DIM] = ref[...]
        wqkv[:, part * D + HEAD_DIM : (part + 1) * D] = theirs(part * D, D)
        wother[:, part * HEAD_DIM : (part + 1) * HEAD_DIM] = theirs(part * D, D)
    wout[:HEAD_DIM, :] = out_ref[...]
    for half in range(D // HEAD_DIM):
        wout[HEAD_DIM:, half * HEAD_DIM : (half + 1) * HEAD_DIM] = theirs(
            3 * D + half * HEAD_DIM, HEAD_DIM
        )
    leave(4, 0, wqkv, wqkv_out)
    leave(4, 1, wout, wout_out)
    acc_vec[...] = jnp.zeros_like(acc_vec)

    for half in range(D // HEAD_DIM):
        cols = slice(half * HEAD_DIM, (half + 1) * HEAD_DIM)
        near = near_rim[half * 2 * WINDOW : (half + 1) * 2 * WINDOW, :]
        far = far_rim[half * 2 * WINDOW : (half + 1) * 2 * WINDOW, :]
        rim_x[:WINDOW, cols] = jnp.where(head == 0, far[:WINDOW], near[:WINDOW])
        rim_x[WINDOW:, cols] = jnp.where(head == 0, near[:WINDOW], far[:WINDOW])
        rim_cot[:, cols] = jnp.where(head == 0, near[WINDOW:], far[WINDOW:])

    att[WINDOW:, :HEAD_DIM] = own_att[WINDOW:, :]
    queries = (own_q, rim_q, qbuf)
    keys = (own_k, rim_k, kbuf)
    values = (own_v, rim_v, vbuf)

    def project_rim(j):
        here = slice(j * WINDOW, (j + 1) * WINDOW)
        there = slice(WINDOW, 2 * WINDOW) if j else slice(0, WINDOW)
        scaled, _ = standardize(rim_x[there, :].astype(F32))
        value = (scaled * gain1_ref[...] + shift1_ref[...]).astype(BF16)
        made = dot(value, wqkv[...]).astype(BF16)
        for part, (_, rim, other) in enumerate((queries, keys, values)):
            rim[there, :] = made[:, part * D : part * D + HEAD_DIM]
            other[here, :] = made[:, part * D + HEAD_DIM : (part + 1) * D]

    def project(i):
        here = slice(WINDOW + i * step, WINDOW + (i + 1) * step)
        made = dot(normed[i * step : (i + 1) * step, :], wother[...]).astype(BF16)
        for part, (_, _, other) in enumerate((queries, keys, values)):
            other[here, :] = made[:, part * HEAD_DIM : (part + 1) * HEAD_DIM]

    current, current_t, offset = masks()
    columns = [slice(h * HEAD_DIM, (h + 1) * HEAD_DIM) for h in range(HEADS)]
    held = {}

    def row_of(bufs, j, h):
        mine, rim, other = bufs
        if h:
            return other[j * WINDOW : (j + 1) * WINDOW, :]
        if 1 <= j <= rows:
            return mine[(j - 1) * WINDOW : j * WINDOW, :]
        return rim[WINDOW:, :] if j else rim[:WINDOW, :]

    def pair(bufs, j, h):
        if h:
            return bufs[2][(j - 1) * WINDOW : (j + 1) * WINDOW, :]
        if 1 < j <= rows:
            return bufs[0][(j - 2) * WINDOW : j * WINDOW, :]
        return jnp.concatenate([row_of(bufs, j - 1, 0), row_of(bufs, j, 0)])

    def grad_of(j, h):
        return gbuf[j * WINDOW : (j + 1) * WINDOW, columns[h]]

    def probs_of(j, h):
        if h:
            return probs.at[j - 1]
        return own_probs.at[j - 1] if 1 < j <= rows else probs.at[rows + 1 + (j > 1)]

    def key_sum(weights, queries):
        zero = jnp.zeros_like(weights)
        both = jnp.concatenate([jnp.where(current, zero, weights), jnp.where(current, weights, zero)])
        made = dot(both, queries)
        return made[:WINDOW], made[WINDOW:]

    def score(j, h):
        held[j, h] = merged_scores(pair(keys, j, h), row_of(queries, j, h), current)

    def soften(j, h):
        r = j - 1
        weights = soft_weights(
            held[j, h], offset, low_mark[r : r + 1, :WINDOW], fill_mark[r : r + 1, :WINDOW]
        )
        probs_of(j, h)[...] = weights
        held[j, h] = weights.astype(BF16)

    def gather(j, h):
        r = j - 1
        made = window_sum(held.pop((j, h)), pair(values, j, h), current_t).astype(BF16)
        if r < rows:
            att[r * WINDOW : (r + 1) * WINDOW, columns[h]] = made
        else:
            halo_att[:, columns[h]] = made

    def feed_forward(first, count, own_rows):
        at = first * WINDOW
        size = count * WINDOW
        here = slice(at, at + size)
        held = {}
        block = 256
        slot = at // step % 2
        grads = hid_grad.at[slot] if own_rows else halo_grad
        xs, cots, atts = (x_ref, cot_ref, att) if own_rows else (rim_x.at[pl.ds(WINDOW, WINDOW)], rim_cot, halo_att)
        there = here if own_rows else slice(0, size)

        def enter():
            if own_rows:
                if at >= 2 * step:
                    leaving[0, at // step - 2].wait()
                    leaving[2, at // step - 2].wait()
                leave(1, at // step, att.at[pl.ds(at, size)], att_out.at[pl.ds(at, size)])
            attended = atts[there, :]
            middle = xs[there, :].astype(F32) + split_dot(attended, wout[...])
            scaled, inverse = standardize(middle)
            held.update(scaled=scaled, inverse=inverse)
            held["normed"] = (scaled * gain2_ref[...] + shift2_ref[...]).astype(BF16)

        def hide(f):
            cols = slice(f * block, (f + 1) * block)
            hidden = dot(held["normed"], up_ref[:, cols]) + up_bias_ref[:, cols]
            active, slope = twice_gelu(hidden)
            grad = dot_lanes(cots[there, :], down_ref[cols, :]) * slope
            grads[:size, cols] = grad.astype(BF16)
            if own_rows:
                act[slot, :size, cols] = active.astype(BF16)
                acc_vec[8:9, cols] += column_sums(grad)

        def weigh(f):
            cols = slice(f * block, (f + 1) * block)
            down_part = dot(cot_t[:, here], act[slot, :size, cols])
            up_part = dot_rows(held["normed"], grads[:size, cols])
            if at:
                acc_down[:, cols] += down_part
                acc_up[:, cols] += up_part
            else:
                acc_down[:, cols] = down_part
                acc_up[:, cols] = up_part

        def back():
            if own_rows:
                leave(0, at // step, act.at[slot], act_out.at[pl.ds(at, size)])
            scaled = held["scaled"]
            g2 = split_dot(grads[:size, :], up_ref[...], dot_lanes)
            cot32 = cots[there, :].astype(F32)
            middle_grad = cot32 + normalize_back(g2 * gain2_ref[...], scaled, held["inverse"])
            mixing_grad = middle_grad.astype(BF16)
            if own_rows:
                mid_grad[slot, :, :] = middle_grad
                leave(2, at // step, mid_grad.at[slot], mid_grad_out.at[pl.ds(at, size)])
                acc_vec[2:3, :D] += column_sums(g2 * scaled)
                acc_vec[3:4, :D] += column_sums(g2)
                out_part = dot_rows(atts[there, :], mixing_grad)
                if at:
                    acc_out[...] += out_part
                else:
                    acc_out[...] = out_part
            made = split_dot(mixing_grad, wout[...], dot_lanes).astype(BF16)
            for g in range(count):
                j = first + 1 + g
                gbuf[j * WINDOW : (j + 1) * WINDOW, :] = made[g * WINDOW : (g + 1) * WINDOW]

        call = functools.partial
        parts = FF // block
        hides = [call(hide, f) for f in range(parts)]
        weighs = [call(weigh, f) for f in range(parts)] if own_rows else []
        return enter, hides, weighs, back

    held_back = {}
    unfinished = {}

    def weigh_grads(j, h):
        held_back[j, h] = merged_scores(pair(values, j, h), grad_of(j, h), current)

    def soften_back(j, h):
        dweights = held_back.pop((j, h))
        weights = probs_of(j, h)[...]
        inner = jnp.sum(weights * dweights, axis=0, keepdims=True)
        dscores = (weights * (dweights - inner)).astype(BF16)
        held_back[j, h] = (dscores, weights.astype(BF16))

    def gather_back(j, h):
        r = j - 1
        dscores, weights = held_back.pop((j, h))
        found = [key_sum(dscores, row_of(queries, j, h)), key_sum(weights, grad_of(j, h))]
        if j > 1:
            there = slice((r - 1) * WINDOW, r * WINDOW)
            for part, (before, _) in enumerate(found):
                total = unfinished[part, h] + before
                at = (part + 1) * D + h * HEAD_DIM
                dqkv[there, at : at + HEAD_DIM] = (total if part else total * SCALE).astype(BF16)
        for part, (_, current_part) in enumerate(found):
            unfinished[part, h] = current_part
        if j <= rows:
            dqkv[r * WINDOW : (r + 1) * WINDOW, columns[h]] = (
                window_sum(dscores, pair(keys, j, h), current_t) * SCALE
            ).astype(BF16)

    def project_back(i):
        at = i * step
        leave(3, i, dqkv.at[pl.ds(at, step)], dqkv_out.at[pl.ds(at, step)])
        made = dot(xhat_t[:, at : at + step], dqkv[at : at + step, :])
        acc_qkv[...] = (acc_qkv[...] + made) if at else made

    def units(first, last):
        return [(j, h) for j in range(first, last + 1) for h in range(HEADS)]

    project_rim(0)
    project_rim(rows + 1)
    for i in range(steps):
        project(i)
    forward = [(j, h) for j, h in units(1, rows + 1) if h or not 1 < j <= rows]
    do(staggered(forward, score, soften, gather))
    feeds = [feed_forward(i * CHUNK, CHUNK, True) for i in range(steps)]
    halo_enter, halo_hides, _, halo_back = feed_forward(rows, 1, False)
    halo = [halo_enter] + halo_hides + [halo_back]
    enter, hides, weighs, back = feeds[0]
    do([enter, halo.pop(0), hides[0], hides[1], weighs[0]])
    for i in range(steps):
        enter, hides, weighs, back = feeds[i]
        for f in range(2, len(hides)):
            do([hides[f], weighs[f - 1]] + halo[:1])
            halo = halo[1:]
        if i + 1 < steps:
            later = feeds[i + 1]
            do([later[0], weighs[-1], later[1][0], back, later[1][1], later[2][0]] + halo[:1])
            halo = halo[1:]
        else:
            do([weighs[-1]] + halo + [back])

    wide = FF // 2
    halves = ((core, keep_ref), (1 - core, send_ref))
    feed, heads = piece_rows(FF, D)
    quarter = feed - VECTOR_ROWS

    def spot(row):
        return row // quarter * (feed + heads) + row % quarter

    def export_down(c, ref, f):
        at = pl.ds(pl.multiple_of(c * wide + f, D), D)
        block = (acc_down[:, at] * 0.5).astype(BF16).T
        for half in range(D // HEAD_DIM):
            to = spot(half * wide + f)
            ref[to : to + D, :] = block[
                :, half * HEAD_DIM : (half + 1) * HEAD_DIM
            ]

    def export_up(c, ref, n):
        at = pl.ds(pl.multiple_of(c * wide + n * HEAD_DIM, HEAD_DIM), HEAD_DIM)
        to = spot(D // HEAD_DIM * wide + n * D)
        ref[to : to + D, :] = acc_up[:, at].astype(BF16)

    def export_heads(c, ref, h, part):
        mine = pl.ds(pl.multiple_of(c * HEAD_DIM, HEAD_DIM), HEAD_DIM)
        true_head = head if h == 0 else 1 - head
        if part < 3:
            at = part * D + h * HEAD_DIM
            block = acc_qkv[mine, at : at + HEAD_DIM]
        else:
            block = acc_out[h * HEAD_DIM : (h + 1) * HEAD_DIM, mine]
        piece, shift = true_head + part // 2 * 2, part % 2 * HEAD_DIM
        first = piece * (feed + heads) + feed + shift
        second = part * (feed + heads) + feed + true_head * HEAD_DIM
        at = jnp.where(c == 0, first, second)
        ref[pl.ds(pl.multiple_of(at, 16), HEAD_DIM), :] = block.astype(BF16)

    def export_vectors(c, ref):
        flat = vec_rows[pl.ds(pl.multiple_of(c * 16, 16), 16), :].astype(BF16)
        for piece in range(4):
            to = piece * (feed + heads) + quarter
            ref[to : to + VECTOR_ROWS, :] = flat

    call = functools.partial
    exports = [call(export_down, c, ref, f) for c, ref in halves for f in range(0, wide, D)]
    exports += [call(export_up, c, ref, n) for c, ref in halves for n in range(wide // HEAD_DIM)]
    exports += [call(export_heads, c, ref, h, 3) for c, ref in halves for h in range(HEADS)]
    backs = staggered(units(1, rows + 1), weigh_grads, soften_back, gather_back)
    marks = []
    for i in range(steps):
        done = [n for n, job in enumerate(backs) if job.func is gather_back and job.args == ((i + 1) * CHUNK + 1, 1)]
        marks.append(done[0] + 1)
    do(merge(backs[: marks[0]], exports))
    for i in range(1, steps):
        project_back(i - 1)
        do(backs[marks[i - 1] : marks[i]])
    do(backs[marks[-1] :])
    project_back(steps - 1)

    gain_t = jnp.broadcast_to(gain1_ref[...], (HEAD_DIM, D)).T
    shift_t = jnp.broadcast_to(shift1_ref[...], (HEAD_DIM, D)).T
    gain_sum = jnp.zeros((D, HEAD_DIM), F32)
    shift_sum = jnp.zeros((D, HEAD_DIM), F32)
    for n in range(3 * D // HEAD_DIM):
        cols = slice(n * HEAD_DIM, (n + 1) * HEAD_DIM)
        product = acc_qkv[:D, cols]
        total = acc_qkv[D : D + 1, cols]
        weight = wqkv[:, cols].astype(F32)
        gain_sum += weight * product
        shift_sum += weight * total
        acc_qkv[:D, cols] = gain_t * product + shift_t * total
    acc_vec[0:1, :D] = column_sums(gain_sum.T)
    acc_vec[1:2, :D] = column_sums(shift_sum.T)
    acc_vec[4:5, :D] = column_sums(cot_sum[...])

    for c, ref in halves:
        do([call(export_heads, c, ref, h, part) for h in range(HEADS) for part in range(3)])
    for n, (row, cols) in enumerate(vector_slots(FF, D)):
        vec_rows[n : n + 1, :] = acc_vec[row : row + 1, cols]
    for c, ref in halves:
        export_vectors(c, ref)
    for (kind, n), copy in leaving.items():
        if kind not in (0, 2) or n >= steps - 2:
            copy.wait()


def layer(rims, made, tokens, up, gain1, shift1, weights, others, gain2, shift2, up_bias):
    own, D = tokens.shape
    FF = up.shape[1]
    rows = own // WINDOW
    count = own + 2 * WINDOW
    half = half_rows(FF, D)
    tokens, up = in_vmem(tokens), in_vmem(up)
    rims, made, others = ([in_vmem(array) for array in arrays] for arrays in (rims, made, others))
    vmem = pl.BlockSpec(memory_space=pltpu.VMEM)
    return pl.pallas_call(
        functools.partial(layer_kernel, rows),
        out_shape=(
            pltpu.VMEM((half, HEAD_DIM), BF16),
            pltpu.VMEM((half, HEAD_DIM), BF16),
            pltpu.HBM((own, FF), BF16),
            pltpu.HBM((own, D), BF16),
            pltpu.HBM((own, D), F32),
            pltpu.HBM((own, 3 * D), BF16),
            pltpu.HBM((D, 3 * D), BF16),
            pltpu.HBM((D, D), BF16),
        ),
        in_specs=[vmem] * (2 + len(made) + 2 + 2 + 4 + 2 + 3),
        out_specs=(vmem, vmem) + (pl.BlockSpec(memory_space=pltpu.HBM),) * 6,
        scratch_shapes=[
            pltpu.VMEM((2, CHUNK * WINDOW, FF), BF16),
            pltpu.VMEM((own, D), BF16),
            pltpu.VMEM((2, CHUNK * WINDOW, D), F32),
            pltpu.VMEM((own, 3 * D), BF16),
            pltpu.VMEM((D, 3 * D), BF16),
            pltpu.VMEM((D, D), BF16),
            pltpu.VMEM((2 * WINDOW, D), BF16),
            pltpu.VMEM((WINDOW, D), BF16),
            pltpu.VMEM((WINDOW, FF), BF16),
            pltpu.VMEM((WINDOW, D), BF16),
            pltpu.VMEM((D, 3 * HEAD_DIM), BF16),
            pltpu.VMEM((2 * WINDOW, HEAD_DIM), BF16),
            pltpu.VMEM((2 * WINDOW, HEAD_DIM), BF16),
            pltpu.VMEM((2 * WINDOW, HEAD_DIM), BF16),
            pltpu.VMEM((count, HEAD_DIM), BF16),
            pltpu.VMEM((count, HEAD_DIM), BF16),
            pltpu.VMEM((count, HEAD_DIM), BF16),
            pltpu.VMEM((count, D), BF16),
            pltpu.VMEM((rows + 3, WINDOW, WINDOW), F32),
            pltpu.VMEM((2, CHUNK * WINDOW, FF), BF16),
            pltpu.VMEM((D, FF), F32),
            pltpu.VMEM((D, FF), F32),
            pltpu.VMEM((D + 16, 3 * D), F32),
            pltpu.VMEM((D, D), F32),
            pltpu.VMEM((16, FF), F32),
            pltpu.VMEM((32, HEAD_DIM), F32),
            pltpu.SemaphoreType.DMA((5, max(rows // CHUNK, 2))),
        ],
        compiler_params=pltpu.CompilerParams(vmem_limit_bytes=34 * 1024 * 1024),
        name="layer",
    )(*rims, *made, tokens, up, gain1, shift1, *weights, *others, gain2, shift2, up_bias)


def token_chunks(streams, out_ref, buf, in_sem, out_sem, fixed, work):
    step = CHUNK * WINDOW
    arriving = [pltpu.make_async_copy(a, b, in_sem.at[0, n]) for n, (a, b) in enumerate(fixed)]
    steps = buf.shape[0] // step
    chunks = []
    for i in range(steps):
        here = pl.ds(i * step, step)
        chunks.append(
            [pltpu.make_async_copy(a.at[here], b.at[here], in_sem.at[i + 1, n]) for n, (a, b) in enumerate(streams)]
        )
    for copy in arriving + [copy for chunk in chunks for copy in chunk]:
        copy.start()
    for copy in arriving:
        copy.wait()
    leaving = []
    for i in range(steps):
        for copy in chunks[i]:
            copy.wait()
        work(slice(i * step, (i + 1) * step))
        here = pl.ds(i * step, step)
        leaving.append(pltpu.make_async_copy(buf.at[here], out_ref.at[here], out_sem.at[i]))
        leaving[-1].start()
    for copy in leaving:
        copy.wait()


def input_grad_kernel(
    x_in, mid_in, dqkv_in, wqkv_in, gain1_ref, out_ref, buf, in_sem, out_sem, x_ref, mid_grad, dqkv, wqkv
):
    def work(here):
        scaled, inverse = standardize(x_ref[here, :].astype(F32))
        g1 = split_dot(dqkv[here, :], wqkv[...], dot_lanes)
        buf[here, :] = (
            mid_grad[here, :] + normalize_back(g1 * gain1_ref[...], scaled, inverse)
        ).astype(BF16)

    streams = ((x_in, x_ref), (mid_in, mid_grad), (dqkv_in, dqkv))
    token_chunks(streams, out_ref, buf, in_sem, out_sem, ((wqkv_in, wqkv),), work)


def mixed_kernel(
    x_in, att_in, act_in, wout_in, down_in, down_bias_ref, out_ref, buf, in_sem, out_sem, x_ref, att, act, wout, down
):
    def work(here):
        middle = x_ref[here, :].astype(F32) + split_dot(att[here, :], wout[...])
        mixed = middle + split_dot(act[here, :], down[...]) * 0.5 + down_bias_ref[...]
        buf[here, :] = mixed.astype(BF16)

    streams = ((x_in, x_ref), (att_in, att), (act_in, act))
    token_chunks(streams, out_ref, buf, in_sem, out_sem, ((wout_in, wout), (down_in, down)), work)


def late(kernel, name, arrays, small):
    own, D = arrays[0].shape
    steps = own // (CHUNK * WINDOW)
    hbm = pl.BlockSpec(memory_space=pltpu.HBM)
    return pl.pallas_call(
        kernel,
        out_shape=pltpu.HBM((own, D), BF16),
        in_specs=[hbm] * len(arrays) + [pl.BlockSpec(memory_space=pltpu.VMEM)],
        out_specs=hbm,
        scratch_shapes=[
            pltpu.VMEM((own, D), BF16),
            pltpu.SemaphoreType.DMA((steps + 1, 3)),
            pltpu.SemaphoreType.DMA((steps,)),
        ]
        + [pltpu.VMEM(array.shape, array.dtype) for array in arrays],
        compiler_params=pltpu.CompilerParams(vmem_limit_bytes=32 * 1024 * 1024),
        name=name,
    )(*[in_hbm(array) for array in arrays], small)


def pack_kernel(query_ref, key_ref, value_ref, out_ref, tok_ref, cot_ref, half_ref, near_ref, far_ref, sem):
    D = query_ref.shape[0]
    own = tok_ref.shape[0]
    head = lax.axis_index("head")
    core = lax.axis_index("seq") % 2
    last = own - WINDOW
    near_from = pl.multiple_of((1 - head) * last, WINDOW)
    far_from = pl.multiple_of(head * last, WINDOW)
    moves = []
    for half in range(D // HEAD_DIM):
        cols = pl.ds(half * HEAD_DIM, HEAD_DIM)
        for k, ref in enumerate((tok_ref, cot_ref)):
            at = (half * 2 + k) * WINDOW
            moves.append((ref.at[pl.ds(near_from, WINDOW), cols], near_ref.at[pl.ds(at, WINDOW)]))
            moves.append((ref.at[pl.ds(far_from, WINDOW), cols], far_ref.at[pl.ds(at, WINDOW)]))
    copies = [pltpu.make_async_copy(a, b, sem.at[n]) for n, (a, b) in enumerate(moves)]
    for copy in copies:
        copy.start()

    def weights(moves):
        sent = [pltpu.make_async_copy(a, b, sem.at[len(copies) + n]) for n, (a, b) in enumerate(moves)]
        for copy in sent:
            copy.start()
        for copy in sent:
            copy.wait()

    @pl.when(core == 0)
    def _():
        weights([(query_ref, half_ref.at[pl.ds(0, D)]), (key_ref, half_ref.at[pl.ds(D, D)])])

    @pl.when(core == 1)
    def _():
        outs = [
            (
                out_ref.at[:, pl.ds(half * HEAD_DIM, HEAD_DIM)],
                half_ref.at[pl.ds(D + half * HEAD_DIM, HEAD_DIM)],
            )
            for half in range(D // HEAD_DIM)
        ]
        weights([(value_ref, half_ref.at[pl.ds(0, D)])] + outs)

    for copy in copies:
        copy.wait()


def pack(query_weight, key_weight, value_weight, out_weight, tokens, cotangent):
    D = query_weight.shape[0]
    rim = 2 * WINDOW * D // HEAD_DIM
    vmem = pl.BlockSpec(memory_space=pltpu.VMEM)
    return pl.pallas_call(
        pack_kernel,
        out_shape=(
            pltpu.VMEM((2 * D, HEAD_DIM), BF16),
            pltpu.VMEM((rim, HEAD_DIM), BF16),
            pltpu.VMEM((rim, HEAD_DIM), BF16),
        ),
        in_specs=[pl.BlockSpec(memory_space=pl.ANY)] * 6,
        out_specs=(vmem, vmem, vmem),
        scratch_shapes=[pltpu.SemaphoreType.DMA((6 * (D // HEAD_DIM) + 1,))],
        name="pack",
    )(query_weight, key_weight, value_weight, out_weight, tokens, cotangent)


def finish_kernel(FF, D, second, mine_ref, *refs):
    if second:
        vectors, refs = (refs[0], refs[7:13]), refs[13:]
    outs, (down_buf, up_buf, heads_buf, vec_rows, sem) = refs[:6], refs[6:]
    query, key, value, out, up, down = outs
    core = lax.axis_index("seq") % 2
    c = 1 - core if second else core
    wide = FF // 2
    copies = []

    def leave(source, target):
        copies.append(pltpu.make_async_copy(source, target, sem.at[len(copies)]))
        copies[-1].start()

    feed = piece_rows(FF, D)[0]
    quarter = feed - VECTOR_ROWS
    for half in range(D // HEAD_DIM):
        at = half * wide // quarter * feed + half * wide % quarter
        down_buf[:, half * HEAD_DIM : (half + 1) * HEAD_DIM] = mine_ref[at : at + wide, :].astype(F32)
    leave(down_buf, down.at[pl.ds(pl.multiple_of(c * wide, wide), wide)])
    start = D // HEAD_DIM * wide
    for n, f in enumerate(range(0, wide, HEAD_DIM)):
        at = (start + n * D) // quarter * feed + (start + n * D) % quarter
        up_buf[:, f : f + HEAD_DIM] = mine_ref[at : at + D, :].astype(F32)
    leave(up_buf, up.at[:, pl.ds(pl.multiple_of(c * wide, wide), wide)])
    start = 4 * feed
    own = pl.ds(pl.multiple_of(c * HEAD_DIM, HEAD_DIM), HEAD_DIM)
    for part, made in enumerate((query, key, value, out)):
        at = start + part * HEAD_DIM
        heads_buf[part] = mine_ref[at : at + HEAD_DIM, :].astype(F32)
        leave(heads_buf.at[part], made.at[:, own] if part == 3 else made.at[own])
    if second:
        other_ref, made = vectors
        at = quarter
        for k, ref in ((c, mine_ref), (core, other_ref)):
            vec_rows[pl.ds(pl.multiple_of(k * 16, 16), 16), :] = ref[at : at + 16, :].astype(F32)
        for s, (n, cols) in enumerate(vector_slots(FF, D)):
            made[5 if n == 8 else n][cols] = vec_rows[s, :]
    for copy in copies:
        copy.wait()


def finish(mine, FF, D, first=None):
    vmem = pl.BlockSpec(memory_space=pltpu.VMEM)
    hbm = pl.BlockSpec(memory_space=pltpu.HBM)
    arrays = [(D, HEAD_DIM)] * 3 + [(HEAD_DIM, D), (D, FF), (FF, D)]
    vectors = [(D,)] * 5 + [(FF,)] if first else []
    wide = FF // 2
    given = (in_vmem(first[0]), *[in_hbm(array) for array in first[1]]) if first else ()
    return pl.pallas_call(
        functools.partial(finish_kernel, FF, D, bool(first)),
        out_shape=tuple(jax.ShapeDtypeStruct(shape, F32) for shape in vectors)
        + tuple(pltpu.HBM(shape, F32) for shape in arrays),
        in_specs=[vmem] + ([vmem] + [hbm] * 6 if first else []),
        out_specs=(vmem,) * len(vectors) + (hbm,) * 6,
        input_output_aliases={2 + n: 6 + n for n in range(6)} if first else {},
        scratch_shapes=[
            pltpu.VMEM((wide, D), F32),
            pltpu.VMEM((D, wide), F32),
            pltpu.VMEM((4, HEAD_DIM, HEAD_DIM), F32),
            pltpu.VMEM((32, HEAD_DIM), F32),
            pltpu.SemaphoreType.DMA((6,)),
        ],
        name="finish_rest" if first else "finish",
    )(in_vmem(mine), *given)


def spans(masks):
    found = [0]
    for mask in masks:
        found = found + [f ^ mask for f in found]
    return found


def stages(count):
    bits = [1 << b for b in range(count.bit_length() - 1)]
    plane, rest = [bits[0], bits[2]], bits[3:]
    found = [plane] + [rest[i : i + 2] for i in range(0, len(rest), 2)]
    if len(found) > 1 and len(found[1]) == 2:
        return [(found[0], found[1][::-1]), (found[1], found[0])] + [(masks, masks) for masks in found[2:]]
    return [(masks, masks) for masks in found]


def partners(value, masks, k):
    count = lax.axis_size("seq") * lax.axis_size("head")
    hops = [spans(side)[k] for side in masks]
    return lax.ppermute(value, BOTH, [(i, i ^ hops[i // 2 % 2]) for i in range(count)])


def all_sum(value, side, FF, D):
    count = lax.axis_size("seq") * lax.axis_size("head")
    place = lax.axis_index("seq") * lax.axis_size("head") + lax.axis_index("head")
    width = value.shape[1]
    made = []
    steps = []
    for masks in stages(count):
        code, other_code = (
            sum(((place & mask) // mask) << j for j, mask in enumerate(bits)) for bits in masks
        )
        steps.append((masks, jnp.where(place & 2 == 0, code, other_code)))

    def exchange(value, send, masks, number):
        if number >= len(side):
            return [partners(send(value, k), masks, k) for k in range(1, 1 << len(masks[0]))]
        work, small = side[number]
        value, small = lax.optimization_barrier((value, small))
        arrived = [partners(send(value, k), masks, k) for k in range(1, 1 << len(masks[0]))]
        arrived, done = lax.optimization_barrier((arrived, work(small)))
        made.append(done)
        return arrived

    def spread(value, masks, code, number):
        found = [value] + exchange(value, lambda v, k: v, masks, number)
        whole = jnp.zeros((len(found),) + value.shape, value.dtype)
        for k, part in enumerate(found):
            whole = lax.dynamic_update_index_in_dim(whole, part, code ^ k, 0)
        return whole

    for number, (masks, code) in enumerate(steps[:-1]):
        parts = value.reshape(1 << len(masks[0]), -1, width)
        total = lax.dynamic_index_in_dim(parts, code, 0, False).astype(F32)
        pick = lambda parts, k, code=code: lax.dynamic_index_in_dim(parts, code ^ k, 0, False)
        for part in exchange(parts, pick, masks, number):
            total = total + part.astype(F32)
        value = total.astype(BF16)
    whole = spread(value, *steps[-1], len(steps) - 1)
    total = whole[0].astype(F32)
    for part in whole[1:]:
        total = total + part.astype(F32)
    value = total.astype(BF16)
    for masks, code in steps[-2:0:-1]:
        value = spread(value, masks, code, len(side)).reshape(-1, width)
    masks, code = steps[0]
    feed, heads = piece_rows(FF, D)
    head = lax.axis_index("head")
    first_core = place & 2 == 0
    mine, other = value[feed : feed + heads // 2], value[feed + heads // 2 :]
    swap = jnp.logical_and(jnp.logical_not(first_core), head == 1)
    value = jnp.concatenate([value[:feed], jnp.where(swap, other, mine), jnp.where(swap, mine, other)])
    short = value[: feed + heads // 2]
    found = [value, partners(short, masks, 1), partners(value, masks, 2), partners(short, masks, 3)]
    whole = jnp.zeros((4 * feed, width), value.dtype)
    by_half = jnp.zeros((2 * heads, width), value.dtype)
    by_part = by_half
    for k, part in enumerate(found):
        whole = lax.dynamic_update_slice_in_dim(whole, part[:feed], (code ^ k) * feed, 0)
        by_part = lax.dynamic_update_slice_in_dim(
            by_part, part[feed : feed + heads // 2], (code ^ k) * (heads // 2), 0
        )
        if k % 2 == 0:
            by_half = lax.dynamic_update_slice_in_dim(by_half, part[feed:], ((code ^ k) // 2) * heads, 0)
    return jnp.concatenate([whole, jnp.where(first_core, by_half, by_part)]), made


def across_cores(value):
    return partners(value, ([2], [2]), 1)


def shards(
    tokens,
    cotangent,
    image_rows,
    image_fill,
    first_gain,
    first_shift,
    query_weight,
    key_weight,
    value_weight,
    out_weight,
    second_gain,
    second_shift,
    up_weight,
    up_bias,
    down_weight,
    down_bias,
):
    own, D = tokens.shape
    FF = up_weight.shape[1]
    devices = lax.axis_size("seq") * lax.axis_size("head")
    half, near, far = pack(query_weight, key_weight, value_weight, out_weight, tokens, cotangent)
    half = lax.ppermute(half, "head", [(0, 1), (1, 0)])
    pairs = [(i, i + 1) for i in range(1, devices - 1, 2)]
    far = lax.ppermute(far, BOTH, pairs + [(b, a) for a, b in pairs])
    near = lax.ppermute(near, "head", [(0, 1), (1, 0)])
    weights = (query_weight, key_weight, value_weight, out_weight)
    gain1, shift1 = first_gain[None], first_shift[None]
    made = local(tokens, cotangent, down_weight, image_rows[None], image_fill[None], gain1, shift1, weights)
    half, near, far, mark = lax.optimization_barrier((half, near, far, made[6]))
    made = (*made[:6], mark, *made[7:])
    keep, send, act, att, mid_grad, dqkv, wqkv, wout = layer(
        (near, far),
        made,
        tokens,
        up_weight,
        gain1,
        shift1,
        weights,
        (half, across_cores(half)),
        second_gain[None],
        second_shift[None],
        up_bias[None],
    )
    side = [
        (lambda small: late(input_grad_kernel, "input_grad", (tokens, mid_grad, dqkv, wqkv), small), gain1),
        (lambda small: late(mixed_kernel, "mixed", (tokens, att, act, wout, down_weight), small), down_bias[None]),
    ]
    summed = (keep.astype(F32) + across_cores(send).astype(F32)).astype(BF16)
    mine, (input_grad, mixed) = all_sum(summed, side, FF, D)
    arrays = finish(mine, FF, D)
    gain1_grad, shift1_grad, gain2_grad, shift2_grad, down_bias_grad, up_bias_grad, *arrays = finish(
        across_cores(mine), FF, D, (mine, arrays)
    )
    query_grad, key_grad, value_grad, out_grad, up_grad, down_grad = arrays
    return (
        mixed,
        input_grad,
        gain1_grad,
        shift1_grad,
        query_grad,
        key_grad,
        value_grad,
        out_grad,
        gain2_grad,
        shift2_grad,
        up_grad,
        up_bias_grad,
        down_grad,
        down_bias_grad,
    )


def solution(mesh):
    stream = P(("seq", "head"), None)
    columns = P(None, "head")
    in_specs = (stream, stream) + (P(),) * 4 + (columns,) * 3 + (P("head", None),) + (P(),) * 6
    out_specs = (
        (stream, stream) + (P(),) * 2 + (columns,) * 3 + (P("head", None),) + (P(),) * 6
    )
    return jax.shard_map(shards, mesh=mesh, in_specs=in_specs, out_specs=out_specs, check_vma=False)
```

```python
import functools

import jax
import jax.numpy as jnp
from jax import lax
from jax.experimental import pallas as pl
from jax.experimental.pallas import tpu as pltpu
from jax.sharding import PartitionSpec as P

HEAD_DIM = 128
HEADS = 2
WINDOW = 96
BOTH = ("seq", "head")

EPSILON = 1e-05
MASKED = -1000000000.0
LOG2E = 1.4426950408889634
SCALE = HEAD_DIM ** (-0.5)

F32 = jnp.float32
BF16 = jnp.bfloat16
LANES = (((1,), (1,)), ((), ()))
ROWS = (((0,), (0,)), ((), ()))

CHUNK = 8
LAG = 6


def dot(a, b):
    return jnp.dot(a, b, preferred_element_type=F32)


def split_dot(a, b, how=None):
    how = how or dot
    half = a.shape[0] // 2
    if half % 16:
        return how(a, b)
    return jnp.concatenate([how(a[:half], b), how(a[half:], b)])


def dot_lanes(a, b):
    return lax.dot_general(a, b, LANES, preferred_element_type=F32)


def dot_rows(a, b):
    return lax.dot_general(a, b, ROWS, preferred_element_type=F32)


def standardize(inputs):
    center = inputs - jnp.mean(inputs, axis=1, keepdims=True)
    spread = jnp.mean(center * center, axis=1, keepdims=True)
    inverse = lax.rsqrt(spread + EPSILON)
    return center * inverse, inverse


def normalize_back(weighted, scaled, inverse):
    return inverse * (
        weighted
        - jnp.mean(weighted, axis=1, keepdims=True)
        - scaled * jnp.mean(weighted * scaled, axis=1, keepdims=True)
    )


def twice_gelu(x):
    z = x * 0.7071067811865476
    below = 1.0 + lax.erf(z)
    bell = jnp.exp2(z * z * -LOG2E)
    return x * below, below + x * bell * 0.7978845608028654


def column_sums(value):
    return jnp.sum(value, axis=0, keepdims=True)


def merge(*lists):
    marked = [
        ((n + 0.5) / len(work), k, n, job) for k, work in enumerate(lists) for n, job in enumerate(work)
    ]
    return [job for *_, job in sorted(marked, key=lambda item: item[:3])]


VECTOR_ROWS = 16


def piece_rows(FF, D):
    return 2 * FF * D // (8 * HEAD_DIM) + VECTOR_ROWS, 4 * D * D // (8 * HEAD_DIM)


def half_rows(FF, D):
    return 4 * sum(piece_rows(FF, D))


def vector_slots(FF, D):
    found = [
        (n, slice(c, c + HEAD_DIM)) for n in range(5) for c in range(0, D, HEAD_DIM)
    ]
    return found + [(8, slice(c, c + HEAD_DIM)) for c in range(0, FF, HEAD_DIM)]


def masks():
    key_id = lax.broadcasted_iota(jnp.int32, (WINDOW, WINDOW), 0)
    query_id = lax.broadcasted_iota(jnp.int32, (WINDOW, WINDOW), 1)
    current = key_id <= query_id
    return current, key_id >= query_id, jnp.where(current, key_id, key_id - WINDOW)


def merged_scores(keys, query, current):
    raw = dot_lanes(keys, query)
    return jnp.where(current, raw[WINDOW:], raw[:WINDOW])


def soft_weights(scores, offset, low, fill):
    keep = (offset >= low) & (offset < fill)
    scores = jnp.where(keep, scores * (SCALE * LOG2E), MASKED * LOG2E)
    lifted = jnp.exp2(scores - jnp.max(scores, axis=0, keepdims=True))
    return lifted * (1.0 / jnp.sum(lifted, axis=0, keepdims=True))


def window_sum(weights, values, current_t):
    turned = weights.T
    zero = jnp.zeros_like(turned)
    return dot(jnp.where(current_t, zero, turned), values[:WINDOW]) + dot(
        jnp.where(current_t, turned, zero), values[WINDOW:]
    )


def staggered(units, *kinds, lag=LAG):
    jobs = []
    for t in range(len(units) + lag * (len(kinds) - 1)):
        for k, kind in enumerate(kinds):
            if 0 <= t - lag * k < len(units):
                jobs.append(functools.partial(kind, *units[t - lag * k]))
    return jobs


def do(jobs):
    for job in jobs:
        job()


def local_kernel(
    rows,
    x_ref,
    cot_in_ref,
    down_in_ref,
    image_rows_ref,
    image_fill_ref,
    gain1_ref,
    shift1_ref,
    query_ref,
    key_ref,
    value_ref,
    normed,
    qbuf,
    kbuf,
    vbuf,
    probs,
    att,
    low_mark,
    fill_mark,
    xhat_t,
    cot_t,
    cot_ref,
    down_ref,
    cot_sum,
    weight,
    in_sem,
):
    D = x_ref.shape[1]
    step = CHUNK * WINDOW
    xhat_t[D:, :] = jnp.ones((16, rows * WINDOW), BF16)
    place = lax.axis_index("seq") * lax.axis_size("head") + lax.axis_index("head")
    for part, ref in enumerate((query_ref, key_ref, value_ref)):
        weight[:, part * HEAD_DIM : (part + 1) * HEAD_DIM] = ref[...]
    later = [
        pltpu.make_async_copy(a, b, in_sem.at[n])
        for n, (a, b) in enumerate(((cot_in_ref, cot_ref), (down_in_ref, down_ref)))
    ]
    for copy in later:
        copy.start()

    images = image_rows_ref.shape[1]
    earlier = lax.broadcasted_iota(jnp.int32, (images, images), 0) <= lax.broadcasted_iota(
        jnp.int32, (images, images), 1
    )
    counts = jnp.broadcast_to(image_rows_ref[...], (8, images)).astype(F32)
    ends = dot(counts.astype(BF16), jnp.where(earlier, 1.0, 0.0).astype(BF16))[:1]
    starts = ends - counts[:1]
    mark_rows = low_mark.shape[0]
    row = (place * rows + lax.broadcasted_iota(jnp.int32, (mark_rows, 1), 0)).astype(F32)
    opens = jnp.sum(jnp.where(starts == row, 1.0, 0.0), axis=1, keepdims=True)
    opens = jnp.where(row >= ends[:, images - 1 :], 1.0, opens)
    missing = WINDOW - image_fill_ref[...].astype(F32)
    short = jnp.sum(jnp.where(ends == row + 1.0, missing, 0.0), axis=1, keepdims=True)
    low_mark[...] = jnp.broadcast_to(
        jnp.where(opens > 0.0, 0.0, -1.0 * WINDOW), low_mark.shape
    ).astype(jnp.int32)
    fill_mark[...] = jnp.broadcast_to(WINDOW - short, fill_mark.shape).astype(jnp.int32)

    for i in range(rows // CHUNK):
        here = slice(i * step, (i + 1) * step)
        scaled, _ = standardize(x_ref[here, :].astype(F32))
        xhat_t[:D, here] = scaled.astype(BF16).T
        value = (scaled * gain1_ref[...] + shift1_ref[...]).astype(BF16)
        normed[here, :] = value
        made = dot(value, weight[...]).astype(BF16)
        for part, buf in enumerate((qbuf, kbuf, vbuf)):
            buf[here, :] = made[:, part * HEAD_DIM : (part + 1) * HEAD_DIM]

    current, current_t, offset = masks()
    held = {}

    def score(r):
        held[r] = merged_scores(
            kbuf[(r - 1) * WINDOW : (r + 1) * WINDOW, :], qbuf[r * WINDOW : (r + 1) * WINDOW, :], current
        )

    def soften(r):
        weights = soft_weights(
            held[r], offset, low_mark[r : r + 1, :WINDOW], fill_mark[r : r + 1, :WINDOW]
        )
        probs[r] = weights
        held[r] = weights.astype(BF16)

    def gather(r):
        values = vbuf[(r - 1) * WINDOW : (r + 1) * WINDOW, :]
        att[r * WINDOW : (r + 1) * WINDOW, :] = window_sum(held.pop(r), values, current_t).astype(BF16)

    do(staggered([(r,) for r in range(1, rows)], score, soften, gather, lag=2))
    for copy in later:
        copy.wait()
    cot_t[...] = cot_ref[...].T
    down_ref[...] = (down_ref[...].astype(F32) * 0.5).astype(BF16)
    total = jnp.zeros((8, D), F32)
    for i in range(rows // CHUNK):
        total += jnp.sum(cot_ref[i * step : (i + 1) * step, :].astype(F32).reshape(step // 8, 8, D), axis=0)
    cot_sum[...] = total


def in_vmem(array):
    return pltpu.with_memory_space_constraint(array, pltpu.VMEM)


def in_hbm(array):
    return pltpu.with_memory_space_constraint(array, pltpu.HBM)


def local(tokens, cotangent, down, image_rows, image_fill, gain1, shift1, weights):
    own, D = tokens.shape
    rows = own // WINDOW
    mark_rows = -(-(rows + 1) // 8) * 8
    vmem = pl.BlockSpec(memory_space=pltpu.VMEM)
    return pl.pallas_call(
        functools.partial(local_kernel, rows),
        out_shape=(
            pltpu.VMEM((own, D), BF16),
            pltpu.VMEM((own, HEAD_DIM), BF16),
            pltpu.VMEM((own, HEAD_DIM), BF16),
            pltpu.VMEM((own, HEAD_DIM), BF16),
            pltpu.VMEM((rows, WINDOW, WINDOW), F32),
            pltpu.VMEM((own, HEAD_DIM), BF16),
            pltpu.VMEM((mark_rows, 128), jnp.int32),
            pltpu.VMEM((mark_rows, 128), jnp.int32),
            pltpu.VMEM((D + 16, own), BF16),
            pltpu.VMEM((D, own), BF16),
            pltpu.VMEM((own, D), BF16),
            pltpu.VMEM(down.shape, BF16),
            pltpu.VMEM((8, D), F32),
        ),
        in_specs=[vmem] + [pl.BlockSpec(memory_space=pltpu.HBM)] * 2 + [vmem] * 7,
        out_specs=(vmem,) * 13,
        scratch_shapes=[
            pltpu.VMEM((D, 3 * HEAD_DIM), BF16),
            pltpu.SemaphoreType.DMA((2,)),
        ],
        compiler_params=pltpu.CompilerParams(vmem_limit_bytes=24 * 1024 * 1024),
        name="local",
    )(
        in_vmem(tokens), in_hbm(cotangent), in_hbm(down), image_rows, image_fill, gain1, shift1, *weights[:3]
    )


def layer_kernel(
    rows,
    near_rim,
    far_rim,
    normed,
    own_q,
    own_k,
    own_v,
    own_probs,
    own_att,
    low_mark,
    fill_mark,
    xhat_t,
    cot_t,
    cot_ref,
    down_ref,
    cot_sum,
    x_ref,
    up_ref,
    gain1_ref,
    shift1_ref,
    query_ref,
    key_ref,
    value_ref,
    out_ref,
    half_ref,
    other_half_ref,
    gain2_ref,
    shift2_ref,
    up_bias_ref,
    keep_ref,
    send_ref,
    act_out,
    att_out,
    mid_grad_out,
    dqkv_out,
    wqkv_out,
    wout_out,
    act,
    att,
    mid_grad,
    dqkv,
    wqkv,
    wout,
    rim_x,
    rim_cot,
    halo_grad,
    halo_att,
    wother,
    rim_q,
    rim_k,
    rim_v,
    qbuf,
    kbuf,
    vbuf,
    gbuf,
    probs,
    hid_grad,
    acc_down,
    acc_up,
    acc_qkv,
    acc_out,
    acc_vec,
    vec_rows,
    out_sem,
):
    D = x_ref.shape[1]
    FF = up_ref.shape[1]
    own = rows * WINDOW
    head = lax.axis_index("head")
    place = lax.axis_index("seq") * lax.axis_size("head") + head
    core = (place & 2) // 2
    step = CHUNK * WINDOW
    steps = rows // CHUNK
    leaving = {}

    def leave(kind, n, source, target):
        leaving[kind, n] = pltpu.make_async_copy(source, target, out_sem.at[kind, n])
        leaving[kind, n].start()

    def theirs(at, size):
        half, at = at // (2 * D), at % (2 * D)
        here, there = half_ref[at : at + size, :], other_half_ref[at : at + size, :]
        return jnp.where(core == half, here, there)

    for part, ref in enumerate((query_ref, key_ref, value_ref)):
        wqkv[:, part * D : part * D + HEAD_DIM] = ref[...]
        wqkv[:, part * D + HEAD_DIM : (part + 1) * D] = theirs(part * D, D)
        wother[:, part * HEAD_DIM : (part + 1) * HEAD_DIM] = theirs(part * D, D)
    wout[:HEAD_DIM, :] = out_ref[...]
    for half in range(D // HEAD_DIM):
        wout[HEAD_DIM:, half * HEAD_DIM : (half + 1) * HEAD_DIM] = theirs(
            3 * D + half * HEAD_DIM, HEAD_DIM
        )
    leave(4, 0, wqkv, wqkv_out)
    leave(4, 1, wout, wout_out)
    acc_vec[...] = jnp.zeros_like(acc_vec)

    for half in range(D // HEAD_DIM):
        cols = slice(half * HEAD_DIM, (half + 1) * HEAD_DIM)
        near = near_rim[half * 2 * WINDOW : (half + 1) * 2 * WINDOW, :]
        far = far_rim[half * 2 * WINDOW : (half + 1) * 2 * WINDOW, :]
        rim_x[:WINDOW, cols] = jnp.where(head == 0, far[:WINDOW], near[:WINDOW])
        rim_x[WINDOW:, cols] = jnp.where(head == 0, near[:WINDOW], far[:WINDOW])
        rim_cot[:, cols] = jnp.where(head == 0, near[WINDOW:], far[WINDOW:])

    att[WINDOW:, :HEAD_DIM] = own_att[WINDOW:, :]
    queries = (own_q, rim_q, qbuf)
    keys = (own_k, rim_k, kbuf)
    values = (own_v, rim_v, vbuf)

    def project_rim(j):
        here = slice(j * WINDOW, (j + 1) * WINDOW)
        there = slice(WINDOW, 2 * WINDOW) if j else slice(0, WINDOW)
        scaled, _ = standardize(rim_x[there, :].astype(F32))
        value = (scaled * gain1_ref[...] + shift1_ref[...]).astype(BF16)
        made = dot(value, wqkv[...]).astype(BF16)
        for part, (_, rim, other) in enumerate((queries, keys, values)):
            rim[there, :] = made[:, part * D : part * D + HEAD_DIM]
            other[here, :] = made[:, part * D + HEAD_DIM : (part + 1) * D]

    def project(i):
        here = slice(WINDOW + i * step, WINDOW + (i + 1) * step)
        made = dot(normed[i * step : (i + 1) * step, :], wother[...]).astype(BF16)
        for part, (_, _, other) in enumerate((queries, keys, values)):
            other[here, :] = made[:, part * HEAD_DIM : (part + 1) * HEAD_DIM]

    current, current_t, offset = masks()
    columns = [slice(h * HEAD_DIM, (h + 1) * HEAD_DIM) for h in range(HEADS)]
    held = {}

    def row_of(bufs, j, h):
        mine, rim, other = bufs
        if h:
            return other[j * WINDOW : (j + 1) * WINDOW, :]
        if 1 <= j <= rows:
            return mine[(j - 1) * WINDOW : j * WINDOW, :]
        return rim[WINDOW:, :] if j else rim[:WINDOW, :]

    def pair(bufs, j, h):
        if h:
            return bufs[2][(j - 1) * WINDOW : (j + 1) * WINDOW, :]
        if 1 < j <= rows:
            return bufs[0][(j - 2) * WINDOW : j * WINDOW, :]
        return jnp.concatenate([row_of(bufs, j - 1, 0), row_of(bufs, j, 0)])

    def grad_of(j, h):
        return gbuf[j * WINDOW : (j + 1) * WINDOW, columns[h]]

    def probs_of(j, h):
        if h:
            return probs.at[j - 1]
        return own_probs.at[j - 1] if 1 < j <= rows else probs.at[rows + 1 + (j > 1)]

    def key_sum(weights, queries):
        zero = jnp.zeros_like(weights)
        both = jnp.concatenate([jnp.where(current, zero, weights), jnp.where(current, weights, zero)])
        made = dot(both, queries)
        return made[:WINDOW], made[WINDOW:]

    def score(j, h):
        held[j, h] = merged_scores(pair(keys, j, h), row_of(queries, j, h), current)

    def soften(j, h):
        r = j - 1
        weights = soft_weights(
            held[j, h], offset, low_mark[r : r + 1, :WINDOW], fill_mark[r : r + 1, :WINDOW]
        )
        probs_of(j, h)[...] = weights
        held[j, h] = weights.astype(BF16)

    def gather(j, h):
        r = j - 1
        made = window_sum(held.pop((j, h)), pair(values, j, h), current_t).astype(BF16)
        if r < rows:
            att[r * WINDOW : (r + 1) * WINDOW, columns[h]] = made
        else:
            halo_att[:, columns[h]] = made

    def feed_forward(first, count, own_rows):
        at = first * WINDOW
        size = count * WINDOW
        here = slice(at, at + size)
        held = {}
        block = 256
        slot = at // step % 2
        grads = hid_grad.at[slot] if own_rows else halo_grad
        xs, cots, atts = (x_ref, cot_ref, att) if own_rows else (rim_x.at[pl.ds(WINDOW, WINDOW)], rim_cot, halo_att)
        there = here if own_rows else slice(0, size)

        def enter():
            if own_rows:
                if at >= 2 * step:
                    leaving[0, at // step - 2].wait()
                    leaving[2, at // step - 2].wait()
                leave(1, at // step, att.at[pl.ds(at, size)], att_out.at[pl.ds(at, size)])
            attended = atts[there, :]
            middle = xs[there, :].astype(F32) + split_dot(attended, wout[...])
            scaled, inverse = standardize(middle)
            held.update(scaled=scaled, inverse=inverse)
            held["normed"] = (scaled * gain2_ref[...] + shift2_ref[...]).astype(BF16)

        def hide(f):
            cols = slice(f * block, (f + 1) * block)
            hidden = dot(held["normed"], up_ref[:, cols]) + up_bias_ref[:, cols]
            active, slope = twice_gelu(hidden)
            grad = dot_lanes(cots[there, :], down_ref[cols, :]) * slope
            grads[:size, cols] = grad.astype(BF16)
            if own_rows:
                act[slot, :size, cols] = active.astype(BF16)
                acc_vec[8:9, cols] += column_sums(grad)

        def weigh(f):
            cols = slice(f * block, (f + 1) * block)
            down_part = dot(cot_t[:, here], act[slot, :size, cols])
            up_part = dot_rows(held["normed"], grads[:size, cols])
            if at:
                acc_down[:, cols] += down_part
                acc_up[:, cols] += up_part
            else:
                acc_down[:, cols] = down_part
                acc_up[:, cols] = up_part

        def back():
            if own_rows:
                leave(0, at // step, act.at[slot], act_out.at[pl.ds(at, size)])
            scaled = held["scaled"]
            g2 = split_dot(grads[:size, :], up_ref[...], dot_lanes)
            cot32 = cots[there, :].astype(F32)
            middle_grad = cot32 + normalize_back(g2 * gain2_ref[...], scaled, held["inverse"])
            mixing_grad = middle_grad.astype(BF16)
            if own_rows:
                mid_grad[slot, :, :] = middle_grad
                leave(2, at // step, mid_grad.at[slot], mid_grad_out.at[pl.ds(at, size)])
                acc_vec[2:3, :D] += column_sums(g2 * scaled)
                acc_vec[3:4, :D] += column_sums(g2)
                out_part = dot_rows(atts[there, :], mixing_grad)
                if at:
                    acc_out[...] += out_part
                else:
                    acc_out[...] = out_part
            made = split_dot(mixing_grad, wout[...], dot_lanes).astype(BF16)
            for g in range(count):
                j = first + 1 + g
                gbuf[j * WINDOW : (j + 1) * WINDOW, :] = made[g * WINDOW : (g + 1) * WINDOW]

        call = functools.partial
        parts = FF // block
        hides = [call(hide, f) for f in range(parts)]
        weighs = [call(weigh, f) for f in range(parts)] if own_rows else []
        return enter, hides, weighs, back

    held_back = {}
    unfinished = {}

    def weigh_grads(j, h):
        held_back[j, h] = merged_scores(pair(values, j, h), grad_of(j, h), current)

    def soften_back(j, h):
        dweights = held_back.pop((j, h))
        weights = probs_of(j, h)[...]
        inner = jnp.sum(weights * dweights, axis=0, keepdims=True)
        dscores = (weights * (dweights - inner)).astype(BF16)
        held_back[j, h] = (dscores, weights.astype(BF16))

    def gather_back(j, h):
        r = j - 1
        dscores, weights = held_back.pop((j, h))
        found = [key_sum(dscores, row_of(queries, j, h)), key_sum(weights, grad_of(j, h))]
        if j > 1:
            there = slice((r - 1) * WINDOW, r * WINDOW)
            for part, (before, _) in enumerate(found):
                total = unfinished[part, h] + before
                at = (part + 1) * D + h * HEAD_DIM
                dqkv[there, at : at + HEAD_DIM] = (total if part else total * SCALE).astype(BF16)
        for part, (_, current_part) in enumerate(found):
            unfinished[part, h] = current_part
        if j <= rows:
            dqkv[r * WINDOW : (r + 1) * WINDOW, columns[h]] = (
                window_sum(dscores, pair(keys, j, h), current_t) * SCALE
            ).astype(BF16)

    def project_back(i):
        at = i * step
        leave(3, i, dqkv.at[pl.ds(at, step)], dqkv_out.at[pl.ds(at, step)])
        made = dot(xhat_t[:, at : at + step], dqkv[at : at + step, :])
        acc_qkv[...] = (acc_qkv[...] + made) if at else made

    def units(first, last):
        return [(j, h) for j in range(first, last + 1) for h in range(HEADS)]

    project_rim(0)
    project_rim(rows + 1)
    for i in range(steps):
        project(i)
    forward = [(j, h) for j, h in units(1, rows + 1) if h or not 1 < j <= rows]
    do(staggered(forward, score, soften, gather))
    feeds = [feed_forward(i * CHUNK, CHUNK, True) for i in range(steps)]
    halo_enter, halo_hides, _, halo_back = feed_forward(rows, 1, False)
    halo = [halo_enter] + halo_hides + [halo_back]
    enter, hides, weighs, back = feeds[0]
    do([enter, halo.pop(0), hides[0], hides[1], weighs[0]])
    for i in range(steps):
        enter, hides, weighs, back = feeds[i]
        for f in range(2, len(hides)):
            do([hides[f], weighs[f - 1]] + halo[:1])
            halo = halo[1:]
        if i + 1 < steps:
            later = feeds[i + 1]
            do([later[0], weighs[-1], later[1][0], back, later[1][1], later[2][0]] + halo[:1])
            halo = halo[1:]
        else:
            do([weighs[-1]] + halo + [back])

    wide = FF // 2
    halves = ((core, keep_ref), (1 - core, send_ref))
    feed, heads = piece_rows(FF, D)
    quarter = feed - VECTOR_ROWS

    def spot(row):
        return row // quarter * (feed + heads) + row % quarter

    def export_down(c, ref, f):
        at = pl.ds(pl.multiple_of(c * wide + f, D), D)
        block = (acc_down[:, at] * 0.5).astype(BF16).T
        for half in range(D // HEAD_DIM):
            to = spot(half * wide + f)
            ref[to : to + D, :] = block[
                :, half * HEAD_DIM : (half + 1) * HEAD_DIM
            ]

    def export_up(c, ref, n):
        at = pl.ds(pl.multiple_of(c * wide + n * HEAD_DIM, HEAD_DIM), HEAD_DIM)
        to = spot(D // HEAD_DIM * wide + n * D)
        ref[to : to + D, :] = acc_up[:, at].astype(BF16)

    def export_heads(c, ref, h, part):
        mine = pl.ds(pl.multiple_of(c * HEAD_DIM, HEAD_DIM), HEAD_DIM)
        true_head = head if h == 0 else 1 - head
        if part < 3:
            at = part * D + h * HEAD_DIM
            block = acc_qkv[mine, at : at + HEAD_DIM]
        else:
            block = acc_out[h * HEAD_DIM : (h + 1) * HEAD_DIM, mine]
        piece, shift = true_head + part // 2 * 2, part % 2 * HEAD_DIM
        first = piece * (feed + heads) + feed + shift
        second = part * (feed + heads) + feed + true_head * HEAD_DIM
        at = jnp.where(c == 0, first, second)
        ref[pl.ds(pl.multiple_of(at, 16), HEAD_DIM), :] = block.astype(BF16)

    def export_vectors(c, ref):
        flat = vec_rows[pl.ds(pl.multiple_of(c * 16, 16), 16), :].astype(BF16)
        for piece in range(4):
            to = piece * (feed + heads) + quarter
            ref[to : to + VECTOR_ROWS, :] = flat

    call = functools.partial
    exports = [call(export_down, c, ref, f) for c, ref in halves for f in range(0, wide, D)]
    exports += [call(export_up, c, ref, n) for c, ref in halves for n in range(wide // HEAD_DIM)]
    exports += [call(export_heads, c, ref, h, 3) for c, ref in halves for h in range(HEADS)]
    backs = staggered(units(1, rows + 1), weigh_grads, soften_back, gather_back)
    marks = []
    for i in range(steps):
        done = [n for n, job in enumerate(backs) if job.func is gather_back and job.args == ((i + 1) * CHUNK + 1, 1)]
        marks.append(done[0] + 1)
    do(merge(backs[: marks[0]], exports))
    for i in range(1, steps):
        project_back(i - 1)
        do(backs[marks[i - 1] : marks[i]])
    do(backs[marks[-1] :])
    project_back(steps - 1)

    gain_t = jnp.broadcast_to(gain1_ref[...], (HEAD_DIM, D)).T
    shift_t = jnp.broadcast_to(shift1_ref[...], (HEAD_DIM, D)).T
    gain_sum = jnp.zeros((D, HEAD_DIM), F32)
    shift_sum = jnp.zeros((D, HEAD_DIM), F32)
    for n in range(3 * D // HEAD_DIM):
        cols = slice(n * HEAD_DIM, (n + 1) * HEAD_DIM)
        product = acc_qkv[:D, cols]
        total = acc_qkv[D : D + 1, cols]
        weight = wqkv[:, cols].astype(F32)
        gain_sum += weight * product
        shift_sum += weight * total
        acc_qkv[:D, cols] = gain_t * product + shift_t * total
    acc_vec[0:1, :D] = column_sums(gain_sum.T)
    acc_vec[1:2, :D] = column_sums(shift_sum.T)
    acc_vec[4:5, :D] = column_sums(cot_sum[...])

    for c, ref in halves:
        do([call(export_heads, c, ref, h, part) for h in range(HEADS) for part in range(3)])
    for n, (row, cols) in enumerate(vector_slots(FF, D)):
        vec_rows[n : n + 1, :] = acc_vec[row : row + 1, cols]
    for c, ref in halves:
        export_vectors(c, ref)
    for (kind, n), copy in leaving.items():
        if kind not in (0, 2) or n >= steps - 2:
            copy.wait()


def layer(rims, made, tokens, up, gain1, shift1, weights, others, gain2, shift2, up_bias):
    own, D = tokens.shape
    FF = up.shape[1]
    rows = own // WINDOW
    count = own + 2 * WINDOW
    half = half_rows(FF, D)
    tokens, up = in_vmem(tokens), in_vmem(up)
    rims, made, others = ([in_vmem(array) for array in arrays] for arrays in (rims, made, others))
    vmem = pl.BlockSpec(memory_space=pltpu.VMEM)
    return pl.pallas_call(
        functools.partial(layer_kernel, rows),
        out_shape=(
            pltpu.VMEM((half, HEAD_DIM), BF16),
            pltpu.VMEM((half, HEAD_DIM), BF16),
            pltpu.HBM((own, FF), BF16),
            pltpu.HBM((own, D), BF16),
            pltpu.HBM((own, D), F32),
            pltpu.HBM((own, 3 * D), BF16),
            pltpu.HBM((D, 3 * D), BF16),
            pltpu.HBM((D, D), BF16),
        ),
        in_specs=[vmem] * (2 + len(made) + 2 + 2 + 4 + 2 + 3),
        out_specs=(vmem, vmem) + (pl.BlockSpec(memory_space=pltpu.HBM),) * 6,
        scratch_shapes=[
            pltpu.VMEM((2, CHUNK * WINDOW, FF), BF16),
            pltpu.VMEM((own, D), BF16),
            pltpu.VMEM((2, CHUNK * WINDOW, D), F32),
            pltpu.VMEM((own, 3 * D), BF16),
            pltpu.VMEM((D, 3 * D), BF16),
            pltpu.VMEM((D, D), BF16),
            pltpu.VMEM((2 * WINDOW, D), BF16),
            pltpu.VMEM((WINDOW, D), BF16),
            pltpu.VMEM((WINDOW, FF), BF16),
            pltpu.VMEM((WINDOW, D), BF16),
            pltpu.VMEM((D, 3 * HEAD_DIM), BF16),
            pltpu.VMEM((2 * WINDOW, HEAD_DIM), BF16),
            pltpu.VMEM((2 * WINDOW, HEAD_DIM), BF16),
            pltpu.VMEM((2 * WINDOW, HEAD_DIM), BF16),
            pltpu.VMEM((count, HEAD_DIM), BF16),
            pltpu.VMEM((count, HEAD_DIM), BF16),
            pltpu.VMEM((count, HEAD_DIM), BF16),
            pltpu.VMEM((count, D), BF16),
            pltpu.VMEM((rows + 3, WINDOW, WINDOW), F32),
            pltpu.VMEM((2, CHUNK * WINDOW, FF), BF16),
            pltpu.VMEM((D, FF), F32),
            pltpu.VMEM((D, FF), F32),
            pltpu.VMEM((D + 16, 3 * D), F32),
            pltpu.VMEM((D, D), F32),
            pltpu.VMEM((16, FF), F32),
            pltpu.VMEM((32, HEAD_DIM), F32),
            pltpu.SemaphoreType.DMA((5, max(rows // CHUNK, 2))),
        ],
        compiler_params=pltpu.CompilerParams(vmem_limit_bytes=34 * 1024 * 1024),
        name="layer",
    )(*rims, *made, tokens, up, gain1, shift1, *weights, *others, gain2, shift2, up_bias)


def token_chunks(streams, out_ref, buf, in_sem, out_sem, fixed, work):
    step = CHUNK * WINDOW
    arriving = [pltpu.make_async_copy(a, b, in_sem.at[0, n]) for n, (a, b) in enumerate(fixed)]
    steps = buf.shape[0] // step
    chunks = []
    for i in range(steps):
        here = pl.ds(i * step, step)
        chunks.append(
            [pltpu.make_async_copy(a.at[here], b.at[here], in_sem.at[i + 1, n]) for n, (a, b) in enumerate(streams)]
        )
    for copy in arriving + [copy for chunk in chunks for copy in chunk]:
        copy.start()
    for copy in arriving:
        copy.wait()
    leaving = []
    for i in range(steps):
        for copy in chunks[i]:
            copy.wait()
        work(slice(i * step, (i + 1) * step))
        here = pl.ds(i * step, step)
        leaving.append(pltpu.make_async_copy(buf.at[here], out_ref.at[here], out_sem.at[i]))
        leaving[-1].start()
    for copy in leaving:
        copy.wait()


def input_grad_kernel(
    x_in, mid_in, dqkv_in, wqkv_in, gain1_ref, out_ref, buf, in_sem, out_sem, x_ref, mid_grad, dqkv, wqkv
):
    def work(here):
        scaled, inverse = standardize(x_ref[here, :].astype(F32))
        g1 = split_dot(dqkv[here, :], wqkv[...], dot_lanes)
        buf[here, :] = (
            mid_grad[here, :] + normalize_back(g1 * gain1_ref[...], scaled, inverse)
        ).astype(BF16)

    streams = ((x_in, x_ref), (mid_in, mid_grad), (dqkv_in, dqkv))
    token_chunks(streams, out_ref, buf, in_sem, out_sem, ((wqkv_in, wqkv),), work)


def mixed_kernel(
    x_in, att_in, act_in, wout_in, down_in, down_bias_ref, out_ref, buf, in_sem, out_sem, x_ref, att, act, wout, down
):
    def work(here):
        middle = x_ref[here, :].astype(F32) + split_dot(att[here, :], wout[...])
        mixed = middle + split_dot(act[here, :], down[...]) * 0.5 + down_bias_ref[...]
        buf[here, :] = mixed.astype(BF16)

    streams = ((x_in, x_ref), (att_in, att), (act_in, act))
    token_chunks(streams, out_ref, buf, in_sem, out_sem, ((wout_in, wout), (down_in, down)), work)


def late(kernel, name, arrays, small):
    own, D = arrays[0].shape
    steps = own // (CHUNK * WINDOW)
    hbm = pl.BlockSpec(memory_space=pltpu.HBM)
    return pl.pallas_call(
        kernel,
        out_shape=pltpu.HBM((own, D), BF16),
        in_specs=[hbm] * len(arrays) + [pl.BlockSpec(memory_space=pltpu.VMEM)],
        out_specs=hbm,
        scratch_shapes=[
            pltpu.VMEM((own, D), BF16),
            pltpu.SemaphoreType.DMA((steps + 1, 3)),
            pltpu.SemaphoreType.DMA((steps,)),
        ]
        + [pltpu.VMEM(array.shape, array.dtype) for array in arrays],
        compiler_params=pltpu.CompilerParams(vmem_limit_bytes=32 * 1024 * 1024),
        name=name,
    )(*[in_hbm(array) for array in arrays], small)


def pack_kernel(query_ref, key_ref, value_ref, out_ref, tok_ref, cot_ref, half_ref, near_ref, far_ref, sem):
    D = query_ref.shape[0]
    own = tok_ref.shape[0]
    head = lax.axis_index("head")
    core = lax.axis_index("seq") % 2
    last = own - WINDOW
    near_from = pl.multiple_of((1 - head) * last, WINDOW)
    far_from = pl.multiple_of(head * last, WINDOW)
    moves = []
    for half in range(D // HEAD_DIM):
        cols = pl.ds(half * HEAD_DIM, HEAD_DIM)
        for k, ref in enumerate((tok_ref, cot_ref)):
            at = (half * 2 + k) * WINDOW
            moves.append((ref.at[pl.ds(near_from, WINDOW), cols], near_ref.at[pl.ds(at, WINDOW)]))
            moves.append((ref.at[pl.ds(far_from, WINDOW), cols], far_ref.at[pl.ds(at, WINDOW)]))
    copies = [pltpu.make_async_copy(a, b, sem.at[n]) for n, (a, b) in enumerate(moves)]
    for copy in copies:
        copy.start()

    def weights(moves):
        sent = [pltpu.make_async_copy(a, b, sem.at[len(copies) + n]) for n, (a, b) in enumerate(moves)]
        for copy in sent:
            copy.start()
        for copy in sent:
            copy.wait()

    @pl.when(core == 0)
    def _():
        weights([(query_ref, half_ref.at[pl.ds(0, D)]), (key_ref, half_ref.at[pl.ds(D, D)])])

    @pl.when(core == 1)
    def _():
        outs = [
            (
                out_ref.at[:, pl.ds(half * HEAD_DIM, HEAD_DIM)],
                half_ref.at[pl.ds(D + half * HEAD_DIM, HEAD_DIM)],
            )
            for half in range(D // HEAD_DIM)
        ]
        weights([(value_ref, half_ref.at[pl.ds(0, D)])] + outs)

    for copy in copies:
        copy.wait()


def pack(query_weight, key_weight, value_weight, out_weight, tokens, cotangent):
    D = query_weight.shape[0]
    rim = 2 * WINDOW * D // HEAD_DIM
    vmem = pl.BlockSpec(memory_space=pltpu.VMEM)
    return pl.pallas_call(
        pack_kernel,
        out_shape=(
            pltpu.VMEM((2 * D, HEAD_DIM), BF16),
            pltpu.VMEM((rim, HEAD_DIM), BF16),
            pltpu.VMEM((rim, HEAD_DIM), BF16),
        ),
        in_specs=[pl.BlockSpec(memory_space=pl.ANY)] * 6,
        out_specs=(vmem, vmem, vmem),
        scratch_shapes=[pltpu.SemaphoreType.DMA((6 * (D // HEAD_DIM) + 1,))],
        name="pack",
    )(query_weight, key_weight, value_weight, out_weight, tokens, cotangent)


def finish_kernel(FF, D, second, mine_ref, *refs):
    if second:
        vectors, refs = (refs[0], refs[7:13]), refs[13:]
    outs, (down_buf, up_buf, heads_buf, vec_rows, sem) = refs[:6], refs[6:]
    query, key, value, out, up, down = outs
    core = lax.axis_index("seq") % 2
    c = 1 - core if second else core
    wide = FF // 2
    copies = []

    def leave(source, target):
        copies.append(pltpu.make_async_copy(source, target, sem.at[len(copies)]))
        copies[-1].start()

    feed = piece_rows(FF, D)[0]
    quarter = feed - VECTOR_ROWS
    for half in range(D // HEAD_DIM):
        at = half * wide // quarter * feed + half * wide % quarter
        down_buf[:, half * HEAD_DIM : (half + 1) * HEAD_DIM] = mine_ref[at : at + wide, :].astype(F32)
    leave(down_buf, down.at[pl.ds(pl.multiple_of(c * wide, wide), wide)])
    start = D // HEAD_DIM * wide
    for n, f in enumerate(range(0, wide, HEAD_DIM)):
        at = (start + n * D) // quarter * feed + (start + n * D) % quarter
        up_buf[:, f : f + HEAD_DIM] = mine_ref[at : at + D, :].astype(F32)
    leave(up_buf, up.at[:, pl.ds(pl.multiple_of(c * wide, wide), wide)])
    start = 4 * feed
    own = pl.ds(pl.multiple_of(c * HEAD_DIM, HEAD_DIM), HEAD_DIM)
    for part, made in enumerate((query, key, value, out)):
        at = start + part * HEAD_DIM
        heads_buf[part] = mine_ref[at : at + HEAD_DIM, :].astype(F32)
        leave(heads_buf.at[part], made.at[:, own] if part == 3 else made.at[own])
    if second:
        other_ref, made = vectors
        at = quarter
        for k, ref in ((c, mine_ref), (core, other_ref)):
            vec_rows[pl.ds(pl.multiple_of(k * 16, 16), 16), :] = ref[at : at + 16, :].astype(F32)
        for s, (n, cols) in enumerate(vector_slots(FF, D)):
            made[5 if n == 8 else n][cols] = vec_rows[s, :]
    for copy in copies:
        copy.wait()


def finish(mine, FF, D, first=None):
    vmem = pl.BlockSpec(memory_space=pltpu.VMEM)
    hbm = pl.BlockSpec(memory_space=pltpu.HBM)
    arrays = [(D, HEAD_DIM)] * 3 + [(HEAD_DIM, D), (D, FF), (FF, D)]
    vectors = [(D,)] * 5 + [(FF,)] if first else []
    wide = FF // 2
    given = (in_vmem(first[0]), *[in_hbm(array) for array in first[1]]) if first else ()
    return pl.pallas_call(
        functools.partial(finish_kernel, FF, D, bool(first)),
        out_shape=tuple(jax.ShapeDtypeStruct(shape, F32) for shape in vectors)
        + tuple(pltpu.HBM(shape, F32) for shape in arrays),
        in_specs=[vmem] + ([vmem] + [hbm] * 6 if first else []),
        out_specs=(vmem,) * len(vectors) + (hbm,) * 6,
        input_output_aliases={2 + n: 6 + n for n in range(6)} if first else {},
        scratch_shapes=[
            pltpu.VMEM((wide, D), F32),
            pltpu.VMEM((D, wide), F32),
            pltpu.VMEM((4, HEAD_DIM, HEAD_DIM), F32),
            pltpu.VMEM((32, HEAD_DIM), F32),
            pltpu.SemaphoreType.DMA((6,)),
        ],
        name="finish_rest" if first else "finish",
    )(in_vmem(mine), *given)


def spans(masks):
    found = [0]
    for mask in masks:
        found = found + [f ^ mask for f in found]
    return found


def stages(count):
    bits = [1 << b for b in range(count.bit_length() - 1)]
    plane, rest = [bits[0], bits[2]], bits[3:]
    found = [plane] + [rest[i : i + 2] for i in range(0, len(rest), 2)]
    if len(found) > 1 and len(found[1]) == 2:
        return [(found[0], found[1][::-1]), (found[1], found[0])] + [(masks, masks) for masks in found[2:]]
    return [(masks, masks) for masks in found]


def partners(value, masks, k):
    count = lax.axis_size("seq") * lax.axis_size("head")
    hops = [spans(side)[k] for side in masks]
    return lax.ppermute(value, BOTH, [(i, i ^ hops[i // 2 % 2]) for i in range(count)])


def all_sum(value, side, FF, D):
    count = lax.axis_size("seq") * lax.axis_size("head")
    place = lax.axis_index("seq") * lax.axis_size("head") + lax.axis_index("head")
    width = value.shape[1]
    made = []
    steps = []
    for masks in stages(count):
        code, other_code = (
            sum(((place & mask) // mask) << j for j, mask in enumerate(bits)) for bits in masks
        )
        steps.append((masks, jnp.where(place & 2 == 0, code, other_code)))

    def exchange(value, send, masks, number):
        if number >= len(side):
            return [partners(send(value, k), masks, k) for k in range(1, 1 << len(masks[0]))]
        work, small = side[number]
        value, small = lax.optimization_barrier((value, small))
        arrived = [partners(send(value, k), masks, k) for k in range(1, 1 << len(masks[0]))]
        arrived, done = lax.optimization_barrier((arrived, work(small)))
        made.append(done)
        return arrived

    def spread(value, masks, code, number):
        found = [value] + exchange(value, lambda v, k: v, masks, number)
        whole = jnp.zeros((len(found),) + value.shape, value.dtype)
        for k, part in enumerate(found):
            whole = lax.dynamic_update_index_in_dim(whole, part, code ^ k, 0)
        return whole

    for number, (masks, code) in enumerate(steps[:-1]):
        parts = value.reshape(1 << len(masks[0]), -1, width)
        total = lax.dynamic_index_in_dim(parts, code, 0, False).astype(F32)
        pick = lambda parts, k, code=code: lax.dynamic_index_in_dim(parts, code ^ k, 0, False)
        for part in exchange(parts, pick, masks, number):
            total = total + part.astype(F32)
        value = total.astype(BF16)
    masks, _ = steps[-1]
    parts = [value] + exchange(value, lambda v, k: v, masks, len(steps) - 1)
    parts = [part.astype(F32) for part in parts]
    while len(parts) > 1:
        parts = [a + b for a, b in zip(parts[::2], parts[1::2])]
    value = parts[0].astype(BF16)
    for masks, code in steps[-2:0:-1]:
        value = spread(value, masks, code, len(side)).reshape(-1, width)
    masks, code = steps[0]
    feed, heads = piece_rows(FF, D)
    head = lax.axis_index("head")
    first_core = place & 2 == 0
    mine, other = value[feed : feed + heads // 2], value[feed + heads // 2 :]
    swap = jnp.logical_and(jnp.logical_not(first_core), head == 1)
    value = jnp.concatenate([value[:feed], jnp.where(swap, other, mine), jnp.where(swap, mine, other)])
    short = value[: feed + heads // 2]
    found = [value, partners(short, masks, 1), partners(value, masks, 2), partners(short, masks, 3)]
    whole = jnp.zeros((4 * feed, width), value.dtype)
    by_half = jnp.zeros((2 * heads, width), value.dtype)
    by_part = by_half
    for k, part in enumerate(found):
        whole = lax.dynamic_update_slice_in_dim(whole, part[:feed], (code ^ k) * feed, 0)
        by_part = lax.dynamic_update_slice_in_dim(
            by_part, part[feed : feed + heads // 2], (code ^ k) * (heads // 2), 0
        )
        if k % 2 == 0:
            by_half = lax.dynamic_update_slice_in_dim(by_half, part[feed:], ((code ^ k) // 2) * heads, 0)
    return jnp.concatenate([whole, jnp.where(first_core, by_half, by_part)]), made


def across_cores(value):
    return partners(value, ([2], [2]), 1)


def shards(
    tokens,
    cotangent,
    image_rows,
    image_fill,
    first_gain,
    first_shift,
    query_weight,
    key_weight,
    value_weight,
    out_weight,
    second_gain,
    second_shift,
    up_weight,
    up_bias,
    down_weight,
    down_bias,
):
    own, D = tokens.shape
    FF = up_weight.shape[1]
    devices = lax.axis_size("seq") * lax.axis_size("head")
    half, near, far = pack(query_weight, key_weight, value_weight, out_weight, tokens, cotangent)
    half = lax.ppermute(half, "head", [(0, 1), (1, 0)])
    pairs = [(i, i + 1) for i in range(1, devices - 1, 2)]
    far = lax.ppermute(far, BOTH, pairs + [(b, a) for a, b in pairs])
    near = lax.ppermute(near, "head", [(0, 1), (1, 0)])
    weights = (query_weight, key_weight, value_weight, out_weight)
    gain1, shift1 = first_gain[None], first_shift[None]
    made = local(tokens, cotangent, down_weight, image_rows[None], image_fill[None], gain1, shift1, weights)
    half, near, far, mark = lax.optimization_barrier((half, near, far, made[6]))
    made = (*made[:6], mark, *made[7:])
    keep, send, act, att, mid_grad, dqkv, wqkv, wout = layer(
        (near, far),
        made,
        tokens,
        up_weight,
        gain1,
        shift1,
        weights,
        (half, across_cores(half)),
        second_gain[None],
        second_shift[None],
        up_bias[None],
    )
    side = [
        (lambda small: late(input_grad_kernel, "input_grad", (tokens, mid_grad, dqkv, wqkv), small), gain1),
        (lambda small: late(mixed_kernel, "mixed", (tokens, att, act, wout, down_weight), small), down_bias[None]),
    ]
    summed = (keep.astype(F32) + across_cores(send).astype(F32)).astype(BF16)
    mine, (input_grad, mixed) = all_sum(summed, side, FF, D)
    arrays = finish(mine, FF, D)
    gain1_grad, shift1_grad, gain2_grad, shift2_grad, down_bias_grad, up_bias_grad, *arrays = finish(
        across_cores(mine), FF, D, (mine, arrays)
    )
    query_grad, key_grad, value_grad, out_grad, up_grad, down_grad = arrays
    return (
        mixed,
        input_grad,
        gain1_grad,
        shift1_grad,
        query_grad,
        key_grad,
        value_grad,
        out_grad,
        gain2_grad,
        shift2_grad,
        up_grad,
        up_bias_grad,
        down_grad,
        down_bias_grad,
    )


def solution(mesh):
    stream = P(("seq", "head"), None)
    columns = P(None, "head")
    in_specs = (stream, stream) + (P(),) * 4 + (columns,) * 3 + (P("head", None),) + (P(),) * 6
    out_specs = (
        (stream, stream) + (P(),) * 2 + (columns,) * 3 + (P("head", None),) + (P(),) * 6
    )
    return jax.shard_map(shards, mesh=mesh, in_specs=in_specs, out_specs=out_specs, check_vma=False)
```
